32 devices in a mesh: elem: 32 (over z, y, x, core).
Axes of the slice: x: 2, y: 2, z: 4, core: 2. Of those that a mesh axis runs over, the one named last changes fastest.
Arguments:
- moment_fields: float32 [3, 512, 4096], P(None, None, 'elem'), may hold values from -6 to 6
- adjoint_fields: float32 [3, 512, 4096], P(None, None, 'elem'), may hold values from -6 to 6
- velocity: float32 [3, 512, 4096], P(None, None, 'elem'), may hold values from -12 to 12
- mass_weights: float32 [512, 4096], P(None, 'elem'), may hold values from 0.5 to 2
- diffusivity: float32 [3], replicated, may hold values from 0.1 to 0.5
- numbering: int32 [4096], P('elem'), may hold values from 0 to 4095, as said below
Outputs:
- moments: float32 [3, 512, 4096], P(None, None, 'elem')
- sensitivities: float32 [3, 512, 4096], P(None, None, 'elem')
The draws below stay inside these ranges and needn't reach their ends.
Inputs may be any that keep to these rules, and one draw needn't show every extreme that they name: `numbering`: rows d * 128 to (d + 1) * 128 - 1 hold, in some order, each of the numbers c * 128 to (c + 1) * 128 - 1 once, where c = (d + 4) % 32.
All inputs are finite; a program needn't handle non-finite values.
Results may differ from the reference program's by a relative error of at most 0.0001.
Values sent between devices are 32-bit elements; how exact they have to be, the bound alone decides.
No kernel may reach another device: no remote copies, remote signals or barrier semaphores. Data moves between devices by JAX's collectives and lax.ppermute only.
A program may use at most 64 MiB of HBM per device.

```python
import math
import jax
import jax.numpy as jnp
import numpy as np
from jax import lax

FIELDS = 3
NODES = 512
DA = 4
EZ = 128
DB = 8
ELEMENTS = 4096


def draw_numbering(key, part):
    column_keys = jax.random.split(key, DA * DB)
    orderings = jax.vmap(lambda one_key: jax.random.permutation(one_key, EZ))(column_keys).astype(jnp.int32)
    device_index = lax.iota(jnp.int32, DA * DB)
    column_index = (device_index + DB // 2) % (DA * DB)
    offsets = column_index[:, None] * EZ
    return (orderings + offsets).reshape(-1).astype(jnp.int32)


def block_levels(own_key, extent, cuts, low, top_value):
    loudness, own = 1.0, jax.random.fold_in(own_key, 6)
    for position, blocks in cuts:
        draws = jnp.exp(jax.random.uniform(jax.random.fold_in(own, position), (blocks,), jnp.float32, low / len(cuts), top_value / len(cuts)))
        loudness = loudness * jnp.repeat(draws, extent[position] // blocks).reshape([-1 if axis == position else 1 for axis in range(len(extent))])
    return loudness


def normal_values(key, extent, width, bound, cuts=(), held_as=jnp.bfloat16):
    array = width * jax.random.normal(key, extent, jnp.float32)
    if cuts:
        array = array * block_levels(key, extent, cuts, -0.22, 0.18)
    return jnp.clip(array, -bound, bound).astype(held_as)


def setup_inputs(seed: int = 0) -> dict:
    key_list = jax.random.split(jax.random.key(seed), 7)
    moment_fields = normal_values(key_list[0], (FIELDS, NODES, ELEMENTS), 1.0, 6.0, ((2, 32),), jnp.float32)
    adjoint_fields = normal_values(key_list[1], (FIELDS, NODES, ELEMENTS), 1.0, 6.0, ((2, 32),), jnp.float32)
    velocity = normal_values(key_list[2], (3, NODES, ELEMENTS), 3.0, 12.0, ((2, 32),), jnp.float32)
    mass_weights = jnp.clip(jnp.exp(math.log(2.0) - 1.3862944 * jax.random.uniform(key_list[3], (NODES, ELEMENTS), jnp.float32) ** block_levels(key_list[3], (NODES, ELEMENTS), ((1, 32),), -0.2, 0.2)), 0.5, 2.0)
    diffusivity = jnp.clip(jnp.exp(jax.random.uniform(key_list[4], (FIELDS,), jnp.float32, math.log(0.1), math.log(0.5))), 0.1, 0.5)
    numbering = draw_numbering(jax.random.fold_in(key_list[6], 71), 0)
    return {"moment_fields": moment_fields, "adjoint_fields": adjoint_fields, "velocity": velocity, "mass_weights": mass_weights, "diffusivity": diffusivity, "numbering": numbering}


time_step = 0.001
highest = lax.Precision.HIGHEST


def gll_tables():
    points = [-1.0, -0.8717401485096066, -0.5917001814331423, -0.2092992179024789, 0.2092992179024789, 0.5917001814331423, 0.8717401485096066, 1.0]
    weights = [0.03571428571428571, 0.21070422714350603, 0.3411226924835044, 0.4124587946587038, 0.4124587946587038, 0.3411226924835044, 0.21070422714350603, 0.03571428571428571]
    barycentric = []
    for left_index in range(8):
        product = 1.0
        for right_index in range(8):
            if right_index != left_index:
                product = product * (points[left_index] - points[right_index])
        barycentric.append(1.0 / product)
    derivative = np.zeros((8, 8))
    for left_index in range(8):
        row_total = 0.0
        for right_index in range(8):
            if left_index != right_index:
                entry = (barycentric[right_index] / barycentric[left_index]) / (points[left_index] - points[right_index])
                derivative[left_index, right_index] = entry
                row_total = row_total + entry
        derivative[left_index, left_index] = -row_total
    return jnp.asarray(derivative, dtype=jnp.float32), jnp.asarray(weights, dtype=jnp.float32)


def gradient(quantity, derivative):
    along_i = jnp.einsum('pi,gijke->gpjke', derivative, quantity, precision=highest)
    along_j = jnp.einsum('pj,gijke->gipke', derivative, quantity, precision=highest)
    along_k = jnp.einsum('pk,gijke->gijpe', derivative, quantity, precision=highest)
    return along_i, along_j, along_k


def transposed(quantity, derivative, direction):
    if direction == 0:
        return jnp.einsum('ip,gijke->gpjke', derivative, quantity, precision=highest)
    if direction == 1:
        return jnp.einsum('jp,gijke->gipke', derivative, quantity, precision=highest)
    return jnp.einsum('kp,gijke->gijpe', derivative, quantity, precision=highest)


def forward_terms(quantity, velocity, mass_cube, diffusivity, derivative):
    gradients = gradient(quantity, derivative)
    advect = velocity[0] * gradients[0] + velocity[1] * gradients[1] + velocity[2] * gradients[2]
    diffuse = transposed(mass_cube * gradients[0], derivative, 0)
    diffuse = diffuse + transposed(mass_cube * gradients[1], derivative, 1)
    diffuse = diffuse + transposed(mass_cube * gradients[2], derivative, 2)
    return -(mass_cube * advect) - diffusivity[:, None, None, None, None] * diffuse


def adjoint_terms(quantity, velocity, mass_cube, diffusivity, derivative):
    gradients = gradient(quantity, derivative)
    scaled = diffusivity[:, None, None, None, None]
    summed = transposed(mass_cube * (velocity[0] * quantity + scaled * gradients[0]), derivative, 0)
    summed = summed + transposed(mass_cube * (velocity[1] * quantity + scaled * gradients[1]), derivative, 1)
    summed = summed + transposed(mass_cube * (velocity[2] * quantity + scaled * gradients[2]), derivative, 2)
    return -summed


def global_numbers(numbering):
    pencil = numbering // EZ
    height = numbering % EZ
    slab_row = pencil // DB
    slab_place = pencil % DB
    node_index = lax.iota(jnp.int32, 512)
    node_i = (node_index // 64)[:, None]
    node_j = ((node_index // 8) % 8)[:, None]
    node_k = (node_index % 8)[:, None]
    coord_x = 7 * slab_row[None, :] + node_i
    coord_y = 7 * slab_place[None, :] + node_j
    coord_z = 7 * height[None, :] + node_k
    return ((coord_x * (7 * DB + 1) + coord_y) * (7 * EZ + 1) + coord_z).astype(jnp.int32)


def assemble(values, global_node):
    count = values.shape[0]
    flattened = values.reshape(count, -1).T
    segment_ids = global_node.reshape(-1)
    totals = jax.ops.segment_sum(flattened, segment_ids, num_segments=(7 * DA + 1) * (7 * DB + 1) * (7 * EZ + 1))
    return totals[segment_ids].T.reshape(values.shape)


def reference(moment_fields, adjoint_fields, velocity, mass_weights, diffusivity, numbering):
    derivative, weights = gll_tables()
    elements = numbering.shape[0]
    count = moment_fields.shape[0]
    global_node = global_numbers(numbering)
    weight_cube = weights[:, None, None] * weights[None, :, None] * weights[None, None, :]
    mass_cube = mass_weights.reshape(8, 8, 8, elements) * weight_cube[:, :, :, None]
    mass_sum = assemble(mass_cube[None], global_node)[0]
    flow = velocity.reshape(3, 8, 8, 8, elements)
    fields_now = moment_fields.reshape(count, 8, 8, 8, elements)
    for step_index in range(2):
        terms = forward_terms(fields_now, flow, mass_cube, diffusivity, derivative)
        fields_now = fields_now + time_step * assemble(terms, global_node) / mass_sum
    adjoint_now = adjoint_fields.reshape(count, 8, 8, 8, elements)
    for step_index in range(2):
        gathered = assemble(adjoint_now / mass_sum, global_node)
        adjoint_now = adjoint_now + time_step * adjoint_terms(gathered, flow, mass_cube, diffusivity, derivative)
    return fields_now.reshape(count, 512, elements), adjoint_now.reshape(count, 512, elements)
```

```python
import functools

import jax
import jax.numpy as jnp
import numpy as np
from jax import lax
from jax.experimental import pallas as pl
from jax.experimental.pallas import tpu as pltpu
from jax.sharding import PartitionSpec as P

DA = 4
DT = 0.001
F32 = jnp.float32
BF16 = jnp.bfloat16


def gll_tables():
    points = [
        -1.0,
        -0.8717401485096066,
        -0.5917001814331423,
        -0.2092992179024789,
        0.2092992179024789,
        0.5917001814331423,
        0.8717401485096066,
        1.0,
    ]
    weights = [
        0.03571428571428571,
        0.21070422714350603,
        0.3411226924835044,
        0.4124587946587038,
        0.4124587946587038,
        0.3411226924835044,
        0.21070422714350603,
        0.03571428571428571,
    ]
    barycentric = []
    for left_index in range(8):
        product = 1.0
        for right_index in range(8):
            if right_index != left_index:
                product = product * (points[left_index] - points[right_index])
        barycentric.append(1.0 / product)
    derivative = np.zeros((8, 8))
    for left_index in range(8):
        row_total = 0.0
        for right_index in range(8):
            if left_index != right_index:
                entry = (
                    barycentric[right_index]
                    / barycentric[left_index]
                    / (points[left_index] - points[right_index])
                )
                derivative[left_index, right_index] = entry
                row_total = row_total + entry
        derivative[left_index, left_index] = -row_total
    return derivative, np.asarray(weights)


DM, WEIGHTS = gll_tables()


def line(table, values):
    sums = [values[q] + values[7 - q] for q in range(4)]
    differences = [values[q] - values[7 - q] for q in range(4)]
    out = [None] * 8
    for i in range(4):
        even = odd = None
        for q in range(4):
            on_sum = float(table[i, q] + table[i, 7 - q]) / 2
            on_difference = float(table[i, q] - table[i, 7 - q]) / 2
            even = sums[q] * on_sum if even is None else even + sums[q] * on_sum
            odd = (
                differences[q] * on_difference
                if odd is None
                else odd + differences[q] * on_difference
            )
        out[i] = odd + even
        out[7 - i] = odd - even
    return out


def rows(i, j):
    return pl.ds((8 * i + j) * 8, 8)


def along_k(table_ref, block):
    wide = jnp.concatenate([block[:256], block[256:]], axis=1)
    high = wide.astype(BF16)
    low = (wide - high.astype(F32)).astype(BF16)
    both = jnp.dot(table_ref[...], high, preferred_element_type=F32)
    rest = jnp.dot(table_ref[:256], low, preferred_element_type=F32)
    out = both[:256] + (both[256:] + rest)
    return jnp.concatenate([out[:, :128], out[:, 128:]], axis=0)


def lanes(block, index):
    wide = jnp.broadcast_to(index[None], (block.shape[0] // 8, 8, 128)).reshape(block.shape)
    return jnp.take_along_axis(block, wide, axis=1, mode="promise_in_bounds")


def set_mass(weight_ref, mass_ref):
    sub = lax.broadcasted_iota(jnp.int32, (8, 128), 0)
    along = jnp.zeros((8, 128), F32)
    for k in range(8):
        along = jnp.where(sub == k, float(WEIGHTS[k]), along)
    for i in range(8):
        for j in range(8):
            r = rows(i, j)
            mass_ref[r] = weight_ref[r] * (along * float(WEIGHTS[i] * WEIGHTS[j]))


def forward(f, source, flow_ref, mass_ref, diff, table_ref, turned_ref, work, target):
    slope = along_k(table_ref, source[...])
    flux = slope * mass_ref[...]
    work[...] = flow_ref[2] * flux + diff * along_k(turned_ref, flux)
    for j in range(8):
        slopes = line(DM, [source[rows(i, j)] for i in range(8)])
        fluxes = [slopes[i] * mass_ref[rows(i, j)] for i in range(8)]
        back = line(DM.T, fluxes)
        for i in range(8):
            r = rows(i, j)
            target[r] = flow_ref[0, r] * fluxes[i] + diff * back[i]
    for i in range(8):
        slopes = line(DM, [source[rows(i, j)] for j in range(8)])
        fluxes = [slopes[j] * mass_ref[rows(i, j)] for j in range(8)]
        back = line(DM.T, fluxes)
        for j in range(8):
            r = rows(i, j)
            target[r] = -(target[r] + work[r] + (flow_ref[1, r] * fluxes[j] + diff * back[j]))


def adjoint(f, source, base, flow_ref, mass_ref, diff, table_ref, turned_ref, work, target):
    slope = along_k(table_ref, source[...])
    flux = (flow_ref[2] * source[...] + diff * slope) * mass_ref[...]
    work[...] = along_k(turned_ref, flux)
    for j in range(8):
        values = [source[rows(i, j)] for i in range(8)]
        slopes = line(DM, values)
        fluxes = [
            (flow_ref[0, rows(i, j)] * values[i] + diff * slopes[i]) * mass_ref[rows(i, j)]
            for i in range(8)
        ]
        back = line(DM.T, fluxes)
        for i in range(8):
            target[rows(i, j)] = back[i]
    for i in range(8):
        values = [source[rows(i, j)] for j in range(8)]
        slopes = line(DM, values)
        fluxes = [
            (flow_ref[1, rows(i, j)] * values[j] + diff * slopes[j]) * mass_ref[rows(i, j)]
            for j in range(8)
        ]
        back = line(DM.T, fluxes)
        for j in range(8):
            r = rows(i, j)
            target[r] = base[r] - DT * (target[r] + work[r] + back[j])


def join_heights(ref, index):
    height, _, below, above = index
    lower = ref[pl.ds(0, 64, stride=8)]
    upper = ref[pl.ds(7, 64, stride=8)]
    tall = jnp.broadcast_to(height[None], (8, 8, 128)).reshape(64, 128)
    ref[pl.ds(0, 64, stride=8)] = lower + jnp.where(tall > 0, lanes(upper, below), 0.0)
    ref[pl.ds(7, 64, stride=8)] = upper + jnp.where(tall < 127, lanes(lower, above), 0.0)


def send_faces(c, ref, index, ends, out):
    inverse = index[1]
    for way in range(2):
        i_face = ref[pl.ds(pl.multiple_of(ends[0][way] * 64, 64), 64)]
        out[way][c] = lanes(i_face, inverse)
        for i in range(8):
            j_face = ref[pl.ds(pl.multiple_of(ends[1][way] * 8 + i * 64, 8), 8)]
            out[2 + way][c, pl.ds(i * 8, 8)] = lanes(j_face, inverse)


def add_faces(c, ref, index, ends, got):
    height = index[0]
    for way in range(2):
        r = pl.ds(pl.multiple_of(ends[0][way] * 64, 64), 64)
        ref[r] = ref[r] + lanes(got[way][c], height)
    for way in range(2):
        for i in range(8):
            r = pl.ds(pl.multiple_of(ends[1][way] * 8 + i * 64, 8), 8)
            ref[r] = ref[r] + lanes(got[2 + way][c, pl.ds(i * 8, 8)], height)


def ends_of(number_ref, columns):
    column = lax.shift_right_logical(number_ref[0], 7)
    row_odd = lax.rem(lax.div(column, columns), 2)
    place_odd = lax.rem(lax.rem(column, columns), 2)
    return ((7 - 7 * row_odd, 7 * row_odd), (7 - 7 * place_odd, 7 * place_odd))


def index_of(index_ref):
    return tuple(index_ref[n] for n in range(4))


def first_kernel(
    columns,
    moment_ref,
    state_ref,
    flow_ref,
    weight_ref,
    diff_ref,
    number_ref,
    numbers_ref,
    table_ref,
    turned_ref,
    index_ref,
    joined_ref,
    ie_ref,
    io_ref,
    je_ref,
    jo_ref,
    mass_ref,
    work_ref,
):
    ends = ends_of(number_ref, columns)
    height = jnp.broadcast_to(numbers_ref[...] & 127, (8, 128))
    square = jnp.broadcast_to(height[:1].astype(F32), (128, 128)).T
    lane = lax.broadcasted_iota(jnp.int32, (128, 128), 1).astype(F32)
    row = lax.broadcasted_iota(jnp.int32, (128, 128), 0).astype(F32)
    inverse = jnp.sum(jnp.where(square == lane, row, 0.0), axis=0, keepdims=True)
    inverse = jnp.broadcast_to(inverse, (8, 128)).astype(jnp.int32)
    index = (
        height,
        inverse,
        lanes(inverse, (height - 1) & 127),
        lanes(inverse, (height + 1) & 127),
    )
    for n in range(4):
        index_ref[n] = index[n]
    set_mass(weight_ref, mass_ref)
    out = (ie_ref, io_ref, je_ref, jo_ref)

    joined_ref[6] = mass_ref[...]
    join_heights(joined_ref.at[6], index)
    send_faces(6, joined_ref.at[6], index, ends, out)

    def one_field(f, carry):
        joined_ref[3 + f] = state_ref[f]
        forward(
            f,
            moment_ref.at[f],
            flow_ref,
            mass_ref,
            diff_ref[f],
            table_ref,
            turned_ref,
            work_ref,
            joined_ref.at[f],
        )
        for c in (f, 3 + f):
            join_heights(joined_ref.at[c], index)
            send_faces(c, joined_ref.at[c], index, ends, out)
        return carry

    lax.fori_loop(0, 3, one_field, 0)


def edge_kernel(columns, count, number_ref, ie_ref, io_ref, je_ref, jo_ref, out_e, out_o):
    ends = ends_of(number_ref, columns)
    for way, (face, out) in enumerate(((je_ref, out_e), (jo_ref, out_o))):
        out[...] = face[...]
        r = pl.ds(pl.multiple_of(ends[1][way] * 8, 8), 8)
        for other, got in enumerate((ie_ref, io_ref)):
            w = pl.ds(pl.multiple_of(ends[0][other] * 8, 8), 8)
            out[:, w] = out[:, w] + got[:, r]


def second_kernel(
    columns,
    moment_ref,
    state_ref,
    flow_ref,
    weight_ref,
    diff_ref,
    number_ref,
    table_ref,
    turned_ref,
    index_ref,
    joined_ref,
    gie_ref,
    gio_ref,
    gje_ref,
    gjo_ref,
    moment_out,
    state_out,
    inverse_out,
    joined_out,
    ie_ref,
    io_ref,
    je_ref,
    jo_ref,
    mass_ref,
    work_ref,
    hold_ref,
):
    ends = ends_of(number_ref, columns)
    index = index_of(index_ref)
    set_mass(weight_ref, mass_ref)
    out = (ie_ref, io_ref, je_ref, jo_ref)
    got = (gie_ref, gio_ref, gje_ref, gjo_ref)
    hold_ref[...] = joined_ref[6]
    add_faces(6, hold_ref, index, ends, got)
    inverse_out[...] = 1.0 / hold_ref[...]

    def one_field(f, carry):
        hold_ref[...] = joined_ref[f]
        add_faces(f, hold_ref, index, ends, got)
        moment_out[f] = moment_ref[f] + DT * (hold_ref[...] * inverse_out[...])
        forward(
            f,
            moment_out.at[f],
            flow_ref,
            mass_ref,
            diff_ref[f],
            table_ref,
            turned_ref,
            work_ref,
            joined_out.at[f],
        )
        hold_ref[...] = joined_ref[3 + f]
        add_faces(3 + f, hold_ref, index, ends, got)
        hold_ref[...] = hold_ref[...] * inverse_out[...]
        adjoint(
            f,
            hold_ref,
            state_ref.at[f],
            flow_ref,
            mass_ref,
            diff_ref[f],
            table_ref,
            turned_ref,
            work_ref,
            state_out.at[f],
        )
        joined_out[3 + f] = state_out[f]
        for c in (f, 3 + f):
            join_heights(joined_out.at[c], index)
            send_faces(c, joined_out.at[c], index, ends, out)
        return carry

    lax.fori_loop(0, 3, one_field, 0)


def third_kernel(
    columns,
    moment_ref,
    state_ref,
    flow_ref,
    weight_ref,
    diff_ref,
    number_ref,
    table_ref,
    turned_ref,
    index_ref,
    inverse_ref,
    joined_ref,
    gie_ref,
    gio_ref,
    gje_ref,
    gjo_ref,
    moment_out,
    state_out,
    mass_ref,
    work_ref,
    hold_ref,
):
    ends = ends_of(number_ref, columns)
    index = index_of(index_ref)
    set_mass(weight_ref, mass_ref)
    got = (gie_ref, gio_ref, gje_ref, gjo_ref)

    def one_field(f, carry):
        hold_ref[...] = joined_ref[f]
        add_faces(f, hold_ref, index, ends, got)
        moment_out[f] = moment_ref[f] + DT * (hold_ref[...] * inverse_ref[...])
        hold_ref[...] = joined_ref[3 + f]
        add_faces(3 + f, hold_ref, index, ends, got)
        hold_ref[...] = hold_ref[...] * inverse_ref[...]
        adjoint(
            f,
            hold_ref,
            state_ref.at[f],
            flow_ref,
            mass_ref,
            diff_ref[f],
            table_ref,
            turned_ref,
            work_ref,
            state_out.at[f],
        )
        return carry

    lax.fori_loop(0, 3, one_field, 0)


VMEM = pl.BlockSpec(memory_space=pltpu.VMEM)
SMEM = pl.BlockSpec(memory_space=pltpu.SMEM)


def call(kernel, specs, shapes, scratch, flops, *operands):
    moved = sum(o.size * 4 for o in operands) + sum(int(np.prod(s)) * 4 for s, _ in shapes)
    return pl.pallas_call(
        kernel,
        out_shape=[jax.ShapeDtypeStruct(s, t) for s, t in shapes],
        in_specs=specs,
        out_specs=[VMEM] * len(shapes),
        scratch_shapes=[pltpu.VMEM(s, F32) for s in scratch],
        compiler_params=pltpu.CompilerParams(vmem_limit_bytes=32 * 1024 * 1024),
        cost_estimate=pl.CostEstimate(flops=flops, bytes_accessed=moved, transcendentals=0),
    )(*operands)


def pairings(devices):
    columns = devices // DA
    device = lambda row, place: (row * columns + place - columns // 2) % devices

    def both(pairs):
        return [(a, b) for a, b in pairs] + [(b, a) for a, b in pairs]

    along_i = [
        both([(device(r, s), device(r + 1, s)) for r in range(way, DA - 1, 2) for s in range(columns)])
        for way in range(2)
    ]
    along_j = [
        both([(device(r, s), device(r, s + 1)) for r in range(DA) for s in range(way, columns - 1, 2)])
        for way in range(2)
    ]
    return along_i, along_j


def split_table(table):
    wide = np.kron(np.eye(32), table).astype(np.float32)
    high = wide.astype(jnp.bfloat16)
    low = (wide - high.astype(np.float32)).astype(jnp.bfloat16)
    return jnp.asarray(np.concatenate([high, low], axis=0))


def shards(moment_fields, adjoint_fields, velocity, mass_weights, diffusivity, numbering):
    devices = lax.axis_size("elem")
    columns = devices // DA
    along_i, along_j = pairings(devices)
    table, turned = split_table(DM), split_table(DM.T)
    numbers = numbering.reshape(1, 128)
    whole = (3, 512, 128)

    def exchange(blocks, pairs):
        return [lax.ppermute(b, "elem", p) for b, p in zip(blocks, pairs)]

    def meet(count, faces):
        got_i = exchange(faces[:2], along_i)
        faces_j = call(
            functools.partial(edge_kernel, columns, count),
            [SMEM] + [VMEM] * 4,
            [((count, 64, 128), F32)] * 2,
            [],
            count * 64 * 128,
            numbering,
            *got_i,
            *faces[2:],
        )
        return got_i + exchange(faces_j, along_j)

    def faces_shape(count):
        return [((count, 64, 128), F32)] * 4

    index, joined, *faces = call(
        functools.partial(first_kernel, columns),
        [VMEM] * 4 + [SMEM] * 2 + [VMEM] * 3,
        [((4, 8, 128), jnp.int32), ((7, 512, 128), F32)] + faces_shape(7),
        [(512, 128)] * 2,
        20_000_000,
        moment_fields,
        adjoint_fields,
        velocity,
        mass_weights,
        diffusivity,
        numbering,
        numbers,
        table,
        turned,
    )
    got = meet(7, faces)
    moment_one, state_one, inverse, joined, *faces = call(
        functools.partial(second_kernel, columns),
        [VMEM] * 4 + [SMEM] * 2 + [VMEM] * 8,
        [(whole, F32), (whole, F32), ((512, 128), F32), ((6, 512, 128), F32)] + faces_shape(6),
        [(512, 128)] * 3,
        40_000_000,
        moment_fields,
        adjoint_fields,
        velocity,
        mass_weights,
        diffusivity,
        numbering,
        table,
        turned,
        index,
        joined,
        *got,
    )
    got = meet(6, faces)
    return tuple(
        call(
            functools.partial(third_kernel, columns),
            [VMEM] * 4 + [SMEM] * 2 + [VMEM] * 9,
            [(whole, F32), (whole, F32)],
            [(512, 128)] * 3,
            20_000_000,
            moment_one,
            state_one,
            velocity,
            mass_weights,
            diffusivity,
            numbering,
            table,
            turned,
            index,
            inverse,
            joined,
            *got,
        )
    )


def solution(mesh):
    in_specs = (
        P(None, None, "elem"),
        P(None, None, "elem"),
        P(None, None, "elem"),
        P(None, "elem"),
        P(),
        P("elem"),
    )
    out_specs = (P(None, None, "elem"), P(None, None, "elem"))
    return jax.shard_map(shards, mesh=mesh, in_specs=in_specs, out_specs=out_specs, check_vma=False)
```

```python
import functools

import jax
import jax.numpy as jnp
import numpy as np
from jax import lax
from jax.experimental import pallas as pl
from jax.experimental.pallas import tpu as pltpu
from jax.sharding import PartitionSpec as P

DA = 4
DT = 0.001
F32 = jnp.float32
BF16 = jnp.bfloat16


def gll_tables():
    points = [
        -1.0,
        -0.8717401485096066,
        -0.5917001814331423,
        -0.2092992179024789,
        0.2092992179024789,
        0.5917001814331423,
        0.8717401485096066,
        1.0,
    ]
    weights = [
        0.03571428571428571,
        0.21070422714350603,
        0.3411226924835044,
        0.4124587946587038,
        0.4124587946587038,
        0.3411226924835044,
        0.21070422714350603,
        0.03571428571428571,
    ]
    barycentric = []
    for left_index in range(8):
        product = 1.0
        for right_index in range(8):
            if right_index != left_index:
                product = product * (points[left_index] - points[right_index])
        barycentric.append(1.0 / product)
    derivative = np.zeros((8, 8))
    for left_index in range(8):
        row_total = 0.0
        for right_index in range(8):
            if left_index != right_index:
                entry = (
                    barycentric[right_index]
                    / barycentric[left_index]
                    / (points[left_index] - points[right_index])
                )
                derivative[left_index, right_index] = entry
                row_total = row_total + entry
        derivative[left_index, left_index] = -row_total
    return derivative, np.asarray(weights)


DM, WEIGHTS = gll_tables()


def line(table, values):
    sums = [values[q] + values[7 - q] for q in range(4)]
    differences = [values[q] - values[7 - q] for q in range(4)]
    out = [None] * 8
    for i in range(4):
        even = odd = None
        for q in range(4):
            on_sum = float(table[i, q] + table[i, 7 - q]) / 2
            on_difference = float(table[i, q] - table[i, 7 - q]) / 2
            even = sums[q] * on_sum if even is None else even + sums[q] * on_sum
            odd = (
                differences[q] * on_difference
                if odd is None
                else odd + differences[q] * on_difference
            )
        out[i] = odd + even
        out[7 - i] = odd - even
    return out


def rows(i, j):
    return pl.ds((8 * i + j) * 8, 8)


def along_k(table_ref, block):
    wide = jnp.concatenate([block[:256], block[256:]], axis=1)
    high = wide.astype(BF16)
    low = (wide - high.astype(F32)).astype(BF16)
    both = jnp.dot(table_ref[...], high, preferred_element_type=F32)
    rest = jnp.dot(table_ref[:256], low, preferred_element_type=F32)
    out = both[:256] + (both[256:] + rest)
    return jnp.concatenate([out[:, :128], out[:, 128:]], axis=0)


def write_table(table, table_ref):
    sub = lax.broadcasted_iota(jnp.int32, (8, 128), 0)
    lane = lax.broadcasted_iota(jnp.int32, (8, 128), 1)
    base = jnp.zeros((8, 128), F32)
    for i in range(8):
        one_row = jnp.zeros((8, 128), F32)
        for q in range(8):
            one_row = jnp.where((lane & 7) == q, float(table[i, q]), one_row)
        base = jnp.where(sub == i, one_row, base)
    high = base.astype(BF16).astype(F32)
    block = lax.shift_right_logical(lane, 3)
    zero = jnp.zeros((8, 128), F32)
    for part, values in enumerate((high, base - high)):
        for a in range(0, 32, 2):
            pair = [jnp.where(block == (a + n) % 16, values, zero) for n in range(2)]
            pair = jnp.concatenate(pair, axis=0)
            wide = [pair, jnp.zeros((16, 128), F32)]
            wide = jnp.concatenate(wide if a < 16 else wide[::-1], axis=1)
            table_ref[pl.ds(256 * part + 8 * a, 16)] = wide.astype(BF16)


def lanes(block, index):
    wide = jnp.broadcast_to(index[None], (block.shape[0] // 8, 8, 128)).reshape(block.shape)
    return jnp.take_along_axis(block, wide, axis=1, mode="promise_in_bounds")


def set_mass(weight_ref, mass_ref):
    sub = lax.broadcasted_iota(jnp.int32, (8, 128), 0)
    along = jnp.zeros((8, 128), F32)
    for k in range(8):
        along = jnp.where(sub == k, float(WEIGHTS[k]), along)
    for i in range(8):
        for j in range(8):
            r = rows(i, j)
            mass_ref[r] = weight_ref[r] * (along * float(WEIGHTS[i] * WEIGHTS[j]))


def forward(f, source, flow_ref, mass_ref, diff, table_ref, turned_ref, work, target):
    slope = along_k(table_ref, source[...])
    flux = slope * mass_ref[...]
    work[...] = flow_ref[2] * flux + diff * along_k(turned_ref, flux)
    for j in range(8):
        slopes = line(DM, [source[rows(i, j)] for i in range(8)])
        fluxes = [slopes[i] * mass_ref[rows(i, j)] for i in range(8)]
        back = line(DM.T, fluxes)
        for i in range(8):
            r = rows(i, j)
            target[r] = flow_ref[0, r] * fluxes[i] + diff * back[i]
    for i in range(8):
        slopes = line(DM, [source[rows(i, j)] for j in range(8)])
        fluxes = [slopes[j] * mass_ref[rows(i, j)] for j in range(8)]
        back = line(DM.T, fluxes)
        for j in range(8):
            r = rows(i, j)
            target[r] = -(target[r] + work[r] + (flow_ref[1, r] * fluxes[j] + diff * back[j]))


def adjoint(f, source, base, flow_ref, mass_ref, diff, table_ref, turned_ref, work, target):
    slope = along_k(table_ref, source[...])
    flux = (flow_ref[2] * source[...] + diff * slope) * mass_ref[...]
    work[...] = along_k(turned_ref, flux)
    for j in range(8):
        values = [source[rows(i, j)] for i in range(8)]
        slopes = line(DM, values)
        fluxes = [
            (flow_ref[0, rows(i, j)] * values[i] + diff * slopes[i]) * mass_ref[rows(i, j)]
            for i in range(8)
        ]
        back = line(DM.T, fluxes)
        for i in range(8):
            target[rows(i, j)] = back[i]
    for i in range(8):
        values = [source[rows(i, j)] for j in range(8)]
        slopes = line(DM, values)
        fluxes = [
            (flow_ref[1, rows(i, j)] * values[j] + diff * slopes[j]) * mass_ref[rows(i, j)]
            for j in range(8)
        ]
        back = line(DM.T, fluxes)
        for j in range(8):
            r = rows(i, j)
            target[r] = base[r] - DT * (target[r] + work[r] + back[j])


def join_heights(ref, index):
    height, _, below, above = index
    lower = ref[pl.ds(0, 64, stride=8)]
    upper = ref[pl.ds(7, 64, stride=8)]
    tall = jnp.broadcast_to(height[None], (8, 8, 128)).reshape(64, 128)
    ref[pl.ds(0, 64, stride=8)] = lower + jnp.where(tall > 0, lanes(upper, below), 0.0)
    ref[pl.ds(7, 64, stride=8)] = upper + jnp.where(tall < 127, lanes(lower, above), 0.0)


def send_faces(c, ref, index, ends, out):
    inverse = index[1]
    for way in range(2):
        i_face = ref[pl.ds(pl.multiple_of(ends[0][way] * 64, 64), 64)]
        out[way][c] = lanes(i_face, inverse)
        for i in range(8):
            j_face = ref[pl.ds(pl.multiple_of(ends[1][way] * 8 + i * 64, 8), 8)]
            out[2 + way][c, pl.ds(i * 8, 8)] = lanes(j_face, inverse)


def partner(ends, axis, way):
    odd, inside = ends[2 + axis]
    return (odd, inside) if way else (1 - odd, 1.0)


def add_faces(c, ref, index, ends, got):
    height = index[0]
    for way in range(2):
        slot, weight = partner(ends, 0, way)
        r = pl.ds(pl.multiple_of(ends[0][way] * 64, 64), 64)
        ref[r] = ref[r] + lanes(got[way][slot, c], height) * weight
    for way in range(2):
        slot, weight = partner(ends, 1, way)
        for i in range(8):
            r = pl.ds(pl.multiple_of(ends[1][way] * 8 + i * 64, 8), 8)
            ref[r] = ref[r] + lanes(got[2 + way][slot, c, pl.ds(i * 8, 8)], height) * weight


def ends_of(columns):
    column = lax.rem(lax.axis_index("elem") + columns // 2, columns * DA)
    row, place = lax.div(column, columns), lax.rem(column, columns)
    row_odd, place_odd = lax.rem(row, 2), lax.rem(place, 2)
    row_inside = jnp.where((row > 0) & (row < DA - 1), 1.0, 0.0)
    place_inside = jnp.where((place > 0) & (place < columns - 1), 1.0, 0.0)
    return (
        (7 - 7 * row_odd, 7 * row_odd),
        (7 - 7 * place_odd, 7 * place_odd),
        (row_odd, row_inside),
        (place_odd, place_inside),
    )


def index_of(index_ref):
    return tuple(index_ref[n] for n in range(4))


def first_kernel(
    columns,
    moment_far,
    state_far,
    flow_far,
    weight_far,
    diff_far,
    numbers_far,
    table_ref,
    turned_ref,
    index_ref,
    joined_ref,
    ie_ref,
    io_ref,
    je_ref,
    jo_ref,
    mass_ref,
    work_ref,
    moment_ref,
    state_ref,
    flow_ref,
    weight_ref,
    numbers_ref,
    diff_ref,
    arrived,
):
    far = (numbers_far, weight_far, state_far, moment_far, flow_far, diff_far)
    near = (numbers_ref, weight_ref, state_ref, moment_ref, flow_ref, diff_ref)
    copies = [pltpu.make_async_copy(a, b, arrived.at[n]) for n, (a, b) in enumerate(zip(far, near))]
    for copy in copies:
        copy.start()
    write_table(DM, table_ref)
    write_table(DM.T, turned_ref)
    ends = ends_of(columns)
    copies[0].wait()
    height = jnp.broadcast_to(numbers_ref[...] & 127, (8, 128))
    square = jnp.broadcast_to(height[:1].astype(F32), (128, 128)).T
    lane = lax.broadcasted_iota(jnp.int32, (128, 128), 1).astype(F32)
    row = lax.broadcasted_iota(jnp.int32, (128, 128), 0).astype(F32)
    inverse = jnp.sum(jnp.where(square == lane, row, 0.0), axis=0, keepdims=True)
    inverse = jnp.broadcast_to(inverse, (8, 128)).astype(jnp.int32)
    index = (
        height,
        inverse,
        lanes(inverse, (height - 1) & 127),
        lanes(inverse, (height + 1) & 127),
    )
    for n in range(4):
        index_ref[n] = index[n]
    copies[1].wait()
    set_mass(weight_ref, mass_ref)
    out = (ie_ref, io_ref, je_ref, jo_ref)

    joined_ref[6] = mass_ref[...]
    join_heights(joined_ref.at[6], index)
    send_faces(6, joined_ref.at[6], index, ends, out)
    for copy in copies[2:]:
        copy.wait()

    def one_field(f, carry):
        joined_ref[3 + f] = state_ref[f]
        forward(
            f,
            moment_ref.at[f],
            flow_ref,
            mass_ref,
            diff_ref[f],
            table_ref,
            turned_ref,
            work_ref,
            joined_ref.at[f],
        )
        for c in (f, 3 + f):
            join_heights(joined_ref.at[c], index)
            send_faces(c, joined_ref.at[c], index, ends, out)
        return carry

    lax.fori_loop(0, 3, one_field, 0)


def edge_kernel(columns, ie_ref, io_ref, je_ref, jo_ref, out_e, out_o):
    ends = ends_of(columns)
    for way, (face, out) in enumerate(((je_ref, out_e), (jo_ref, out_o))):
        out[...] = face[...]
        r = pl.ds(pl.multiple_of(ends[1][way] * 8, 8), 8)
        for other, got in enumerate((ie_ref, io_ref)):
            w = pl.ds(pl.multiple_of(ends[0][other] * 8, 8), 8)
            slot, weight = partner(ends, 0, other)
            out[:, w] = out[:, w] + got[slot, :, r] * weight


def second_kernel(
    columns,
    moment_ref,
    state_ref,
    flow_ref,
    weight_ref,
    diff_ref,
    table_ref,
    turned_ref,
    index_ref,
    joined_ref,
    gie_ref,
    gio_ref,
    gje_ref,
    gjo_ref,
    moment_out,
    state_out,
    inverse_out,
    joined_out,
    ie_ref,
    io_ref,
    je_ref,
    jo_ref,
    mass_ref,
    work_ref,
    hold_ref,
):
    ends = ends_of(columns)
    index = index_of(index_ref)
    set_mass(weight_ref, mass_ref)
    out = (ie_ref, io_ref, je_ref, jo_ref)
    got = (gie_ref, gio_ref, gje_ref, gjo_ref)
    hold_ref[...] = joined_ref[6]
    add_faces(6, hold_ref, index, ends, got)
    inverse_out[...] = 1.0 / hold_ref[...]

    def one_field(f, carry):
        hold_ref[...] = joined_ref[f]
        add_faces(f, hold_ref, index, ends, got)
        moment_out[f] = moment_ref[f] + DT * (hold_ref[...] * inverse_out[...])
        forward(
            f,
            moment_out.at[f],
            flow_ref,
            mass_ref,
            diff_ref[f],
            table_ref,
            turned_ref,
            work_ref,
            joined_out.at[f],
        )
        hold_ref[...] = joined_ref[3 + f]
        add_faces(3 + f, hold_ref, index, ends, got)
        hold_ref[...] = hold_ref[...] * inverse_out[...]
        adjoint(
            f,
            hold_ref,
            state_ref.at[f],
            flow_ref,
            mass_ref,
            diff_ref[f],
            table_ref,
            turned_ref,
            work_ref,
            state_out.at[f],
        )
        joined_out[3 + f] = state_out[f]
        for c in (f, 3 + f):
            join_heights(joined_out.at[c], index)
            send_faces(c, joined_out.at[c], index, ends, out)
        return carry

    lax.fori_loop(0, 3, one_field, 0)


def third_kernel(
    columns,
    moment_ref,
    state_ref,
    flow_ref,
    weight_ref,
    diff_ref,
    table_ref,
    turned_ref,
    index_ref,
    inverse_ref,
    joined_ref,
    gie_ref,
    gio_ref,
    gje_ref,
    gjo_ref,
    moment_out,
    state_out,
    mass_ref,
    work_ref,
    hold_ref,
):
    ends = ends_of(columns)
    index = index_of(index_ref)
    set_mass(weight_ref, mass_ref)
    got = (gie_ref, gio_ref, gje_ref, gjo_ref)

    def one_field(f, carry):
        hold_ref[...] = joined_ref[f]
        add_faces(f, hold_ref, index, ends, got)
        moment_out[f] = moment_ref[f] + DT * (hold_ref[...] * inverse_ref[...])
        hold_ref[...] = joined_ref[3 + f]
        add_faces(3 + f, hold_ref, index, ends, got)
        hold_ref[...] = hold_ref[...] * inverse_ref[...]
        adjoint(
            f,
            hold_ref,
            state_ref.at[f],
            flow_ref,
            mass_ref,
            diff_ref[f],
            table_ref,
            turned_ref,
            work_ref,
            state_out.at[f],
        )
        return carry

    lax.fori_loop(0, 3, one_field, 0)


VMEM = pl.BlockSpec(memory_space=pltpu.VMEM)
SMEM = pl.BlockSpec(memory_space=pltpu.SMEM)
FAR = pl.BlockSpec(memory_space=pltpu.HBM)


def call(kernel, specs, shapes, scratch, flops, *operands):
    moved = sum(o.size * 4 for o in operands) + sum(int(np.prod(s)) * 4 for s, _ in shapes)
    return pl.pallas_call(
        kernel,
        out_shape=[jax.ShapeDtypeStruct(s, t) for s, t in shapes],
        in_specs=specs,
        out_specs=[VMEM] * len(shapes),
        scratch_shapes=scratch,
        compiler_params=pltpu.CompilerParams(vmem_limit_bytes=32 * 1024 * 1024),
        cost_estimate=pl.CostEstimate(flops=flops, bytes_accessed=moved, transcendentals=0),
    )(*operands)


def pairings(devices):
    columns = devices // DA
    device = lambda row, place: (row * columns + place - columns // 2) % devices

    along_i = [
        [(device(r, s), device((r + 1) % DA, s)) for r in range(way, DA, 2) for s in range(columns)]
        for way in range(2)
    ]
    along_j = [
        [
            (device(r, s), device(r, (s + 1) % columns))
            for r in range(DA)
            for s in range(way, columns, 2)
        ]
        for way in range(2)
    ]
    return along_i, along_j


def shards(moment_fields, adjoint_fields, velocity, mass_weights, diffusivity, numbering):
    devices = lax.axis_size("elem")
    columns = devices // DA
    along_i, along_j = pairings(devices)
    numbers = numbering.reshape(1, 128)
    whole = (3, 512, 128)

    def exchange(blocks, pairs):
        return [
            lax.all_gather(b, "elem", axis_index_groups=p) for b, p in zip(blocks, pairs)
        ]

    def meet(count, faces):
        got_i = exchange(faces[:2], along_i)
        faces_j = call(
            functools.partial(edge_kernel, columns),
            [VMEM] * 4,
            [((count, 64, 128), F32)] * 2,
            [],
            count * 64 * 128,
            *got_i,
            *faces[2:],
        )
        return got_i + exchange(faces_j, along_j)

    def far(array):
        return pltpu.with_memory_space_constraint(array, pltpu.HBM)

    def faces_shape(count):
        return [((count, 64, 128), F32)] * 4

    table, turned, index, joined, *faces = call(
        functools.partial(first_kernel, columns),
        [FAR] * 6,
        [((512, 256), BF16)] * 2 + [((4, 8, 128), jnp.int32), ((7, 512, 128), F32)] + faces_shape(7),
        [pltpu.VMEM((512, 128), F32)] * 2
        + [pltpu.VMEM(whole, F32)] * 3
        + [pltpu.VMEM((512, 128), F32), pltpu.VMEM((1, 128), jnp.int32)]
        + [pltpu.SMEM((3,), F32), pltpu.SemaphoreType.DMA((6,))],
        20_000_000,
        *map(far, (moment_fields, adjoint_fields, velocity, mass_weights)),
        *map(far, (diffusivity, numbers)),
    )
    got = meet(7, faces)
    moment_one, state_one, inverse, joined, *faces = call(
        functools.partial(second_kernel, columns),
        [VMEM] * 4 + [SMEM] + [VMEM] * 8,
        [(whole, F32), (whole, F32), ((512, 128), F32), ((6, 512, 128), F32)] + faces_shape(6),
        [pltpu.VMEM((512, 128), F32)] * 3,
        40_000_000,
        moment_fields,
        adjoint_fields,
        velocity,
        mass_weights,
        diffusivity,
        table,
        turned,
        index,
        joined,
        *got,
    )
    got = meet(6, faces)
    return tuple(
        call(
            functools.partial(third_kernel, columns),
            [VMEM] * 4 + [SMEM] + [VMEM] * 9,
            [(whole, F32), (whole, F32)],
            [pltpu.VMEM((512, 128), F32)] * 3,
            20_000_000,
            moment_one,
            state_one,
            velocity,
            mass_weights,
            diffusivity,
            table,
            turned,
            index,
            inverse,
            joined,
            *got,
        )
    )


def solution(mesh):
    in_specs = (
        P(None, None, "elem"),
        P(None, None, "elem"),
        P(None, None, "elem"),
        P(None, "elem"),
        P(),
        P("elem"),
    )
    out_specs = (P(None, None, "elem"), P(None, None, "elem"))
    return jax.shard_map(shards, mesh=mesh, in_specs=in_specs, out_specs=out_specs, check_vma=False)
```

```python
import functools

import jax
import jax.numpy as jnp
import numpy as np
from jax import lax
from jax.experimental import pallas as pl
from jax.experimental.pallas import tpu as pltpu
from jax.sharding import PartitionSpec as P

DA = 4
DT = 0.001
F32 = jnp.float32
BF16 = jnp.bfloat16


def gll_tables():
    points = [
        -1.0,
        -0.8717401485096066,
        -0.5917001814331423,
        -0.2092992179024789,
        0.2092992179024789,
        0.5917001814331423,
        0.8717401485096066,
        1.0,
    ]
    weights = [
        0.03571428571428571,
        0.21070422714350603,
        0.3411226924835044,
        0.4124587946587038,
        0.4124587946587038,
        0.3411226924835044,
        0.21070422714350603,
        0.03571428571428571,
    ]
    barycentric = []
    for left_index in range(8):
        product = 1.0
        for right_index in range(8):
            if right_index != left_index:
                product = product * (points[left_index] - points[right_index])
        barycentric.append(1.0 / product)
    derivative = np.zeros((8, 8))
    for left_index in range(8):
        row_total = 0.0
        for right_index in range(8):
            if left_index != right_index:
                entry = (
                    barycentric[right_index]
                    / barycentric[left_index]
                    / (points[left_index] - points[right_index])
                )
                derivative[left_index, right_index] = entry
                row_total = row_total + entry
        derivative[left_index, left_index] = -row_total
    return derivative, np.asarray(weights)


DM, WEIGHTS = gll_tables()


def line(table, values):
    sums = [values[q] + values[7 - q] for q in range(4)]
    differences = [values[q] - values[7 - q] for q in range(4)]
    out = [None] * 8
    for i in range(4):
        even = odd = None
        for q in range(4):
            on_sum = float(table[i, q] + table[i, 7 - q]) / 2
            on_difference = float(table[i, q] - table[i, 7 - q]) / 2
            even = sums[q] * on_sum if even is None else even + sums[q] * on_sum
            odd = (
                differences[q] * on_difference
                if odd is None
                else odd + differences[q] * on_difference
            )
        out[i] = odd + even
        out[7 - i] = odd - even
    return out


def rows(i, j):
    return pl.ds((8 * i + j) * 8, 8)


def along_k(table_ref, block):
    wide = jnp.concatenate([block[:256], block[256:]], axis=1)
    high = wide.astype(BF16)
    low = (wide - high.astype(F32)).astype(BF16)
    both = jnp.dot(table_ref[...], high, preferred_element_type=F32)
    rest = jnp.dot(table_ref[:256], low, preferred_element_type=F32)
    out = both[:256] + (both[256:] + rest)
    return jnp.concatenate([out[:, :128], out[:, 128:]], axis=0)


def write_table(table, table_ref):
    sub = lax.broadcasted_iota(jnp.int32, (8, 128), 0)
    lane = lax.broadcasted_iota(jnp.int32, (8, 128), 1)
    base = jnp.zeros((8, 128), F32)
    for i in range(8):
        one_row = jnp.zeros((8, 128), F32)
        for q in range(8):
            one_row = jnp.where((lane & 7) == q, float(table[i, q]), one_row)
        base = jnp.where(sub == i, one_row, base)
    high = base.astype(BF16).astype(F32)
    block = lax.shift_right_logical(lane, 3)
    zero = jnp.zeros((8, 128), F32)
    for part, values in enumerate((high, base - high)):
        for a in range(0, 32, 2):
            pair = [jnp.where(block == (a + n) % 16, values, zero) for n in range(2)]
            pair = jnp.concatenate(pair, axis=0)
            wide = [pair, jnp.zeros((16, 128), F32)]
            wide = jnp.concatenate(wide if a < 16 else wide[::-1], axis=1)
            table_ref[pl.ds(256 * part + 8 * a, 16)] = wide.astype(BF16)


def lanes(block, index):
    wide = jnp.broadcast_to(index[None], (block.shape[0] // 8, 8, 128)).reshape(block.shape)
    return jnp.take_along_axis(block, wide, axis=1, mode="promise_in_bounds")


def set_mass(weight_ref, mass_ref):
    sub = lax.broadcasted_iota(jnp.int32, (8, 128), 0)
    along = jnp.zeros((8, 128), F32)
    for k in range(8):
        along = jnp.where(sub == k, float(WEIGHTS[k]), along)
    for i in range(8):
        for j in range(8):
            r = rows(i, j)
            mass_ref[r] = weight_ref[r] * (along * float(WEIGHTS[i] * WEIGHTS[j]))


def forward(source, flow_ref, mass_ref, diff, table_ref, turned_ref, work, target):
    slope = along_k(table_ref, source[...])
    flux = slope * mass_ref[...]
    work[...] = flow_ref[2] * flux + diff * along_k(turned_ref, flux)
    for j in range(8):
        slopes = line(DM, [source[rows(i, j)] for i in range(8)])
        fluxes = [slopes[i] * mass_ref[rows(i, j)] for i in range(8)]
        back = line(DM.T, fluxes)
        for i in range(8):
            r = rows(i, j)
            target[r] = flow_ref[0, r] * fluxes[i] + diff * back[i]
    for i in range(8):
        slopes = line(DM, [source[rows(i, j)] for j in range(8)])
        fluxes = [slopes[j] * mass_ref[rows(i, j)] for j in range(8)]
        back = line(DM.T, fluxes)
        for j in range(8):
            r = rows(i, j)
            target[r] = -(target[r] + work[r] + (flow_ref[1, r] * fluxes[j] + diff * back[j]))


def adjoint(source, base, flow_ref, mass_ref, diff, table_ref, turned_ref, work, target):
    slope = along_k(table_ref, source[...])
    flux = (flow_ref[2] * source[...] + diff * slope) * mass_ref[...]
    work[...] = along_k(turned_ref, flux)
    for j in range(8):
        values = [source[rows(i, j)] for i in range(8)]
        slopes = line(DM, values)
        fluxes = [
            (flow_ref[0, rows(i, j)] * values[i] + diff * slopes[i]) * mass_ref[rows(i, j)]
            for i in range(8)
        ]
        back = line(DM.T, fluxes)
        for i in range(8):
            target[rows(i, j)] = back[i]
    for i in range(8):
        values = [source[rows(i, j)] for j in range(8)]
        slopes = line(DM, values)
        fluxes = [
            (flow_ref[1, rows(i, j)] * values[j] + diff * slopes[j]) * mass_ref[rows(i, j)]
            for j in range(8)
        ]
        back = line(DM.T, fluxes)
        for j in range(8):
            r = rows(i, j)
            target[r] = base[r] - DT * (target[r] + work[r] + back[j])


def join_heights(ref, index):
    height, _, below, above = index
    lower = ref[pl.ds(0, 64, stride=8)]
    upper = ref[pl.ds(7, 64, stride=8)]
    tall = jnp.broadcast_to(height[None], (8, 8, 128)).reshape(64, 128)
    ref[pl.ds(0, 64, stride=8)] = lower + jnp.where(tall > 0, lanes(upper, below), 0.0)
    ref[pl.ds(7, 64, stride=8)] = upper + jnp.where(tall < 127, lanes(lower, above), 0.0)


def send_faces(c, ref, index, ends, out):
    inverse = index[1]
    for way in range(2):
        i_face = ref[pl.ds(pl.multiple_of(ends[0][way] * 64, 64), 64)]
        out[way][c] = lanes(i_face, inverse)
        for i in range(8):
            j_face = ref[pl.ds(pl.multiple_of(ends[1][way] * 8 + i * 64, 8), 8)]
            out[2 + way][c, pl.ds(i * 8, 8)] = lanes(j_face, inverse)


def add_faces(c, ref, index, ends, got):
    height = index[0]
    for way in range(2):
        r = pl.ds(pl.multiple_of(ends[0][way] * 64, 64), 64)
        ref[r] = ref[r] + lanes(got[way][c], height)
    for way in range(2):
        for i in range(8):
            r = pl.ds(pl.multiple_of(ends[1][way] * 8 + i * 64, 8), 8)
            ref[r] = ref[r] + lanes(got[2 + way][c, pl.ds(i * 8, 8)], height)


def ends_of(columns):
    column = lax.rem(lax.axis_index("elem") + columns // 2, columns * DA)
    row_odd = lax.rem(lax.div(column, columns), 2)
    place_odd = lax.rem(lax.rem(column, columns), 2)
    return ((7 - 7 * row_odd, 7 * row_odd), (7 - 7 * place_odd, 7 * place_odd))


def index_of(index_ref):
    return tuple(index_ref[n] for n in range(4))


def index_kernel(
    columns,
    state_far,
    weight_far,
    numbers_far,
    table_ref,
    turned_ref,
    index_ref,
    mass_ref,
    joined_ref,
    ie_ref,
    io_ref,
    je_ref,
    jo_ref,
    weight_ref,
    numbers_ref,
    arrived,
):
    far = (numbers_far, weight_far, state_far)
    near = (numbers_ref, weight_ref, joined_ref.at[pl.ds(0, 3)])
    copies = [pltpu.make_async_copy(a, b, arrived.at[n]) for n, (a, b) in enumerate(zip(far, near))]
    for copy in copies:
        copy.start()
    write_table(DM, table_ref)
    write_table(DM.T, turned_ref)
    ends = ends_of(columns)
    copies[0].wait()
    height = jnp.broadcast_to(numbers_ref[...] & 127, (8, 128))
    square = jnp.broadcast_to(height[:1].astype(F32), (128, 128)).T
    lane = lax.broadcasted_iota(jnp.int32, (128, 128), 1).astype(F32)
    row = lax.broadcasted_iota(jnp.int32, (128, 128), 0).astype(F32)
    inverse = jnp.sum(jnp.where(square == lane, row, 0.0), axis=0, keepdims=True)
    inverse = jnp.broadcast_to(inverse, (8, 128)).astype(jnp.int32)
    index = (
        height,
        inverse,
        lanes(inverse, (height - 1) & 127),
        lanes(inverse, (height + 1) & 127),
    )
    for n in range(4):
        index_ref[n] = index[n]
    copies[1].wait()
    set_mass(weight_ref, mass_ref)
    joined_ref[3] = mass_ref[...]
    copies[2].wait()
    out = (ie_ref, io_ref, je_ref, jo_ref)
    for c in range(4):
        join_heights(joined_ref.at[c], index)
        send_faces(c, joined_ref.at[c], index, ends, out)


def moment_kernel(
    columns,
    moment_ref,
    flow_ref,
    diff_ref,
    table_ref,
    turned_ref,
    index_ref,
    mass_ref,
    joined_ref,
    ie_ref,
    io_ref,
    je_ref,
    jo_ref,
    work_ref,
):
    ends = ends_of(columns)
    index = index_of(index_ref)
    out = (ie_ref, io_ref, je_ref, jo_ref)

    def one_field(f, carry):
        forward(
            moment_ref.at[f],
            flow_ref,
            mass_ref,
            diff_ref[f],
            table_ref,
            turned_ref,
            work_ref,
            joined_ref.at[f],
        )
        join_heights(joined_ref.at[f], index)
        send_faces(f, joined_ref.at[f], index, ends, out)
        return carry

    lax.fori_loop(0, 3, one_field, 0)


def edge_kernel(columns, ie_ref, io_ref, je_ref, jo_ref, out_e, out_o):
    ends = ends_of(columns)
    for way, (face, out) in enumerate(((je_ref, out_e), (jo_ref, out_o))):
        out[...] = face[...]
        r = pl.ds(pl.multiple_of(ends[1][way] * 8, 8), 8)
        for other, got in enumerate((ie_ref, io_ref)):
            w = pl.ds(pl.multiple_of(ends[0][other] * 8, 8), 8)
            out[:, w] = out[:, w] + got[:, r]


def state_kernel(
    columns,
    first,
    state_ref,
    flow_ref,
    diff_ref,
    table_ref,
    turned_ref,
    index_ref,
    mass_ref,
    joined_ref,
    *refs,
):
    ends = ends_of(columns)
    index = index_of(index_ref)
    if first:
        got, (inverse_ref, state_out, joined_out), refs = refs[:4], refs[4:7], refs[7:]
        out, (work_ref, hold_ref) = refs[:4], refs[4:]
        hold_ref[...] = joined_ref[3]
        add_faces(3, hold_ref, index, ends, got)
        inverse_ref[...] = 1.0 / hold_ref[...]
    else:
        inverse_ref, *got = refs[:5]
        state_out, work_ref, hold_ref = refs[5:]

    def one_field(f, carry):
        hold_ref[...] = joined_ref[f]
        add_faces(f, hold_ref, index, ends, got)
        hold_ref[...] = hold_ref[...] * inverse_ref[...]
        adjoint(
            hold_ref,
            state_ref.at[f],
            flow_ref,
            mass_ref,
            diff_ref[f],
            table_ref,
            turned_ref,
            work_ref,
            state_out.at[f],
        )
        if first:
            joined_out[f] = state_out[f]
            join_heights(joined_out.at[f], index)
            send_faces(f, joined_out.at[f], index, ends, out)
        return carry

    lax.fori_loop(0, 3, one_field, 0)


def moment_step(f, ends, index, moment_ref, joined_ref, inverse_ref, got, hold_ref, moment_out):
    hold_ref[...] = joined_ref[f]
    add_faces(f, hold_ref, index, ends, got)
    moment_out[f] = moment_ref[f] + DT * (hold_ref[...] * inverse_ref[...])


def middle_kernel(
    columns,
    moment_ref,
    flow_ref,
    diff_ref,
    table_ref,
    turned_ref,
    index_ref,
    mass_ref,
    inverse_ref,
    joined_ref,
    gie_ref,
    gio_ref,
    gje_ref,
    gjo_ref,
    moment_out,
    joined_out,
    ie_ref,
    io_ref,
    je_ref,
    jo_ref,
    work_ref,
    hold_ref,
):
    ends = ends_of(columns)
    index = index_of(index_ref)
    out = (ie_ref, io_ref, je_ref, jo_ref)
    got = (gie_ref, gio_ref, gje_ref, gjo_ref)

    def one_field(f, carry):
        moment_step(f, ends, index, moment_ref, joined_ref, inverse_ref, got, hold_ref, moment_out)
        forward(
            moment_out.at[f],
            flow_ref,
            mass_ref,
            diff_ref[f],
            table_ref,
            turned_ref,
            work_ref,
            joined_out.at[f],
        )
        join_heights(joined_out.at[f], index)
        send_faces(f, joined_out.at[f], index, ends, out)
        return carry

    lax.fori_loop(0, 3, one_field, 0)


def last_kernel(
    columns,
    moment_ref,
    index_ref,
    inverse_ref,
    joined_ref,
    gie_ref,
    gio_ref,
    gje_ref,
    gjo_ref,
    moment_out,
    hold_ref,
):
    ends = ends_of(columns)
    index = index_of(index_ref)
    got = (gie_ref, gio_ref, gje_ref, gjo_ref)

    def one_field(f, carry):
        moment_step(f, ends, index, moment_ref, joined_ref, inverse_ref, got, hold_ref, moment_out)
        return carry

    lax.fori_loop(0, 3, one_field, 0)


VMEM = pl.BlockSpec(memory_space=pltpu.VMEM)
SMEM = pl.BlockSpec(memory_space=pltpu.SMEM)
FAR = pl.BlockSpec(memory_space=pltpu.HBM)


def call(kernel, specs, shapes, scratch, flops, *operands):
    moved = sum(o.size * 4 for o in operands) + sum(int(np.prod(s)) * 4 for s, _ in shapes)
    return pl.pallas_call(
        kernel,
        out_shape=[jax.ShapeDtypeStruct(s, t) for s, t in shapes],
        in_specs=specs,
        out_specs=[VMEM] * len(shapes),
        scratch_shapes=scratch,
        compiler_params=pltpu.CompilerParams(vmem_limit_bytes=32 * 1024 * 1024),
        cost_estimate=pl.CostEstimate(flops=flops, bytes_accessed=moved, transcendentals=0),
    )(*operands)


def pairings(devices):
    columns = devices // DA
    device = lambda row, place: (row * columns + place - columns // 2) % devices

    def both(pairs):
        return [(a, b) for a, b in pairs] + [(b, a) for a, b in pairs]

    along_i = [
        both([(device(r, s), device(r + 1, s)) for r in range(way, DA - 1, 2) for s in range(columns)])
        for way in range(2)
    ]
    along_j = [
        both([(device(r, s), device(r, s + 1)) for r in range(DA) for s in range(way, columns - 1, 2)])
        for way in range(2)
    ]
    return along_i, along_j


def shards(moment_fields, adjoint_fields, velocity, mass_weights, diffusivity, numbering):
    devices = lax.axis_size("elem")
    columns = devices // DA
    along_i, along_j = pairings(devices)
    whole, block = ((3, 512, 128), F32), ((512, 128), F32)
    work = pltpu.VMEM((512, 128), F32)

    def exchange(blocks, pairs):
        return [lax.ppermute(b, "elem", p) for b, p in zip(blocks, pairs)]

    def meet(count, faces):
        got_i = exchange(faces[:2], along_i)
        faces_j = call(
            functools.partial(edge_kernel, columns),
            [VMEM] * 4,
            [((count, 64, 128), F32)] * 2,
            [],
            count * 64 * 128,
            *got_i,
            *faces[2:],
        )
        return got_i + exchange(faces_j, along_j)

    def far(array):
        return pltpu.with_memory_space_constraint(array, pltpu.HBM)

    def faces_shape(count):
        return [((count, 64, 128), F32)] * 4

    table, turned, index, mass, joined_state, *faces_state = call(
        functools.partial(index_kernel, columns),
        [FAR] * 3,
        [((512, 256), BF16)] * 2
        + [((4, 8, 128), jnp.int32), block, ((4, 512, 128), F32)]
        + faces_shape(4),
        [
            work,
            pltpu.VMEM((1, 128), jnp.int32),
            pltpu.SemaphoreType.DMA((3,)),
        ],
        1_000_000,
        *map(far, (adjoint_fields, mass_weights, numbering.reshape(1, 128))),
    )
    tables = (diffusivity, table, turned, index, mass)
    got_state = meet(4, faces_state)
    joined_moment, *faces_moment = call(
        functools.partial(moment_kernel, columns),
        [VMEM] * 2 + [SMEM] + [VMEM] * 4,
        [whole] + faces_shape(3),
        [work],
        20_000_000,
        moment_fields,
        velocity,
        *tables,
    )
    got_moment = meet(3, faces_moment)
    inverse, state, joined_state, *faces_state = call(
        functools.partial(state_kernel, columns, True),
        [VMEM] * 2 + [SMEM] + [VMEM] * 9,
        [block, whole, whole] + faces_shape(3),
        [work] * 2,
        20_000_000,
        adjoint_fields,
        velocity,
        *tables,
        joined_state,
        *got_state,
    )
    got_state = meet(3, faces_state)
    moment, joined_moment, *faces_moment = call(
        functools.partial(middle_kernel, columns),
        [VMEM] * 2 + [SMEM] + [VMEM] * 10,
        [whole, whole] + faces_shape(3),
        [work] * 2,
        20_000_000,
        moment_fields,
        velocity,
        *tables,
        inverse,
        joined_moment,
        *got_moment,
    )
    got_moment = meet(3, faces_moment)
    (state,) = call(
        functools.partial(state_kernel, columns, False),
        [VMEM] * 2 + [SMEM] + [VMEM] * 10,
        [whole],
        [work] * 2,
        20_000_000,
        state,
        velocity,
        *tables,
        joined_state,
        inverse,
        *got_state,
    )
    (moment,) = call(
        functools.partial(last_kernel, columns),
        [VMEM] * 8,
        [whole],
        [work],
        1_000_000,
        moment,
        index,
        inverse,
        joined_moment,
        *got_moment,
    )
    return moment, state


def solution(mesh):
    in_specs = (
        P(None, None, "elem"),
        P(None, None, "elem"),
        P(None, None, "elem"),
        P(None, "elem"),
        P(),
        P("elem"),
    )
    out_specs = (P(None, None, "elem"), P(None, None, "elem"))
    return jax.shard_map(shards, mesh=mesh, in_specs=in_specs, out_specs=out_specs, check_vma=False)
```

```python
import functools

import jax
import jax.numpy as jnp
import numpy as np
from jax import lax
from jax.experimental import pallas as pl
from jax.experimental.pallas import tpu as pltpu
from jax.sharding import PartitionSpec as P

DA = 4
DT = 0.001
F32 = jnp.float32
BF16 = jnp.bfloat16


def gll_tables():
    points = [
        -1.0,
        -0.8717401485096066,
        -0.5917001814331423,
        -0.2092992179024789,
        0.2092992179024789,
        0.5917001814331423,
        0.8717401485096066,
        1.0,
    ]
    weights = [
        0.03571428571428571,
        0.21070422714350603,
        0.3411226924835044,
        0.4124587946587038,
        0.4124587946587038,
        0.3411226924835044,
        0.21070422714350603,
        0.03571428571428571,
    ]
    barycentric = []
    for left_index in range(8):
        product = 1.0
        for right_index in range(8):
            if right_index != left_index:
                product = product * (points[left_index] - points[right_index])
        barycentric.append(1.0 / product)
    derivative = np.zeros((8, 8))
    for left_index in range(8):
        row_total = 0.0
        for right_index in range(8):
            if left_index != right_index:
                entry = (
                    barycentric[right_index]
                    / barycentric[left_index]
                    / (points[left_index] - points[right_index])
                )
                derivative[left_index, right_index] = entry
                row_total = row_total + entry
        derivative[left_index, left_index] = -row_total
    return derivative, np.asarray(weights)


DM, WEIGHTS = gll_tables()


def line(table, values):
    sums = [values[q] + values[7 - q] for q in range(4)]
    differences = [values[q] - values[7 - q] for q in range(4)]
    out = [None] * 8
    for i in range(4):
        even = odd = None
        for q in range(4):
            on_sum = float(table[i, q] + table[i, 7 - q]) / 2
            on_difference = float(table[i, q] - table[i, 7 - q]) / 2
            even = sums[q] * on_sum if even is None else even + sums[q] * on_sum
            odd = (
                differences[q] * on_difference
                if odd is None
                else odd + differences[q] * on_difference
            )
        out[i] = odd + even
        out[7 - i] = odd - even
    return out


def rows(i, j):
    return pl.ds((8 * i + j) * 8, 8)


def along_k(table_ref, block):
    wide = jnp.concatenate([block[:256], block[256:]], axis=1)
    high = wide.astype(BF16)
    low = (wide - high.astype(F32)).astype(BF16)
    both = jnp.dot(table_ref[...], high, preferred_element_type=F32)
    rest = jnp.dot(table_ref[:256], low, preferred_element_type=F32)
    out = both[:256] + (both[256:] + rest)
    return jnp.concatenate([out[:, :128], out[:, 128:]], axis=0)


def write_table(table, table_ref):
    sub = lax.broadcasted_iota(jnp.int32, (8, 128), 0)
    lane = lax.broadcasted_iota(jnp.int32, (8, 128), 1)
    base = jnp.zeros((8, 128), F32)
    for i in range(8):
        one_row = jnp.zeros((8, 128), F32)
        for q in range(8):
            one_row = jnp.where((lane & 7) == q, float(table[i, q]), one_row)
        base = jnp.where(sub == i, one_row, base)
    high = base.astype(BF16).astype(F32)
    block = lax.shift_right_logical(lane, 3)
    zero = jnp.zeros((8, 128), F32)
    for part, values in enumerate((high, base - high)):
        for a in range(0, 32, 2):
            pair = [jnp.where(block == (a + n) % 16, values, zero) for n in range(2)]
            pair = jnp.concatenate(pair, axis=0)
            wide = [pair, jnp.zeros((16, 128), F32)]
            wide = jnp.concatenate(wide if a < 16 else wide[::-1], axis=1)
            table_ref[pl.ds(256 * part + 8 * a, 16)] = wide.astype(BF16)


def spread(diff, block):
    return (diff[None] * block.reshape(-1, 8, 128)).reshape(block.shape)


def lanes(block, index):
    wide = jnp.broadcast_to(index[None], (block.shape[0] // 8, 8, 128)).reshape(block.shape)
    return jnp.take_along_axis(block, wide, axis=1, mode="promise_in_bounds")


def set_mass(weight_ref, mass_ref):
    sub = lax.broadcasted_iota(jnp.int32, (8, 128), 0)
    along = jnp.zeros((8, 128), F32)
    for k in range(8):
        along = jnp.where(sub == k, float(WEIGHTS[k]), along)
    for i in range(8):
        for j in range(8):
            r = rows(i, j)
            mass_ref[r] = weight_ref[r] * (along * float(WEIGHTS[i] * WEIGHTS[j]))


def forward_k(source, flow_ref, mass_ref, diff, table_ref, turned_ref, work):
    flux = along_k(table_ref, source[...]) * mass_ref[...]
    work[...] = flow_ref[2] * flux + spread(diff, along_k(turned_ref, flux))


def adjoint_k(source, flow_ref, mass_ref, diff, table_ref, turned_ref, work):
    slope = along_k(table_ref, source[...])
    flux = (flow_ref[2] * source[...] + spread(diff, slope)) * mass_ref[...]
    work[...] = along_k(turned_ref, flux)


def forward(source, flow_ref, mass_ref, diff, work, target):
    for j in range(8):
        slopes = line(DM, [source[rows(i, j)] for i in range(8)])
        fluxes = [slopes[i] * mass_ref[rows(i, j)] for i in range(8)]
        back = line(DM.T, fluxes)
        for i in range(8):
            r = rows(i, j)
            target[r] = flow_ref[0, r] * fluxes[i] + diff * back[i]
    for i in range(8):
        slopes = line(DM, [source[rows(i, j)] for j in range(8)])
        fluxes = [slopes[j] * mass_ref[rows(i, j)] for j in range(8)]
        back = line(DM.T, fluxes)
        for j in range(8):
            r = rows(i, j)
            target[r] = -(target[r] + work[r] + (flow_ref[1, r] * fluxes[j] + diff * back[j]))


def adjoint(source, base, flow_ref, mass_ref, diff, work, target):
    for j in range(8):
        values = [source[rows(i, j)] for i in range(8)]
        slopes = line(DM, values)
        fluxes = [
            (flow_ref[0, rows(i, j)] * values[i] + diff * slopes[i]) * mass_ref[rows(i, j)]
            for i in range(8)
        ]
        back = line(DM.T, fluxes)
        for i in range(8):
            target[rows(i, j)] = back[i]
    for i in range(8):
        values = [source[rows(i, j)] for j in range(8)]
        slopes = line(DM, values)
        fluxes = [
            (flow_ref[1, rows(i, j)] * values[j] + diff * slopes[j]) * mass_ref[rows(i, j)]
            for j in range(8)
        ]
        back = line(DM.T, fluxes)
        for j in range(8):
            r = rows(i, j)
            target[r] = base[r] - DT * (target[r] + work[r] + back[j])


def join_heights(ref, index):
    height, _, below, above = index
    lower = ref[pl.ds(0, 64, stride=8)]
    upper = ref[pl.ds(7, 64, stride=8)]
    tall = jnp.broadcast_to(height[None], (8, 8, 128)).reshape(64, 128)
    ref[pl.ds(0, 64, stride=8)] = lower + jnp.where(tall > 0, lanes(upper, below), 0.0)
    ref[pl.ds(7, 64, stride=8)] = upper + jnp.where(tall < 127, lanes(lower, above), 0.0)


def send_faces(c, ref, index, ends, out):
    inverse = index[1]
    for way in range(2):
        i_face = ref[pl.ds(pl.multiple_of(ends[0][way] * 64, 64), 64)]
        out[way][c] = lanes(i_face, inverse)
        for i in range(8):
            j_face = ref[pl.ds(pl.multiple_of(ends[1][way] * 8 + i * 64, 8), 8)]
            out[2 + way][c, pl.ds(i * 8, 8)] = lanes(j_face, inverse)


def add_faces(c, ref, index, ends, got):
    height = index[0]
    for way in range(2):
        r = pl.ds(pl.multiple_of(ends[0][way] * 64, 64), 64)
        part = lanes(got[way][c], height)
        ref[r] = ref[r] + (part * ends[2][0] if way else part)
    for way in range(2):
        for i in range(8):
            r = pl.ds(pl.multiple_of(ends[1][way] * 8 + i * 64, 8), 8)
            part = lanes(got[2 + way][c, pl.ds(i * 8, 8)], height)
            ref[r] = ref[r] + (part * ends[2][1] if way else part)


def ends_of(columns):
    column = lax.rem(lax.axis_index("elem") + columns // 2, columns * DA)
    row, place = lax.div(column, columns), lax.rem(column, columns)
    row_odd, place_odd = lax.rem(row, 2), lax.rem(place, 2)
    row_inside = jnp.where((row > 0) & (row < DA - 1), 1.0, 0.0)
    place_inside = jnp.where((place > 0) & (place < columns - 1), 1.0, 0.0)
    return (
        (7 - 7 * row_odd, 7 * row_odd),
        (7 - 7 * place_odd, 7 * place_odd),
        (row_inside, place_inside),
    )


def index_of(index_ref):
    return tuple(index_ref[n] for n in range(4))


def index_kernel(
    columns,
    moment_far,
    state_far,
    flow_far,
    weight_far,
    diff_far,
    numbers_far,
    moment_ref,
    state_ref,
    flow_ref,
    diff_ref,
    table_ref,
    turned_ref,
    index_ref,
    mass_ref,
    joined_ref,
    ie_ref,
    io_ref,
    je_ref,
    jo_ref,
    weight_ref,
    numbers_ref,
    scalar_ref,
    arrived,
):
    far = (numbers_far, weight_far, state_far, diff_far, moment_far, flow_far)
    near = (numbers_ref, weight_ref, state_ref, scalar_ref, moment_ref, flow_ref)
    copies = [pltpu.make_async_copy(a, b, arrived.at[n]) for n, (a, b) in enumerate(zip(far, near))]
    for copy in copies:
        copy.start()
    write_table(DM, table_ref)
    write_table(DM.T, turned_ref)
    ends = ends_of(columns)
    copies[0].wait()
    height = jnp.broadcast_to(numbers_ref[...] & 127, (8, 128))
    square = jnp.broadcast_to(height[:1].astype(F32), (128, 128)).T
    lane = lax.broadcasted_iota(jnp.int32, (128, 128), 1).astype(F32)
    row = lax.broadcasted_iota(jnp.int32, (128, 128), 0).astype(F32)
    inverse = jnp.sum(jnp.where(square == lane, row, 0.0), axis=0, keepdims=True)
    inverse = jnp.broadcast_to(inverse, (8, 128)).astype(jnp.int32)
    index = (
        height,
        inverse,
        lanes(inverse, (height - 1) & 127),
        lanes(inverse, (height + 1) & 127),
    )
    for n in range(4):
        index_ref[n] = index[n]
    copies[1].wait()
    set_mass(weight_ref, mass_ref)
    joined_ref[3] = mass_ref[...]
    copies[2].wait()
    out = (ie_ref, io_ref, je_ref, jo_ref)
    for c in range(3):
        joined_ref[c] = state_ref[c]
    for c in range(4):
        join_heights(joined_ref.at[c], index)
        send_faces(c, joined_ref.at[c], index, ends, out)
    copies[3].wait()
    for f in range(3):
        diff_ref[f] = jnp.full((8, 128), scalar_ref[f], F32)
    copies[4].wait()
    copies[5].wait()


def moment_kernel(
    columns,
    moment_ref,
    flow_ref,
    diff_ref,
    table_ref,
    turned_ref,
    index_ref,
    mass_ref,
    joined_ref,
    ie_ref,
    io_ref,
    je_ref,
    jo_ref,
    work_ref,
):
    ends = ends_of(columns)
    index = index_of(index_ref)
    out = (ie_ref, io_ref, je_ref, jo_ref)

    for f in range(3):
        at = (flow_ref, mass_ref, diff_ref[f])
        forward_k(moment_ref.at[f], *at, table_ref, turned_ref, work_ref.at[f])
    for f in range(3):
        at = (flow_ref, mass_ref, diff_ref[f])
        forward(moment_ref.at[f], *at, work_ref.at[f], joined_ref.at[f])
        join_heights(joined_ref.at[f], index)
        send_faces(f, joined_ref.at[f], index, ends, out)


def edge_kernel(columns, ie_ref, io_ref, je_ref, jo_ref, out_e, out_o):
    ends = ends_of(columns)
    for way, (face, out) in enumerate(((je_ref, out_e), (jo_ref, out_o))):
        out[...] = face[...]
        r = pl.ds(pl.multiple_of(ends[1][way] * 8, 8), 8)
        for other, got in enumerate((ie_ref, io_ref)):
            w = pl.ds(pl.multiple_of(ends[0][other] * 8, 8), 8)
            part = got[:, r]
            out[:, w] = out[:, w] + (part * ends[2][0] if other else part)


def state_kernel(
    columns,
    first,
    state_ref,
    flow_ref,
    diff_ref,
    table_ref,
    turned_ref,
    index_ref,
    mass_ref,
    joined_ref,
    *refs,
):
    ends = ends_of(columns)
    index = index_of(index_ref)
    if first:
        got, (inverse_ref, state_out, joined_out), refs = refs[:4], refs[4:7], refs[7:]
        out, (work_ref, hold_ref) = refs[:4], refs[4:]
        held = hold_ref.at[0]
        held[...] = joined_ref[3]
        add_faces(3, held, index, ends, got)
        inverse_ref[...] = 1.0 / held[...]
    else:
        inverse_ref, *got = refs[:5]
        state_out, work_ref, hold_ref = refs[5:]

    for f in range(3):
        held = hold_ref.at[f]
        held[...] = joined_ref[f]
        add_faces(f, held, index, ends, got)
        held[...] = held[...] * inverse_ref[...]
        at = (flow_ref, mass_ref, diff_ref[f])
        adjoint_k(held, *at, table_ref, turned_ref, work_ref.at[f])
    for f in range(3):
        at = (flow_ref, mass_ref, diff_ref[f])
        adjoint(hold_ref.at[f], state_ref.at[f], *at, work_ref.at[f], state_out.at[f])
        if first:
            joined_out[f] = state_out[f]
            join_heights(joined_out.at[f], index)
            send_faces(f, joined_out.at[f], index, ends, out)


def moment_step(f, ends, index, moment_ref, joined_ref, inverse_ref, got, hold_ref, moment_out):
    held = hold_ref.at[f]
    held[...] = joined_ref[f]
    add_faces(f, held, index, ends, got)
    moment_out[f] = moment_ref[f] + DT * (held[...] * inverse_ref[...])


def middle_kernel(
    columns,
    moment_ref,
    flow_ref,
    diff_ref,
    table_ref,
    turned_ref,
    index_ref,
    mass_ref,
    inverse_ref,
    joined_ref,
    gie_ref,
    gio_ref,
    gje_ref,
    gjo_ref,
    moment_out,
    joined_out,
    ie_ref,
    io_ref,
    je_ref,
    jo_ref,
    work_ref,
    hold_ref,
):
    ends = ends_of(columns)
    index = index_of(index_ref)
    out = (ie_ref, io_ref, je_ref, jo_ref)
    got = (gie_ref, gio_ref, gje_ref, gjo_ref)

    for f in range(3):
        moment_step(f, ends, index, moment_ref, joined_ref, inverse_ref, got, hold_ref, moment_out)
        at = (flow_ref, mass_ref, diff_ref[f])
        forward_k(moment_out.at[f], *at, table_ref, turned_ref, work_ref.at[f])
    for f in range(3):
        at = (flow_ref, mass_ref, diff_ref[f])
        forward(moment_out.at[f], *at, work_ref.at[f], joined_out.at[f])
        join_heights(joined_out.at[f], index)
        send_faces(f, joined_out.at[f], index, ends, out)


def last_kernel(
    columns,
    moment_ref,
    index_ref,
    inverse_ref,
    joined_ref,
    gie_ref,
    gio_ref,
    gje_ref,
    gjo_ref,
    moment_out,
    hold_ref,
):
    ends = ends_of(columns)
    index = index_of(index_ref)
    got = (gie_ref, gio_ref, gje_ref, gjo_ref)

    for f in range(3):
        moment_step(f, ends, index, moment_ref, joined_ref, inverse_ref, got, hold_ref, moment_out)


VMEM = pl.BlockSpec(memory_space=pltpu.VMEM)
FAR = pl.BlockSpec(memory_space=pltpu.HBM)


def call(kernel, specs, shapes, scratch, flops, *operands):
    moved = sum(o.size * 4 for o in operands) + sum(int(np.prod(s)) * 4 for s, _ in shapes)
    return pl.pallas_call(
        kernel,
        out_shape=[jax.ShapeDtypeStruct(s, t) for s, t in shapes],
        in_specs=specs,
        out_specs=[VMEM] * len(shapes),
        scratch_shapes=scratch,
        compiler_params=pltpu.CompilerParams(vmem_limit_bytes=32 * 1024 * 1024),
        cost_estimate=pl.CostEstimate(flops=flops, bytes_accessed=moved, transcendentals=0),
    )(*operands)


def pairings(devices):
    columns = devices // DA
    device = lambda row, place: (row * columns + place - columns // 2) % devices

    def both(pairs):
        paired = {device for pair in pairs for device in pair}
        alone = [(device, device) for device in range(devices) if device not in paired]
        return pairs + [(b, a) for a, b in pairs] + alone

    along_i = [
        both([(device(r, s), device(r + 1, s)) for r in range(way, DA - 1, 2) for s in range(columns)])
        for way in range(2)
    ]
    along_j = [
        both([(device(r, s), device(r, s + 1)) for r in range(DA) for s in range(way, columns - 1, 2)])
        for way in range(2)
    ]
    return along_i, along_j


def shards(moment_fields, adjoint_fields, velocity, mass_weights, diffusivity, numbering):
    devices = lax.axis_size("elem")
    columns = devices // DA
    along_i, along_j = pairings(devices)
    whole, block = ((3, 512, 128), F32), ((512, 128), F32)
    work = pltpu.VMEM((3, 512, 128), F32)

    def exchange(blocks, pairs):
        return [lax.ppermute(b, "elem", p) for b, p in zip(blocks, pairs)]

    def meet(count, faces):
        got_i = exchange(faces[:2], along_i)
        faces_j = call(
            functools.partial(edge_kernel, columns),
            [VMEM] * 4,
            [((count, 64, 128), F32)] * 2,
            [],
            count * 64 * 128,
            *got_i,
            *faces[2:],
        )
        return got_i + exchange(faces_j, along_j)

    def far(array):
        return pltpu.with_memory_space_constraint(array, pltpu.HBM)

    def faces_shape(count):
        return [((count, 64, 128), F32)] * 4

    moment, state, flow, diff, table, turned, index, mass, joined_state, *faces_state = call(
        functools.partial(index_kernel, columns),
        [FAR] * 6,
        [whole] * 3
        + [((3, 8, 128), F32)]
        + [((512, 256), BF16)] * 2
        + [((4, 8, 128), jnp.int32), block, ((4, 512, 128), F32)]
        + faces_shape(4),
        [
            pltpu.VMEM((512, 128), F32),
            pltpu.VMEM((1, 128), jnp.int32),
            pltpu.SMEM((3,), F32),
            pltpu.SemaphoreType.DMA((6,)),
        ],
        1_000_000,
        *map(far, (moment_fields, adjoint_fields, velocity, mass_weights)),
        *map(far, (diffusivity, numbering.reshape(1, 128))),
    )
    tables = (flow, diff, table, turned, index, mass)
    got_state = meet(4, faces_state)
    joined_moment, *faces_moment = call(
        functools.partial(moment_kernel, columns),
        [VMEM] * 7,
        [whole] + faces_shape(3),
        [work],
        20_000_000,
        moment,
        *tables,
    )
    got_moment = meet(3, faces_moment)
    inverse, state, joined_state, *faces_state = call(
        functools.partial(state_kernel, columns, True),
        [VMEM] * 12,
        [block, whole, whole] + faces_shape(3),
        [work] * 2,
        20_000_000,
        state,
        *tables,
        joined_state,
        *got_state,
    )
    got_state = meet(3, faces_state)
    moment, joined_moment, *faces_moment = call(
        functools.partial(middle_kernel, columns),
        [VMEM] * 13,
        [whole, whole] + faces_shape(3),
        [work] * 2,
        20_000_000,
        moment,
        *tables,
        inverse,
        joined_moment,
        *got_moment,
    )
    got_moment = meet(3, faces_moment)
    (state,) = call(
        functools.partial(state_kernel, columns, False),
        [VMEM] * 13,
        [whole],
        [work] * 2,
        20_000_000,
        state,
        *tables,
        joined_state,
        inverse,
        *got_state,
    )
    (moment,) = call(
        functools.partial(last_kernel, columns),
        [VMEM] * 8,
        [whole],
        [work],
        1_000_000,
        moment,
        index,
        inverse,
        joined_moment,
        *got_moment,
    )
    return moment, state


def solution(mesh):
    in_specs = (
        P(None, None, "elem"),
        P(None, None, "elem"),
        P(None, None, "elem"),
        P(None, "elem"),
        P(),
        P("elem"),
    )
    out_specs = (P(None, None, "elem"), P(None, None, "elem"))
    return jax.shard_map(shards, mesh=mesh, in_specs=in_specs, out_specs=out_specs, check_vma=False)
```

```python
import functools

import jax
import jax.numpy as jnp
import numpy as np
from jax import lax
from jax.experimental import pallas as pl
from jax.experimental.pallas import tpu as pltpu
from jax.sharding import PartitionSpec as P

DA = 4
DT = 0.001
F32 = jnp.float32
BF16 = jnp.bfloat16


def gll_tables():
    points = [
        -1.0,
        -0.8717401485096066,
        -0.5917001814331423,
        -0.2092992179024789,
        0.2092992179024789,
        0.5917001814331423,
        0.8717401485096066,
        1.0,
    ]
    weights = [
        0.03571428571428571,
        0.21070422714350603,
        0.3411226924835044,
        0.4124587946587038,
        0.4124587946587038,
        0.3411226924835044,
        0.21070422714350603,
        0.03571428571428571,
    ]
    barycentric = []
    for left_index in range(8):
        product = 1.0
        for right_index in range(8):
            if right_index != left_index:
                product = product * (points[left_index] - points[right_index])
        barycentric.append(1.0 / product)
    derivative = np.zeros((8, 8))
    for left_index in range(8):
        row_total = 0.0
        for right_index in range(8):
            if left_index != right_index:
                entry = (
                    barycentric[right_index]
                    / barycentric[left_index]
                    / (points[left_index] - points[right_index])
                )
                derivative[left_index, right_index] = entry
                row_total = row_total + entry
        derivative[left_index, left_index] = -row_total
    return derivative, np.asarray(weights)


DM, WEIGHTS = gll_tables()


def line(table, values):
    sums = [values[q] + values[7 - q] for q in range(4)]
    differences = [values[q] - values[7 - q] for q in range(4)]
    out = [None] * 8
    for i in range(4):
        even = odd = None
        for q in range(4):
            on_sum = float(table[i, q] + table[i, 7 - q]) / 2
            on_difference = float(table[i, q] - table[i, 7 - q]) / 2
            even = sums[q] * on_sum if even is None else even + sums[q] * on_sum
            odd = (
                differences[q] * on_difference
                if odd is None
                else odd + differences[q] * on_difference
            )
        out[i] = odd + even
        out[7 - i] = odd - even
    return out


def rows(i, j):
    return pl.ds((8 * i + j) * 8, 8)


def along_k(table_ref, block):
    wide = jnp.concatenate([block[:256], block[256:]], axis=1)
    high = wide.astype(BF16)
    low = (wide - high.astype(F32)).astype(BF16)
    both = jnp.dot(table_ref[...], high, preferred_element_type=F32)
    rest = jnp.dot(table_ref[:256], low, preferred_element_type=F32)
    out = both[:256] + (both[256:] + rest)
    return jnp.concatenate([out[:, :128], out[:, 128:]], axis=0)


def write_table(table, table_ref):
    sub = lax.broadcasted_iota(jnp.int32, (8, 128), 0)
    lane = lax.broadcasted_iota(jnp.int32, (8, 128), 1)
    base = jnp.zeros((8, 128), F32)
    for i in range(8):
        one_row = jnp.zeros((8, 128), F32)
        for q in range(8):
            one_row = jnp.where((lane & 7) == q, float(table[i, q]), one_row)
        base = jnp.where(sub == i, one_row, base)
    high = base.astype(BF16).astype(F32)
    block = lax.shift_right_logical(lane, 3)
    zero = jnp.zeros((8, 128), F32)
    for part, values in enumerate((high, base - high)):
        for a in range(0, 32, 2):
            pair = [jnp.where(block == (a + n) % 16, values, zero) for n in range(2)]
            pair = jnp.concatenate(pair, axis=0)
            wide = [pair, jnp.zeros((16, 128), F32)]
            wide = jnp.concatenate(wide if a < 16 else wide[::-1], axis=1)
            table_ref[pl.ds(256 * part + 8 * a, 16)] = wide.astype(BF16)


def spread(diff, block):
    return (diff[None] * block.reshape(-1, 8, 128)).reshape(block.shape)


def lanes(block, index):
    wide = jnp.broadcast_to(index[None], (block.shape[0] // 8, 8, 128)).reshape(block.shape)
    return jnp.take_along_axis(block, wide, axis=1, mode="promise_in_bounds")


def set_mass(weight_ref, mass_ref):
    sub = lax.broadcasted_iota(jnp.int32, (8, 128), 0)
    along = jnp.zeros((8, 128), F32)
    for k in range(8):
        along = jnp.where(sub == k, float(WEIGHTS[k]), along)
    for i in range(8):
        for j in range(8):
            r = rows(i, j)
            mass_ref[r] = weight_ref[r] * (along * float(WEIGHTS[i] * WEIGHTS[j]))


def forward_k(source, flow_ref, mass_ref, diff, table_ref, turned_ref, work):
    flux = along_k(table_ref, source[...]) * mass_ref[...]
    work[...] = flow_ref[2] * flux + spread(diff, along_k(turned_ref, flux))


def adjoint_k(source, flow_ref, mass_ref, diff, table_ref, turned_ref, work):
    slope = along_k(table_ref, source[...])
    flux = (flow_ref[2] * source[...] + spread(diff, slope)) * mass_ref[...]
    work[...] = along_k(turned_ref, flux)


def forward(source, flow_ref, mass_ref, diff, work, target):
    for j in range(8):
        slopes = line(DM, [source[rows(i, j)] for i in range(8)])
        fluxes = [slopes[i] * mass_ref[rows(i, j)] for i in range(8)]
        back = line(DM.T, fluxes)
        for i in range(8):
            r = rows(i, j)
            target[r] = flow_ref[0, r] * fluxes[i] + diff * back[i]
    for i in range(8):
        slopes = line(DM, [source[rows(i, j)] for j in range(8)])
        fluxes = [slopes[j] * mass_ref[rows(i, j)] for j in range(8)]
        back = line(DM.T, fluxes)
        for j in range(8):
            r = rows(i, j)
            target[r] = -(target[r] + work[r] + (flow_ref[1, r] * fluxes[j] + diff * back[j]))


def adjoint(source, base, flow_ref, mass_ref, diff, work, target):
    for j in range(8):
        values = [source[rows(i, j)] for i in range(8)]
        slopes = line(DM, values)
        fluxes = [
            (flow_ref[0, rows(i, j)] * values[i] + diff * slopes[i]) * mass_ref[rows(i, j)]
            for i in range(8)
        ]
        back = line(DM.T, fluxes)
        for i in range(8):
            target[rows(i, j)] = back[i]
    for i in range(8):
        values = [source[rows(i, j)] for j in range(8)]
        slopes = line(DM, values)
        fluxes = [
            (flow_ref[1, rows(i, j)] * values[j] + diff * slopes[j]) * mass_ref[rows(i, j)]
            for j in range(8)
        ]
        back = line(DM.T, fluxes)
        for j in range(8):
            r = rows(i, j)
            target[r] = base[r] - DT * (target[r] + work[r] + back[j])


def join_heights(ref, index):
    height, _, below, above = index
    lower = ref[pl.ds(0, 64, stride=8)]
    upper = ref[pl.ds(7, 64, stride=8)]
    tall = jnp.broadcast_to(height[None], (8, 8, 128)).reshape(64, 128)
    ref[pl.ds(0, 64, stride=8)] = lower + jnp.where(tall > 0, lanes(upper, below), 0.0)
    ref[pl.ds(7, 64, stride=8)] = upper + jnp.where(tall < 127, lanes(lower, above), 0.0)


def send_faces(c, ref, index, ends, out):
    inverse = index[1]
    for way in range(2):
        i_face = ref[pl.ds(pl.multiple_of(ends[0][way] * 64, 64), 64)]
        out[way][c] = lanes(i_face, inverse)
        for i in range(8):
            j_face = ref[pl.ds(pl.multiple_of(ends[1][way] * 8 + i * 64, 8), 8)]
            out[2 + way][c, pl.ds(i * 8, 8)] = lanes(j_face, inverse)


def add_faces(c, ref, index, ends, got):
    height = index[0]
    for way in range(2):
        r = pl.ds(pl.multiple_of(ends[0][way] * 64, 64), 64)
        part = lanes(got[way][c], height)
        ref[r] = ref[r] + (part * ends[2][0] if way else part)
    for way in range(2):
        for i in range(8):
            r = pl.ds(pl.multiple_of(ends[1][way] * 8 + i * 64, 8), 8)
            part = lanes(got[2 + way][c, pl.ds(i * 8, 8)], height)
            ref[r] = ref[r] + (part * ends[2][1] if way else part)


def ends_of(columns):
    column = lax.rem(lax.axis_index("elem") + columns // 2, columns * DA)
    row, place = lax.div(column, columns), lax.rem(column, columns)
    row_odd, place_odd = lax.rem(row, 2), lax.rem(place, 2)
    row_inside = jnp.where((row > 0) & (row < DA - 1), 1.0, 0.0)
    place_inside = jnp.where((place > 0) & (place < columns - 1), 1.0, 0.0)
    return (
        (7 - 7 * row_odd, 7 * row_odd),
        (7 - 7 * place_odd, 7 * place_odd),
        (row_inside, place_inside),
    )


def index_of(index_ref):
    return tuple(index_ref[n] for n in range(4))


def index_kernel(
    columns,
    moment_far,
    state_far,
    flow_far,
    weight_far,
    diff_far,
    numbers_far,
    moment_ref,
    state_ref,
    flow_ref,
    diff_ref,
    table_ref,
    turned_ref,
    index_ref,
    mass_ref,
    joined_ref,
    ie_ref,
    io_ref,
    je_ref,
    jo_ref,
    weight_ref,
    numbers_ref,
    scalar_ref,
    arrived,
):
    far = (numbers_far, weight_far, state_far, diff_far, moment_far, flow_far)
    near = (numbers_ref, weight_ref, state_ref, scalar_ref, moment_ref, flow_ref)
    copies = [pltpu.make_async_copy(a, b, arrived.at[n]) for n, (a, b) in enumerate(zip(far, near))]
    for copy in copies:
        copy.start()
    write_table(DM, table_ref)
    write_table(DM.T, turned_ref)
    ends = ends_of(columns)
    copies[0].wait()
    height = jnp.broadcast_to(numbers_ref[...] & 127, (8, 128))
    square = jnp.broadcast_to(height[:1].astype(F32), (128, 128)).T
    lane = lax.broadcasted_iota(jnp.int32, (128, 128), 1).astype(F32)
    row = lax.broadcasted_iota(jnp.int32, (128, 128), 0).astype(F32)
    inverse = jnp.sum(jnp.where(square == lane, row, 0.0), axis=0, keepdims=True)
    inverse = jnp.broadcast_to(inverse, (8, 128)).astype(jnp.int32)
    index = (
        height,
        inverse,
        lanes(inverse, (height - 1) & 127),
        lanes(inverse, (height + 1) & 127),
    )
    for n in range(4):
        index_ref[n] = index[n]
    copies[1].wait()
    set_mass(weight_ref, mass_ref)
    joined_ref[3] = mass_ref[...]
    copies[2].wait()
    out = (ie_ref, io_ref, je_ref, jo_ref)
    for c in range(3):
        joined_ref[c] = state_ref[c]
    for c in range(4):
        join_heights(joined_ref.at[c], index)
        send_faces(c, joined_ref.at[c], index, ends, out)
    copies[3].wait()
    for f in range(3):
        diff_ref[f] = jnp.full((8, 128), scalar_ref[f], F32)
    copies[4].wait()
    copies[5].wait()


def moment_kernel(
    columns,
    moment_ref,
    flow_ref,
    diff_ref,
    table_ref,
    turned_ref,
    index_ref,
    mass_ref,
    joined_ref,
    ie_ref,
    io_ref,
    je_ref,
    jo_ref,
    work_ref,
):
    ends = ends_of(columns)
    index = index_of(index_ref)
    out = (ie_ref, io_ref, je_ref, jo_ref)

    for f in range(3):
        at = (flow_ref, mass_ref, diff_ref[f])
        forward_k(moment_ref.at[f], *at, table_ref, turned_ref, work_ref.at[f])
    for f in range(3):
        at = (flow_ref, mass_ref, diff_ref[f])
        forward(moment_ref.at[f], *at, work_ref.at[f], joined_ref.at[f])
        join_heights(joined_ref.at[f], index)
        send_faces(f, joined_ref.at[f], index, ends, out)


def edge_kernel(columns, ie_ref, io_ref, je_ref, jo_ref, out_e, out_o):
    ends = ends_of(columns)
    for way, (face, out) in enumerate(((je_ref, out_e), (jo_ref, out_o))):
        out[...] = face[...]
        r = pl.ds(pl.multiple_of(ends[1][way] * 8, 8), 8)
        for other, got in enumerate((ie_ref, io_ref)):
            w = pl.ds(pl.multiple_of(ends[0][other] * 8, 8), 8)
            part = got[:, r]
            out[:, w] = out[:, w] + (part * ends[2][0] if other else part)


def state_kernel(
    columns,
    first,
    state_ref,
    flow_ref,
    diff_ref,
    table_ref,
    turned_ref,
    index_ref,
    mass_ref,
    joined_ref,
    *refs,
):
    ends = ends_of(columns)
    index = index_of(index_ref)
    if first:
        got, (inverse_ref, state_out, joined_out), refs = refs[:4], refs[4:7], refs[7:]
        out, (work_ref, hold_ref) = refs[:4], refs[4:]
        held = hold_ref.at[0]
        held[...] = joined_ref[3]
        add_faces(3, held, index, ends, got)
        inverse_ref[...] = 1.0 / held[...]
    else:
        inverse_ref, *got = refs[:5]
        state_out, work_ref, hold_ref = refs[5:]

    for f in range(3):
        held = hold_ref.at[f]
        held[...] = joined_ref[f]
        add_faces(f, held, index, ends, got)
        held[...] = held[...] * inverse_ref[...]
        at = (flow_ref, mass_ref, diff_ref[f])
        adjoint_k(held, *at, table_ref, turned_ref, work_ref.at[f])
    for f in range(3):
        at = (flow_ref, mass_ref, diff_ref[f])
        adjoint(hold_ref.at[f], state_ref.at[f], *at, work_ref.at[f], state_out.at[f])
        if first:
            joined_out[f] = state_out[f]
            join_heights(joined_out.at[f], index)
            send_faces(f, joined_out.at[f], index, ends, out)


def moment_step(f, ends, index, moment_ref, joined_ref, inverse_ref, got, hold_ref, moment_out):
    held = hold_ref.at[f]
    held[...] = joined_ref[f]
    add_faces(f, held, index, ends, got)
    moment_out[f] = moment_ref[f] + DT * (held[...] * inverse_ref[...])


def middle_kernel(
    columns,
    moment_ref,
    flow_ref,
    diff_ref,
    table_ref,
    turned_ref,
    index_ref,
    mass_ref,
    inverse_ref,
    joined_ref,
    gie_ref,
    gio_ref,
    gje_ref,
    gjo_ref,
    moment_out,
    joined_out,
    ie_ref,
    io_ref,
    je_ref,
    jo_ref,
    work_ref,
    hold_ref,
):
    ends = ends_of(columns)
    index = index_of(index_ref)
    out = (ie_ref, io_ref, je_ref, jo_ref)
    got = (gie_ref, gio_ref, gje_ref, gjo_ref)

    for f in range(3):
        moment_step(f, ends, index, moment_ref, joined_ref, inverse_ref, got, hold_ref, moment_out)
        at = (flow_ref, mass_ref, diff_ref[f])
        forward_k(moment_out.at[f], *at, table_ref, turned_ref, work_ref.at[f])
    for f in range(3):
        at = (flow_ref, mass_ref, diff_ref[f])
        forward(moment_out.at[f], *at, work_ref.at[f], joined_out.at[f])
        join_heights(joined_out.at[f], index)
        send_faces(f, joined_out.at[f], index, ends, out)


def last_kernel(
    columns,
    moment_ref,
    index_ref,
    inverse_ref,
    joined_ref,
    gie_ref,
    gio_ref,
    gje_ref,
    gjo_ref,
    moment_out,
    hold_ref,
):
    ends = ends_of(columns)
    index = index_of(index_ref)
    got = (gie_ref, gio_ref, gje_ref, gjo_ref)

    for f in range(3):
        moment_step(f, ends, index, moment_ref, joined_ref, inverse_ref, got, hold_ref, moment_out)


VMEM = pl.BlockSpec(memory_space=pltpu.VMEM)
FAR = pl.BlockSpec(memory_space=pltpu.HBM)


def call(kernel, specs, shapes, scratch, flops, *operands):
    moved = sum(o.size * 4 for o in operands) + sum(int(np.prod(s)) * 4 for s, _ in shapes)
    return pl.pallas_call(
        kernel,
        out_shape=[jax.ShapeDtypeStruct(s, t) for s, t in shapes],
        in_specs=specs,
        out_specs=[VMEM] * len(shapes),
        scratch_shapes=scratch,
        compiler_params=pltpu.CompilerParams(vmem_limit_bytes=32 * 1024 * 1024),
        cost_estimate=pl.CostEstimate(flops=flops, bytes_accessed=moved, transcendentals=0),
    )(*operands)


def pairings(devices):
    columns = devices // DA
    device = lambda row, place: (row % DA * columns + place - columns // 2) % devices

    def both(pairs):
        return pairs + [(b, a) for a, b in pairs]

    places, halves = range(columns), range(0, columns, 2)
    along_i = [
        [(device(r, s), device(r + 1, s)) for r in range(0, DA, 2) for s in places],
        [(device(r, s), device(r + 1, s)) for r in range(1, DA - 1, 2) for s in places]
        + [(device(r, s), device(r, s + 1)) for r in (0, DA - 1) for s in halves],
    ]
    along_j = [
        [(device(r, s), device(r, s + 1)) for r in range(DA) for s in halves],
        [(device(r, s - 1), device(r, s)) for r in range(DA) for s in halves if s]
        + [(device(r, columns - 1), device(r + 1, 0)) for r in range(DA)],
    ]
    return [both(p) for p in along_i], [both(p) for p in along_j]


def shards(moment_fields, adjoint_fields, velocity, mass_weights, diffusivity, numbering):
    devices = lax.axis_size("elem")
    columns = devices // DA
    along_i, along_j = pairings(devices)
    whole, block = ((3, 512, 128), F32), ((512, 128), F32)
    work = pltpu.VMEM((3, 512, 128), F32)

    def exchange(blocks, pairs):
        return [lax.ppermute(b, "elem", p) for b, p in zip(blocks, pairs)]

    def meet(count, faces):
        got_i = exchange(faces[:2], along_i)
        faces_j = call(
            functools.partial(edge_kernel, columns),
            [VMEM] * 4,
            [((count, 64, 128), F32)] * 2,
            [],
            count * 64 * 128,
            *got_i,
            *faces[2:],
        )
        return got_i + exchange(faces_j, along_j)

    def far(array):
        return pltpu.with_memory_space_constraint(array, pltpu.HBM)

    def faces_shape(count):
        return [((count, 64, 128), F32)] * 4

    moment, state, flow, diff, table, turned, index, mass, joined_state, *faces_state = call(
        functools.partial(index_kernel, columns),
        [FAR] * 6,
        [whole] * 3
        + [((3, 8, 128), F32)]
        + [((512, 256), BF16)] * 2
        + [((4, 8, 128), jnp.int32), block, ((4, 512, 128), F32)]
        + faces_shape(4),
        [
            pltpu.VMEM((512, 128), F32),
            pltpu.VMEM((1, 128), jnp.int32),
            pltpu.SMEM((3,), F32),
            pltpu.SemaphoreType.DMA((6,)),
        ],
        1_000_000,
        *map(far, (moment_fields, adjoint_fields, velocity, mass_weights)),
        *map(far, (diffusivity, numbering.reshape(1, 128))),
    )
    tables = (flow, diff, table, turned, index, mass)
    got_state = meet(4, faces_state)
    joined_moment, *faces_moment = call(
        functools.partial(moment_kernel, columns),
        [VMEM] * 7,
        [whole] + faces_shape(3),
        [work],
        20_000_000,
        moment,
        *tables,
    )
    got_moment = meet(3, faces_moment)
    inverse, state, joined_state, *faces_state = call(
        functools.partial(state_kernel, columns, True),
        [VMEM] * 12,
        [block, whole, whole] + faces_shape(3),
        [work] * 2,
        20_000_000,
        state,
        *tables,
        joined_state,
        *got_state,
    )
    got_state = meet(3, faces_state)
    moment, joined_moment, *faces_moment = call(
        functools.partial(middle_kernel, columns),
        [VMEM] * 13,
        [whole, whole] + faces_shape(3),
        [work] * 2,
        20_000_000,
        moment,
        *tables,
        inverse,
        joined_moment,
        *got_moment,
    )
    got_moment = meet(3, faces_moment)
    (state,) = call(
        functools.partial(state_kernel, columns, False),
        [VMEM] * 13,
        [whole],
        [work] * 2,
        20_000_000,
        state,
        *tables,
        joined_state,
        inverse,
        *got_state,
    )
    (moment,) = call(
        functools.partial(last_kernel, columns),
        [VMEM] * 8,
        [whole],
        [work],
        1_000_000,
        moment,
        index,
        inverse,
        joined_moment,
        *got_moment,
    )
    return moment, state


def solution(mesh):
    in_specs = (
        P(None, None, "elem"),
        P(None, None, "elem"),
        P(None, None, "elem"),
        P(None, "elem"),
        P(),
        P("elem"),
    )
    out_specs = (P(None, None, "elem"), P(None, None, "elem"))
    return jax.shard_map(shards, mesh=mesh, in_specs=in_specs, out_specs=out_specs, check_vma=False)
```

```python
import functools

import jax
import jax.numpy as jnp
import numpy as np
from jax import lax
from jax.experimental import pallas as pl
from jax.experimental.pallas import tpu as pltpu
from jax.sharding import PartitionSpec as P

DA = 4
DT = 0.001
F32 = jnp.float32
BF16 = jnp.bfloat16


def gll_tables():
    points = [
        -1.0,
        -0.8717401485096066,
        -0.5917001814331423,
        -0.2092992179024789,
        0.2092992179024789,
        0.5917001814331423,
        0.8717401485096066,
        1.0,
    ]
    weights = [
        0.03571428571428571,
        0.21070422714350603,
        0.3411226924835044,
        0.4124587946587038,
        0.4124587946587038,
        0.3411226924835044,
        0.21070422714350603,
        0.03571428571428571,
    ]
    barycentric = []
    for left_index in range(8):
        product = 1.0
        for right_index in range(8):
            if right_index != left_index:
                product = product * (points[left_index] - points[right_index])
        barycentric.append(1.0 / product)
    derivative = np.zeros((8, 8))
    for left_index in range(8):
        row_total = 0.0
        for right_index in range(8):
            if left_index != right_index:
                entry = (
                    barycentric[right_index]
                    / barycentric[left_index]
                    / (points[left_index] - points[right_index])
                )
                derivative[left_index, right_index] = entry
                row_total = row_total + entry
        derivative[left_index, left_index] = -row_total
    return derivative, np.asarray(weights)


DM, WEIGHTS = gll_tables()


def line(table, values):
    sums = [values[q] + values[7 - q] for q in range(4)]
    differences = [values[q] - values[7 - q] for q in range(4)]
    out = [None] * 8
    for i in range(4):
        even = odd = None
        for q in range(4):
            on_sum = float(table[i, q] + table[i, 7 - q]) / 2
            on_difference = float(table[i, q] - table[i, 7 - q]) / 2
            even = sums[q] * on_sum if even is None else even + sums[q] * on_sum
            odd = (
                differences[q] * on_difference
                if odd is None
                else odd + differences[q] * on_difference
            )
        out[i] = odd + even
        out[7 - i] = odd - even
    return out


def rows(i, j):
    return pl.ds((8 * i + j) * 8, 8)


def along_k(table_ref, block):
    wide = jnp.concatenate([block[:256], block[256:]], axis=1)
    high = wide.astype(BF16)
    low = (wide - high.astype(F32)).astype(BF16)
    parts = jnp.concatenate([high, high, low], axis=0)
    out = jnp.dot(table_ref[...], parts, preferred_element_type=F32)
    return jnp.concatenate([out[:, :128], out[:, 128:]], axis=0)


def write_table(table, table_ref):
    sub = lax.broadcasted_iota(jnp.int32, (8, 128), 0)
    lane = lax.broadcasted_iota(jnp.int32, (8, 128), 1)
    base = jnp.zeros((8, 128), F32)
    for i in range(8):
        one_row = jnp.zeros((8, 128), F32)
        for q in range(8):
            one_row = jnp.where((lane & 7) == q, float(table[i, q]), one_row)
        base = jnp.where(sub == i, one_row, base)
    high = base.astype(BF16).astype(F32)
    block = lax.shift_right_logical(lane, 3)
    zero = jnp.zeros((8, 128), F32)
    empty = jnp.zeros((16, 128), F32)
    for a in range(0, 32, 2):
        parts = []
        for values in (high, base - high):
            pair = [jnp.where(block == (a + n) % 16, values, zero) for n in range(2)]
            pair = jnp.concatenate(pair, axis=0)
            parts.append([pair, empty] if a < 16 else [empty, pair])
        wide = jnp.concatenate(parts[0] + parts[1] + parts[0], axis=1)
        table_ref[pl.ds(8 * a, 16)] = wide.astype(BF16)


def lanes(block, index):
    wide = jnp.broadcast_to(index[None], (block.shape[0] // 8, 8, 128)).reshape(block.shape)
    return jnp.take_along_axis(block, wide, axis=1, mode="promise_in_bounds")


def set_mass(weight_ref, mass_ref):
    sub = lax.broadcasted_iota(jnp.int32, (8, 128), 0)
    along = jnp.zeros((8, 128), F32)
    for k in range(8):
        along = jnp.where(sub == k, float(WEIGHTS[k]), along)
    for i in range(8):
        for j in range(8):
            r = rows(i, j)
            mass_ref[r] = weight_ref[r] * (along * float(WEIGHTS[i] * WEIGHTS[j]))


def forward_k(source, carry_ref, weigh, table_ref, turned_ref, work):
    slope = along_k(table_ref, source[...])
    work[...] = carry_ref[2] * slope + along_k(turned_ref, weigh[...] * slope)


def adjoint_k(source, carry_ref, weigh, table_ref, turned_ref, work):
    slope = along_k(table_ref, source[...])
    work[...] = along_k(turned_ref, carry_ref[2] * source[...] + weigh[...] * slope)


def forward(source, carry_ref, weigh, work, target):
    for j in range(8):
        slopes = line(DM, [source[rows(i, j)] for i in range(8)])
        back = line(DM.T, [weigh[rows(i, j)] * slopes[i] for i in range(8)])
        for i in range(8):
            r = rows(i, j)
            target[r] = work[r] + (carry_ref[0, r] * slopes[i] + back[i])
    for i in range(8):
        slopes = line(DM, [source[rows(i, j)] for j in range(8)])
        back = line(DM.T, [weigh[rows(i, j)] * slopes[j] for j in range(8)])
        for j in range(8):
            r = rows(i, j)
            target[r] = target[r] + (carry_ref[1, r] * slopes[j] + back[j])


def adjoint(source, base, carry_ref, weigh, work, target):
    for j in range(8):
        values = [source[rows(i, j)] for i in range(8)]
        slopes = line(DM, values)
        fluxes = [
            carry_ref[0, rows(i, j)] * values[i] + weigh[rows(i, j)] * slopes[i] for i in range(8)
        ]
        back = line(DM.T, fluxes)
        for i in range(8):
            r = rows(i, j)
            target[r] = base[r] - (work[r] + back[i])
    for i in range(8):
        values = [source[rows(i, j)] for j in range(8)]
        slopes = line(DM, values)
        fluxes = [
            carry_ref[1, rows(i, j)] * values[j] + weigh[rows(i, j)] * slopes[j] for j in range(8)
        ]
        back = line(DM.T, fluxes)
        for j in range(8):
            r = rows(i, j)
            target[r] = target[r] - back[j]


def join_heights(ref, index):
    height, _, below, above = index
    lower = ref[pl.ds(0, 64, stride=8)]
    upper = ref[pl.ds(7, 64, stride=8)]
    tall = jnp.broadcast_to(height[None], (8, 8, 128)).reshape(64, 128)
    ref[pl.ds(0, 64, stride=8)] = lower + jnp.where(tall > 0, lanes(upper, below), 0.0)
    ref[pl.ds(7, 64, stride=8)] = upper + jnp.where(tall < 127, lanes(lower, above), 0.0)


def send_faces(c, ref, index, ends, out):
    inverse = index[1]
    for way in range(2):
        i_face = ref[pl.ds(pl.multiple_of(ends[0][way] * 64, 64), 64)]
        out[way][c] = lanes(i_face, inverse)
        for i in range(8):
            j_face = ref[pl.ds(pl.multiple_of(ends[1][way] * 8 + i * 64, 8), 8)]
            out[2 + way][c, pl.ds(i * 8, 8)] = lanes(j_face, inverse)


def add_faces(c, ref, index, ends, got):
    height = index[0]
    for way in range(2):
        r = pl.ds(pl.multiple_of(ends[0][way] * 64, 64), 64)
        part = lanes(got[way][c], height)
        ref[r] = ref[r] + (part * ends[2][0] if way else part)
    for way in range(2):
        for i in range(8):
            r = pl.ds(pl.multiple_of(ends[1][way] * 8 + i * 64, 8), 8)
            part = lanes(got[2 + way][c, pl.ds(i * 8, 8)], height)
            ref[r] = ref[r] + (part * ends[2][1] if way else part)


def ends_of(columns):
    column = lax.rem(lax.axis_index("elem") + columns // 2, columns * DA)
    row, place = lax.div(column, columns), lax.rem(column, columns)
    row_odd, place_odd = lax.rem(row, 2), lax.rem(place, 2)
    row_inside = jnp.where((row > 0) & (row < DA - 1), 1.0, 0.0)
    place_inside = jnp.where((place > 0) & (place < columns - 1), 1.0, 0.0)
    return (
        (7 - 7 * row_odd, 7 * row_odd),
        (7 - 7 * place_odd, 7 * place_odd),
        (row_inside, place_inside),
    )


def index_of(index_ref):
    return tuple(index_ref[n] for n in range(4))


def index_kernel(
    columns,
    moment_far,
    state_far,
    flow_far,
    weight_far,
    diff_far,
    numbers_far,
    moment_ref,
    state_ref,
    carry_ref,
    weigh_ref,
    table_ref,
    turned_ref,
    index_ref,
    joined_ref,
    ie_ref,
    io_ref,
    je_ref,
    jo_ref,
    weight_ref,
    mass_ref,
    flow_ref,
    numbers_ref,
    diff_ref,
    arrived,
):
    far = (numbers_far, weight_far, state_far, diff_far, moment_far, flow_far)
    near = (numbers_ref, weight_ref, state_ref, diff_ref, moment_ref, flow_ref)
    copies = [pltpu.make_async_copy(a, b, arrived.at[n]) for n, (a, b) in enumerate(zip(far, near))]
    for copy in copies:
        copy.start()
    write_table(DM, table_ref)
    write_table(DM.T, turned_ref)
    ends = ends_of(columns)
    copies[0].wait()
    height = jnp.broadcast_to(numbers_ref[...] & 127, (8, 128))
    square = jnp.broadcast_to(height[:1].astype(F32), (128, 128)).T
    lane = lax.broadcasted_iota(jnp.int32, (128, 128), 1).astype(F32)
    row = lax.broadcasted_iota(jnp.int32, (128, 128), 0).astype(F32)
    inverse = jnp.sum(jnp.where(square == lane, row, 0.0), axis=0, keepdims=True)
    inverse = jnp.broadcast_to(inverse, (8, 128)).astype(jnp.int32)
    index = (
        height,
        inverse,
        lanes(inverse, (height - 1) & 127),
        lanes(inverse, (height + 1) & 127),
    )
    for n in range(4):
        index_ref[n] = index[n]
    copies[1].wait()
    set_mass(weight_ref, mass_ref)
    joined_ref[3] = mass_ref[...]
    copies[2].wait()
    out = (ie_ref, io_ref, je_ref, jo_ref)
    for c in range(3):
        joined_ref[c] = state_ref[c]
    for c in range(4):
        join_heights(joined_ref.at[c], index)
        send_faces(c, joined_ref.at[c], index, ends, out)
    copies[3].wait()
    for f in range(3):
        weigh_ref[f] = mass_ref[...] * (DT * diff_ref[f])
    copies[5].wait()
    for d in range(3):
        carry_ref[d] = mass_ref[...] * (DT * flow_ref[d])
    copies[4].wait()


def moment_kernel(
    columns,
    moment_ref,
    carry_ref,
    weigh_ref,
    table_ref,
    turned_ref,
    index_ref,
    joined_ref,
    ie_ref,
    io_ref,
    je_ref,
    jo_ref,
    work_ref,
):
    ends = ends_of(columns)
    index = index_of(index_ref)
    out = (ie_ref, io_ref, je_ref, jo_ref)

    for f in range(3):
        at = (carry_ref, weigh_ref.at[f])
        forward_k(moment_ref.at[f], *at, table_ref, turned_ref, work_ref.at[f])
    for f in range(3):
        at = (carry_ref, weigh_ref.at[f])
        forward(moment_ref.at[f], *at, work_ref.at[f], joined_ref.at[f])
        join_heights(joined_ref.at[f], index)
        send_faces(f, joined_ref.at[f], index, ends, out)


def edge_kernel(columns, ie_ref, io_ref, je_ref, jo_ref, out_e, out_o):
    ends = ends_of(columns)
    for way, (face, out) in enumerate(((je_ref, out_e), (jo_ref, out_o))):
        out[...] = face[...]
        r = pl.ds(pl.multiple_of(ends[1][way] * 8, 8), 8)
        for other, got in enumerate((ie_ref, io_ref)):
            w = pl.ds(pl.multiple_of(ends[0][other] * 8, 8), 8)
            part = got[:, r]
            out[:, w] = out[:, w] + (part * ends[2][0] if other else part)


def state_kernel(
    columns,
    first,
    state_ref,
    carry_ref,
    weigh_ref,
    table_ref,
    turned_ref,
    index_ref,
    joined_ref,
    *refs,
):
    ends = ends_of(columns)
    index = index_of(index_ref)
    if first:
        got, (inverse_ref, state_out, joined_out), refs = refs[:4], refs[4:7], refs[7:]
        out, (work_ref, hold_ref) = refs[:4], refs[4:]
        held = hold_ref.at[0]
        held[...] = joined_ref[3]
        add_faces(3, held, index, ends, got)
        inverse_ref[...] = 1.0 / held[...]
    else:
        inverse_ref, *got = refs[:5]
        state_far, work_ref, hold_ref, state_out, sent = refs[5:]

    for f in range(3):
        held = hold_ref.at[f]
        held[...] = joined_ref[f]
        add_faces(f, held, index, ends, got)
        held[...] = held[...] * inverse_ref[...]
        at = (carry_ref, weigh_ref.at[f])
        adjoint_k(held, *at, table_ref, turned_ref, work_ref.at[f])
    for f in range(3):
        at = (carry_ref, weigh_ref.at[f])
        adjoint(hold_ref.at[f], state_ref.at[f], *at, work_ref.at[f], state_out.at[f])
        if first:
            joined_out[f] = state_out[f]
            join_heights(joined_out.at[f], index)
            send_faces(f, joined_out.at[f], index, ends, out)
        else:
            send_out(f, state_out, state_far, sent).start()
    if not first:
        for f in range(3):
            send_out(f, state_out, state_far, sent).wait()


def send_out(f, near, far, sent):
    return pltpu.make_async_copy(near.at[f], far.at[f], sent.at[f])


def moment_step(f, ends, index, moment_ref, joined_ref, inverse_ref, got, hold_ref, moment_out):
    held = hold_ref.at[f]
    held[...] = joined_ref[f]
    add_faces(f, held, index, ends, got)
    moment_out[f] = moment_ref[f] - held[...] * inverse_ref[...]


def middle_kernel(
    columns,
    moment_ref,
    carry_ref,
    weigh_ref,
    table_ref,
    turned_ref,
    index_ref,
    inverse_ref,
    joined_ref,
    gie_ref,
    gio_ref,
    gje_ref,
    gjo_ref,
    moment_out,
    joined_out,
    ie_ref,
    io_ref,
    je_ref,
    jo_ref,
    work_ref,
    hold_ref,
):
    ends = ends_of(columns)
    index = index_of(index_ref)
    out = (ie_ref, io_ref, je_ref, jo_ref)
    got = (gie_ref, gio_ref, gje_ref, gjo_ref)

    for f in range(3):
        moment_step(f, ends, index, moment_ref, joined_ref, inverse_ref, got, hold_ref, moment_out)
        at = (carry_ref, weigh_ref.at[f])
        forward_k(moment_out.at[f], *at, table_ref, turned_ref, work_ref.at[f])
    for f in range(3):
        at = (carry_ref, weigh_ref.at[f])
        forward(moment_out.at[f], *at, work_ref.at[f], joined_out.at[f])
        join_heights(joined_out.at[f], index)
        send_faces(f, joined_out.at[f], index, ends, out)


def last_kernel(
    columns,
    moment_ref,
    index_ref,
    inverse_ref,
    joined_ref,
    gie_ref,
    gio_ref,
    gje_ref,
    gjo_ref,
    moment_far,
    hold_ref,
    moment_out,
    sent,
):
    ends = ends_of(columns)
    index = index_of(index_ref)
    got = (gie_ref, gio_ref, gje_ref, gjo_ref)

    for f in range(3):
        moment_step(f, ends, index, moment_ref, joined_ref, inverse_ref, got, hold_ref, moment_out)
        send_out(f, moment_out, moment_far, sent).start()
    for f in range(3):
        send_out(f, moment_out, moment_far, sent).wait()


VMEM = pl.BlockSpec(memory_space=pltpu.VMEM)
FAR = pl.BlockSpec(memory_space=pltpu.HBM)


def call(kernel, specs, shapes, scratch, flops, *operands, out=VMEM):
    moved = sum(o.size * 4 for o in operands) + sum(int(np.prod(s)) * 4 for s, _ in shapes)
    return pl.pallas_call(
        kernel,
        out_shape=[jax.ShapeDtypeStruct(s, t) for s, t in shapes],
        in_specs=specs,
        out_specs=[out] * len(shapes),
        scratch_shapes=scratch,
        compiler_params=pltpu.CompilerParams(vmem_limit_bytes=32 * 1024 * 1024),
        cost_estimate=pl.CostEstimate(flops=flops, bytes_accessed=moved, transcendentals=0),
    )(*operands)


def pairings(devices):
    columns = devices // DA
    device = lambda row, place: (row % DA * columns + place - columns // 2) % devices

    def both(pairs):
        return pairs + [(b, a) for a, b in pairs]

    places, halves = range(columns), range(0, columns, 2)
    along_i = [
        [(device(r, s), device(r + 1, s)) for r in range(0, DA, 2) for s in places],
        [(device(r, s), device(r + 1, s)) for r in range(1, DA - 1, 2) for s in places]
        + [(device(r, s), device(r, s + 1)) for r in (0, DA - 1) for s in halves],
    ]
    along_j = [
        [(device(r, s), device(r, s + 1)) for r in range(DA) for s in halves],
        [(device(r, s - 1), device(r, s)) for r in range(DA) for s in halves if s]
        + [(device(r, columns - 1), device(r + 1, 0)) for r in range(DA)],
    ]
    return [both(p) for p in along_i], [both(p) for p in along_j]


def shards(moment_fields, adjoint_fields, velocity, mass_weights, diffusivity, numbering):
    devices = lax.axis_size("elem")
    columns = devices // DA
    along_i, along_j = pairings(devices)
    whole, block = ((3, 512, 128), F32), ((512, 128), F32)
    work = pltpu.VMEM((3, 512, 128), F32)

    def exchange(blocks, pairs):
        return [lax.ppermute(b, "elem", p) for b, p in zip(blocks, pairs)]

    def meet(count, faces):
        got_i = exchange(faces[:2], along_i)
        faces_j = call(
            functools.partial(edge_kernel, columns),
            [VMEM] * 4,
            [((count, 64, 128), F32)] * 2,
            [],
            count * 64 * 128,
            *got_i,
            *faces[2:],
        )
        return got_i + exchange(faces_j[::-1], along_j[::-1])[::-1]

    def far(array):
        return pltpu.with_memory_space_constraint(array, pltpu.HBM)

    def faces_shape(count):
        return [((count, 64, 128), F32)] * 4

    moment, state, carry, weigh, table, turned, index, joined_state, *faces_state = call(
        functools.partial(index_kernel, columns),
        [FAR] * 6,
        [whole] * 4
        + [((256, 768), BF16)] * 2
        + [((4, 8, 128), jnp.int32), ((4, 512, 128), F32)]
        + faces_shape(4),
        [
            pltpu.VMEM((512, 128), F32),
            pltpu.VMEM((512, 128), F32),
            work,
            pltpu.VMEM((1, 128), jnp.int32),
            pltpu.SMEM((3,), F32),
            pltpu.SemaphoreType.DMA((6,)),
        ],
        1_000_000,
        *map(far, (moment_fields, adjoint_fields, velocity, mass_weights)),
        *map(far, (diffusivity, numbering.reshape(1, 128))),
    )
    tables = (carry, weigh, table, turned, index)
    got_state = meet(4, faces_state)
    joined_moment, *faces_moment = call(
        functools.partial(moment_kernel, columns),
        [VMEM] * 6,
        [whole] + faces_shape(3),
        [work],
        20_000_000,
        moment,
        *tables,
    )
    got_moment = meet(3, faces_moment)
    inverse, state, joined_state, *faces_state = call(
        functools.partial(state_kernel, columns, True),
        [VMEM] * 11,
        [block, whole, whole] + faces_shape(3),
        [work] * 2,
        20_000_000,
        state,
        *tables,
        joined_state,
        *got_state,
    )
    got_state = meet(3, faces_state)
    moment, joined_moment, *faces_moment = call(
        functools.partial(middle_kernel, columns),
        [VMEM] * 12,
        [whole, whole] + faces_shape(3),
        [work] * 2,
        20_000_000,
        moment,
        *tables,
        inverse,
        joined_moment,
        *got_moment,
    )
    got_moment = meet(3, faces_moment)
    (state,) = call(
        functools.partial(state_kernel, columns, False),
        [VMEM] * 12,
        [whole],
        [work] * 3 + [pltpu.SemaphoreType.DMA((3,))],
        20_000_000,
        state,
        *tables,
        joined_state,
        inverse,
        *got_state,
        out=FAR,
    )
    (moment,) = call(
        functools.partial(last_kernel, columns),
        [VMEM] * 8,
        [whole],
        [work] * 2 + [pltpu.SemaphoreType.DMA((3,))],
        1_000_000,
        moment,
        index,
        inverse,
        joined_moment,
        *got_moment,
        out=FAR,
    )
    return moment, state


def solution(mesh):
    in_specs = (
        P(None, None, "elem"),
        P(None, None, "elem"),
        P(None, None, "elem"),
        P(None, "elem"),
        P(),
        P("elem"),
    )
    out_specs = (P(None, None, "elem"), P(None, None, "elem"))
    return jax.shard_map(shards, mesh=mesh, in_specs=in_specs, out_specs=out_specs, check_vma=False)
```

```python
import functools

import jax
import jax.numpy as jnp
import numpy as np
from jax import lax
from jax.experimental import pallas as pl
from jax.experimental.pallas import tpu as pltpu
from jax.sharding import PartitionSpec as P

DA = 4
DT = 0.001
F32 = jnp.float32
BF16 = jnp.bfloat16


def gll_tables():
    points = [
        -1.0,
        -0.8717401485096066,
        -0.5917001814331423,
        -0.2092992179024789,
        0.2092992179024789,
        0.5917001814331423,
        0.8717401485096066,
        1.0,
    ]
    weights = [
        0.03571428571428571,
        0.21070422714350603,
        0.3411226924835044,
        0.4124587946587038,
        0.4124587946587038,
        0.3411226924835044,
        0.21070422714350603,
        0.03571428571428571,
    ]
    barycentric = []
    for left_index in range(8):
        product = 1.0
        for right_index in range(8):
            if right_index != left_index:
                product = product * (points[left_index] - points[right_index])
        barycentric.append(1.0 / product)
    derivative = np.zeros((8, 8))
    for left_index in range(8):
        row_total = 0.0
        for right_index in range(8):
            if left_index != right_index:
                entry = (
                    barycentric[right_index]
                    / barycentric[left_index]
                    / (points[left_index] - points[right_index])
                )
                derivative[left_index, right_index] = entry
                row_total = row_total + entry
        derivative[left_index, left_index] = -row_total
    return derivative, np.asarray(weights)


DM, WEIGHTS = gll_tables()


def line(table, values):
    sums = [values[q] + values[7 - q] for q in range(4)]
    differences = [values[q] - values[7 - q] for q in range(4)]
    out = [None] * 8
    for i in range(4):
        even = odd = None
        for q in range(4):
            on_sum = float(table[i, q] + table[i, 7 - q]) / 2
            on_difference = float(table[i, q] - table[i, 7 - q]) / 2
            even = sums[q] * on_sum if even is None else even + sums[q] * on_sum
            odd = (
                differences[q] * on_difference
                if odd is None
                else odd + differences[q] * on_difference
            )
        out[i] = odd + even
        out[7 - i] = odd - even
    return out


def rows(i, j):
    return pl.ds((8 * i + j) * 8, 8)


def along_k(table_ref, block):
    wide = jnp.concatenate([block[:256], block[256:]], axis=1)
    high = wide.astype(BF16)
    low = (wide - high.astype(F32)).astype(BF16)
    parts = jnp.concatenate([high, high, low], axis=0)
    out = jnp.dot(table_ref[...], parts, preferred_element_type=F32)
    return jnp.concatenate([out[:, :128], out[:, 128:]], axis=0)


def write_table(table, table_ref):
    sub = lax.broadcasted_iota(jnp.int32, (8, 128), 0)
    lane = lax.broadcasted_iota(jnp.int32, (8, 128), 1)
    base = jnp.zeros((8, 128), F32)
    for i in range(8):
        one_row = jnp.zeros((8, 128), F32)
        for q in range(8):
            one_row = jnp.where((lane & 7) == q, float(table[i, q]), one_row)
        base = jnp.where(sub == i, one_row, base)
    high = base.astype(BF16).astype(F32)
    block = lax.shift_right_logical(lane, 3)
    zero = jnp.zeros((8, 128), F32)
    empty = jnp.zeros((16, 128), F32)
    for a in range(0, 32, 2):
        parts = []
        for values in (high, base - high):
            pair = [jnp.where(block == (a + n) % 16, values, zero) for n in range(2)]
            pair = jnp.concatenate(pair, axis=0)
            parts.append([pair, empty] if a < 16 else [empty, pair])
        wide = jnp.concatenate(parts[0] + parts[1] + parts[0], axis=1)
        table_ref[pl.ds(8 * a, 16)] = wide.astype(BF16)


def lanes(block, index):
    wide = jnp.broadcast_to(index[None], (block.shape[0] // 8, 8, 128)).reshape(block.shape)
    return jnp.take_along_axis(block, wide, axis=1, mode="promise_in_bounds")


def set_mass(weight_ref, mass_ref):
    sub = lax.broadcasted_iota(jnp.int32, (8, 128), 0)
    along = jnp.zeros((8, 128), F32)
    for k in range(8):
        along = jnp.where(sub == k, float(WEIGHTS[k]), along)
    for i in range(8):
        for j in range(8):
            r = rows(i, j)
            mass_ref[r] = weight_ref[r] * (along * float(WEIGHTS[i] * WEIGHTS[j]))


def slope_k(source, table_ref, slope):
    slope[...] = along_k(table_ref, source[...])


def forward_k(carry_ref, weigh, turned_ref, slope, work):
    work[...] = carry_ref[2] * slope[...] + along_k(turned_ref, weigh[...] * slope[...])


def adjoint_k(source, carry_ref, weigh, turned_ref, slope, work):
    work[...] = along_k(turned_ref, carry_ref[2] * source[...] + weigh[...] * slope[...])


def forward_i(source, carry_ref, weigh, target):
    for j in range(8):
        slopes = line(DM, [source[rows(i, j)] for i in range(8)])
        back = line(DM.T, [weigh[rows(i, j)] * slopes[i] for i in range(8)])
        for i in range(8):
            r = rows(i, j)
            target[r] = carry_ref[0, r] * slopes[i] + back[i]


def forward_j(source, carry_ref, weigh, work, target):
    for i in range(8):
        slopes = line(DM, [source[rows(i, j)] for j in range(8)])
        back = line(DM.T, [weigh[rows(i, j)] * slopes[j] for j in range(8)])
        for j in range(8):
            r = rows(i, j)
            target[r] = target[r] + (carry_ref[1, r] * slopes[j] + (back[j] + work[r]))


def adjoint_lines(d, source, carry_ref, weigh, line_rows):
    for these in line_rows:
        values = [source[r] for r in these]
        slopes = line(DM, values)
        fluxes = [carry_ref[d, r] * v + weigh[r] * g for r, v, g in zip(these, values, slopes)]
        yield from zip(these, line(DM.T, fluxes))


def adjoint_i(source, base, carry_ref, weigh, target):
    lines = [[rows(i, j) for i in range(8)] for j in range(8)]
    for r, back in adjoint_lines(0, source, carry_ref, weigh, lines):
        target[r] = base[r] - back


def adjoint_j(source, carry_ref, weigh, work, target):
    lines = [[rows(i, j) for j in range(8)] for i in range(8)]
    for r, back in adjoint_lines(1, source, carry_ref, weigh, lines):
        target[r] = target[r] - (back + work[r])


def forward(sources, carry_ref, weigh_ref, table_ref, turned_ref, slope_ref, work_ref, target, finish):
    slope_k(sources.at[0], table_ref, slope_ref.at[0])
    for f in range(3):
        at = (carry_ref, weigh_ref.at[f])
        forward_i(sources.at[f], *at, target.at[f])
        forward_k(*at, turned_ref, slope_ref.at[f], work_ref.at[f])
        if f < 2:
            slope_k(sources.at[f + 1], table_ref, slope_ref.at[f + 1])
        forward_j(sources.at[f], *at, work_ref.at[f], target.at[f])
        finish(f)


def adjoint(
    sources, base, carry_ref, weigh_ref, table_ref, turned_ref, slope_ref, work_ref, target, finish
):
    slope_k(sources.at[0], table_ref, slope_ref.at[0])
    for f in range(3):
        at = (carry_ref, weigh_ref.at[f])
        adjoint_i(sources.at[f], base.at[f], *at, target.at[f])
        adjoint_k(sources.at[f], *at, turned_ref, slope_ref.at[f], work_ref.at[f])
        if f < 2:
            slope_k(sources.at[f + 1], table_ref, slope_ref.at[f + 1])
        adjoint_j(sources.at[f], *at, work_ref.at[f], target.at[f])
        finish(f)


def join_heights(ref, index):
    height, _, below, above = index
    lower = ref[pl.ds(0, 64, stride=8)]
    upper = ref[pl.ds(7, 64, stride=8)]
    tall = jnp.broadcast_to(height[None], (8, 8, 128)).reshape(64, 128)
    ref[pl.ds(0, 64, stride=8)] = lower + jnp.where(tall > 0, lanes(upper, below), 0.0)
    ref[pl.ds(7, 64, stride=8)] = upper + jnp.where(tall < 127, lanes(lower, above), 0.0)


def send_faces(c, ref, index, ends, out):
    inverse = index[1]
    for way in range(2):
        i_face = ref[pl.ds(pl.multiple_of(ends[0][way] * 64, 64), 64)]
        out[way][c] = lanes(i_face, inverse)
        for i in range(8):
            j_face = ref[pl.ds(pl.multiple_of(ends[1][way] * 8 + i * 64, 8), 8)]
            out[2 + way][c, pl.ds(i * 8, 8)] = lanes(j_face, inverse)


def add_faces(c, ref, index, ends, got):
    height = index[0]
    for way in range(2):
        r = pl.ds(pl.multiple_of(ends[0][way] * 64, 64), 64)
        part = lanes(got[way][c], height)
        ref[r] = ref[r] + (part * ends[2][0] if way else part)
    for way in range(2):
        for i in range(8):
            r = pl.ds(pl.multiple_of(ends[1][way] * 8 + i * 64, 8), 8)
            part = lanes(got[3 - way][c, pl.ds(i * 8, 8)], height)
            ref[r] = ref[r] + (part * ends[2][1] if way else part)


def ends_of(columns):
    column = lax.rem(lax.axis_index("elem") + columns // 2, columns * DA)
    row, place = lax.div(column, columns), lax.rem(column, columns)
    row_odd, place_odd = lax.rem(row, 2), lax.rem(place, 2)
    row_inside = jnp.where((row > 0) & (row < DA - 1), 1.0, 0.0)
    place_inside = jnp.where((place > 0) & (place < columns - 1), 1.0, 0.0)
    return (
        (7 - 7 * row_odd, 7 * row_odd),
        (7 - 7 * place_odd, 7 * place_odd),
        (row_inside, place_inside),
    )


def index_of(index_ref):
    return tuple(index_ref[n] for n in range(4))


def index_kernel(
    columns,
    moment_far,
    state_far,
    flow_far,
    weight_far,
    diff_far,
    numbers_far,
    moment_ref,
    state_ref,
    carry_ref,
    weigh_ref,
    table_ref,
    turned_ref,
    index_ref,
    joined_ref,
    ie_ref,
    io_ref,
    je_ref,
    jo_ref,
    weight_ref,
    mass_ref,
    flow_ref,
    numbers_ref,
    diff_ref,
    arrived,
):
    far = (numbers_far, weight_far, state_far, diff_far, moment_far, flow_far)
    near = (numbers_ref, weight_ref, state_ref, diff_ref, moment_ref, flow_ref)
    copies = [pltpu.make_async_copy(a, b, arrived.at[n]) for n, (a, b) in enumerate(zip(far, near))]
    for copy in copies:
        copy.start()
    write_table(DM, table_ref)
    write_table(DM.T, turned_ref)
    ends = ends_of(columns)
    copies[0].wait()
    height = jnp.broadcast_to(numbers_ref[...] & 127, (8, 128))
    square = jnp.broadcast_to(height[:1].astype(F32), (128, 128)).T
    lane = lax.broadcasted_iota(jnp.int32, (128, 128), 1).astype(F32)
    row = lax.broadcasted_iota(jnp.int32, (128, 128), 0).astype(F32)
    inverse = jnp.sum(jnp.where(square == lane, row, 0.0), axis=0, keepdims=True)
    inverse = jnp.broadcast_to(inverse, (8, 128)).astype(jnp.int32)
    index = (
        height,
        inverse,
        lanes(inverse, (height - 1) & 127),
        lanes(inverse, (height + 1) & 127),
    )
    for n in range(4):
        index_ref[n] = index[n]
    copies[1].wait()
    set_mass(weight_ref, mass_ref)
    joined_ref[3] = mass_ref[...]
    copies[2].wait()
    out = (ie_ref, io_ref, je_ref, jo_ref)
    for c in range(3):
        joined_ref[c] = state_ref[c]
    for c in range(4):
        join_heights(joined_ref.at[c], index)
        send_faces(c, joined_ref.at[c], index, ends, out)
    copies[3].wait()
    for f in range(3):
        weigh_ref[f] = mass_ref[...] * (DT * diff_ref[f])
    copies[5].wait()
    for d in range(3):
        carry_ref[d] = mass_ref[...] * (DT * flow_ref[d])
    copies[4].wait()


def moment_kernel(
    columns,
    moment_ref,
    carry_ref,
    weigh_ref,
    table_ref,
    turned_ref,
    index_ref,
    joined_ref,
    ie_ref,
    io_ref,
    je_ref,
    jo_ref,
    slope_ref,
    work_ref,
):
    ends = ends_of(columns)
    index = index_of(index_ref)
    out = (ie_ref, io_ref, je_ref, jo_ref)

    def finish(f):
        join_heights(joined_ref.at[f], index)
        send_faces(f, joined_ref.at[f], index, ends, out)

    at = (carry_ref, weigh_ref, table_ref, turned_ref, slope_ref, work_ref)
    forward(moment_ref, *at, joined_ref, finish)


def edge_kernel(columns, way, ie_ref, io_ref, face, *refs):
    ends, out = ends_of(columns), refs[-1]
    out[...] = face[...]
    r = pl.ds(pl.multiple_of(ends[1][way] * 8, 8), 8)
    for other, got in enumerate((ie_ref, io_ref)):
        w = pl.ds(pl.multiple_of(ends[0][other] * 8, 8), 8)
        part = got[:, r]
        out[:, w] = out[:, w] + (part * ends[2][0] if other else part)


def state_kernel(
    columns,
    first,
    state_ref,
    carry_ref,
    weigh_ref,
    table_ref,
    turned_ref,
    index_ref,
    joined_ref,
    *refs,
):
    ends = ends_of(columns)
    index = index_of(index_ref)
    if first:
        got, (inverse_ref, state_out, joined_out), refs = refs[:4], refs[4:7], refs[7:]
        out, (slope_ref, work_ref, hold_ref) = refs[:4], refs[4:]
        held = hold_ref.at[0]
        held[...] = joined_ref[3]
        add_faces(3, held, index, ends, got)
        inverse_ref[...] = 1.0 / held[...]
    else:
        inverse_ref, *got = refs[:5]
        state_far, token_ref, slope_ref, work_ref, hold_ref, state_out, sent = refs[5:]
        token_ref[...] = jnp.zeros_like(token_ref)
    for f in range(3):
        held = hold_ref.at[f]
        held[...] = joined_ref[f]
        add_faces(f, held, index, ends, got)
        held[...] = held[...] * inverse_ref[...]

    def finish(f):
        if first:
            joined_out[f] = state_out[f]
            join_heights(joined_out.at[f], index)
            send_faces(f, joined_out.at[f], index, ends, out)
        else:
            send_out(f, state_out, state_far, sent).start()

    at = (carry_ref, weigh_ref, table_ref, turned_ref, slope_ref, work_ref)
    adjoint(hold_ref, state_ref, *at, state_out, finish)
    if not first:
        for f in range(3):
            send_out(f, state_out, state_far, sent).wait()


def send_out(f, near, far, sent):
    return pltpu.make_async_copy(near.at[f], far.at[f], sent.at[f])


def moment_step(f, ends, index, moment_ref, joined_ref, inverse_ref, got, hold_ref, moment_out):
    held = hold_ref.at[f]
    held[...] = joined_ref[f]
    add_faces(f, held, index, ends, got)
    moment_out[f] = moment_ref[f] - held[...] * inverse_ref[...]


def middle_kernel(
    columns,
    moment_ref,
    carry_ref,
    weigh_ref,
    table_ref,
    turned_ref,
    index_ref,
    inverse_ref,
    joined_ref,
    gie_ref,
    gio_ref,
    gjo_ref,
    gje_ref,
    moment_out,
    joined_out,
    ie_ref,
    io_ref,
    je_ref,
    jo_ref,
    slope_ref,
    work_ref,
    hold_ref,
):
    ends = ends_of(columns)
    index = index_of(index_ref)
    out = (ie_ref, io_ref, je_ref, jo_ref)
    got = (gie_ref, gio_ref, gjo_ref, gje_ref)
    for f in range(3):
        moment_step(f, ends, index, moment_ref, joined_ref, inverse_ref, got, hold_ref, moment_out)

    def finish(f):
        join_heights(joined_out.at[f], index)
        send_faces(f, joined_out.at[f], index, ends, out)

    at = (carry_ref, weigh_ref, table_ref, turned_ref, slope_ref, work_ref)
    forward(moment_out, *at, joined_out, finish)


def last_kernel(
    columns,
    moment_ref,
    index_ref,
    inverse_ref,
    joined_ref,
    gie_ref,
    gio_ref,
    gjo_ref,
    gje_ref,
    moment_far,
    hold_ref,
    moment_out,
    sent,
):
    ends = ends_of(columns)
    index = index_of(index_ref)
    got = (gie_ref, gio_ref, gjo_ref, gje_ref)

    for f in range(3):
        moment_step(f, ends, index, moment_ref, joined_ref, inverse_ref, got, hold_ref, moment_out)
        send_out(f, moment_out, moment_far, sent).start()
    for f in range(3):
        send_out(f, moment_out, moment_far, sent).wait()


VMEM = pl.BlockSpec(memory_space=pltpu.VMEM)
FAR = pl.BlockSpec(memory_space=pltpu.HBM)


def call(kernel, specs, shapes, scratch, flops, *operands, first_out=VMEM):
    moved = sum(o.size * 4 for o in operands) + sum(int(np.prod(s)) * 4 for s, _ in shapes)
    return pl.pallas_call(
        kernel,
        out_shape=[jax.ShapeDtypeStruct(s, t) for s, t in shapes],
        in_specs=specs,
        out_specs=[first_out] + [VMEM] * (len(shapes) - 1),
        scratch_shapes=scratch,
        compiler_params=pltpu.CompilerParams(vmem_limit_bytes=32 * 1024 * 1024),
        cost_estimate=pl.CostEstimate(flops=flops, bytes_accessed=moved, transcendentals=0),
    )(*operands)


def pairings(devices):
    columns = devices // DA
    device = lambda row, place: (row % DA * columns + place - columns // 2) % devices

    def both(pairs):
        return pairs + [(b, a) for a, b in pairs]

    places, halves = range(columns), range(0, columns, 2)
    along_i = [
        [(device(r, s), device(r + 1, s)) for r in range(0, DA, 2) for s in places],
        [(device(r, s), device(r + 1, s)) for r in range(1, DA - 1, 2) for s in places]
        + [(device(r, s), device(r, s + 1)) for r in (0, DA - 1) for s in halves],
    ]
    along_j = [
        [(device(r, s), device(r, s + 1)) for r in range(DA) for s in halves],
        [(device(r, s - 1), device(r, s)) for r in range(DA) for s in halves if s]
        + [(device(r, columns - 1), device(r + 1, 0)) for r in range(DA)],
    ]
    return [both(p) for p in along_i], [both(p) for p in along_j]


def shards(moment_fields, adjoint_fields, velocity, mass_weights, diffusivity, numbering):
    devices = lax.axis_size("elem")
    columns = devices // DA
    along_i, along_j = pairings(devices)
    whole, block = ((3, 512, 128), F32), ((512, 128), F32)
    work = pltpu.VMEM((3, 512, 128), F32)

    def exchange(block, pairs):
        return lax.ppermute(block, "elem", pairs)

    def settle(block, *after):
        anywhere = pl.BlockSpec(memory_space=pl.ANY)
        return pl.pallas_call(
            lambda *refs: None,
            out_shape=jax.ShapeDtypeStruct(block.shape, block.dtype),
            in_specs=[anywhere] * (1 + len(after)),
            out_specs=anywhere,
            input_output_aliases={0: 0},
        )(block, *after)

    def edge(count, way, *operands):
        return call(
            functools.partial(edge_kernel, columns, way),
            [VMEM] * len(operands),
            [((count, 64, 128), F32)],
            [],
            count * 64 * 128,
            *operands,
        )[0]

    def meet(count, faces):
        got_i = [exchange(faces[way], along_i[way]) for way in range(2)]
        far_face = edge(count, 1, *got_i, faces[3])
        near_face = edge(count, 0, *got_i, faces[2], far_face)
        return got_i + [exchange(far_face, along_j[1]), exchange(near_face, along_j[0])]

    def settled(got, *after):
        return got[:2] + [settle(got[2], *after), got[3]]

    def far(array):
        return pltpu.with_memory_space_constraint(array, pltpu.HBM)

    def faces_shape(count):
        return [((count, 64, 128), F32)] * 4

    moment, state, carry, weigh, table, turned, index, joined_state, *faces_state = call(
        functools.partial(index_kernel, columns),
        [FAR] * 6,
        [whole] * 4
        + [((256, 768), BF16)] * 2
        + [((4, 8, 128), jnp.int32), ((4, 512, 128), F32)]
        + faces_shape(4),
        [
            pltpu.VMEM((512, 128), F32),
            pltpu.VMEM((512, 128), F32),
            work,
            pltpu.VMEM((1, 128), jnp.int32),
            pltpu.SMEM((3,), F32),
            pltpu.SemaphoreType.DMA((6,)),
        ],
        1_000_000,
        *map(far, (moment_fields, adjoint_fields, velocity, mass_weights)),
        *map(far, (diffusivity, numbering.reshape(1, 128))),
    )
    tables = (carry, weigh, table, turned, index)
    got_state = meet(4, faces_state)
    joined_moment, *faces_moment = call(
        functools.partial(moment_kernel, columns),
        [VMEM] * 6,
        [whole] + faces_shape(3),
        [work] * 2,
        20_000_000,
        moment,
        *tables,
    )
    got_moment = meet(3, faces_moment)
    inverse, state, joined_state, *faces_state = call(
        functools.partial(state_kernel, columns, True),
        [VMEM] * 11,
        [block, whole, whole] + faces_shape(3),
        [work] * 3,
        20_000_000,
        state,
        *tables,
        joined_state,
        *settled(got_state),
    )
    got_state = meet(3, faces_state)
    moment, joined_moment, *faces_moment = call(
        functools.partial(middle_kernel, columns),
        [VMEM] * 12,
        [whole, whole] + faces_shape(3),
        [work] * 3,
        20_000_000,
        moment,
        *tables,
        inverse,
        joined_moment,
        *settled(got_moment, inverse),
    )
    got_moment = meet(3, faces_moment)
    state, token = call(
        functools.partial(state_kernel, columns, False),
        [VMEM] * 12,
        [whole, ((8, 128), F32)],
        [work] * 4 + [pltpu.SemaphoreType.DMA((3,))],
        20_000_000,
        state,
        *tables,
        joined_state,
        inverse,
        *settled(got_state),
        first_out=FAR,
    )
    (moment,) = call(
        functools.partial(last_kernel, columns),
        [VMEM] * 8,
        [whole],
        [work] * 2 + [pltpu.SemaphoreType.DMA((3,))],
        1_000_000,
        moment,
        index,
        inverse,
        joined_moment,
        *settled(got_moment, token),
        first_out=FAR,
    )
    return moment, state


def solution(mesh):
    in_specs = (
        P(None, None, "elem"),
        P(None, None, "elem"),
        P(None, None, "elem"),
        P(None, "elem"),
        P(),
        P("elem"),
    )
    out_specs = (P(None, None, "elem"), P(None, None, "elem"))
    return jax.shard_map(shards, mesh=mesh, in_specs=in_specs, out_specs=out_specs, check_vma=False)
```

```python
import functools

import jax
import jax.numpy as jnp
import numpy as np
from jax import lax
from jax.experimental import pallas as pl
from jax.experimental.pallas import tpu as pltpu
from jax.sharding import PartitionSpec as P

DA = 4
DT = 0.001
F32 = jnp.float32
BF16 = jnp.bfloat16


def gll_tables():
    points = [
        -1.0,
        -0.8717401485096066,
        -0.5917001814331423,
        -0.2092992179024789,
        0.2092992179024789,
        0.5917001814331423,
        0.8717401485096066,
        1.0,
    ]
    weights = [
        0.03571428571428571,
        0.21070422714350603,
        0.3411226924835044,
        0.4124587946587038,
        0.4124587946587038,
        0.3411226924835044,
        0.21070422714350603,
        0.03571428571428571,
    ]
    barycentric = []
    for left_index in range(8):
        product = 1.0
        for right_index in range(8):
            if right_index != left_index:
                product = product * (points[left_index] - points[right_index])
        barycentric.append(1.0 / product)
    derivative = np.zeros((8, 8))
    for left_index in range(8):
        row_total = 0.0
        for right_index in range(8):
            if left_index != right_index:
                entry = (
                    barycentric[right_index]
                    / barycentric[left_index]
                    / (points[left_index] - points[right_index])
                )
                derivative[left_index, right_index] = entry
                row_total = row_total + entry
        derivative[left_index, left_index] = -row_total
    return derivative, np.asarray(weights)


DM, WEIGHTS = gll_tables()


def line(table, values):
    sums = [values[q] + values[7 - q] for q in range(4)]
    differences = [values[q] - values[7 - q] for q in range(4)]
    out = [None] * 8
    for i in range(4):
        even = odd = None
        for q in range(4):
            on_sum = float(table[i, q] + table[i, 7 - q]) / 2
            on_difference = float(table[i, q] - table[i, 7 - q]) / 2
            even = sums[q] * on_sum if even is None else even + sums[q] * on_sum
            odd = (
                differences[q] * on_difference
                if odd is None
                else odd + differences[q] * on_difference
            )
        out[i] = odd + even
        out[7 - i] = odd - even
    return out


def rows(i, j):
    return pl.ds((8 * i + j) * 8, 8)


def along_k(table_ref, block):
    wide = jnp.concatenate([block[:256], block[256:]], axis=1)
    high = wide.astype(BF16)
    low = (wide - high.astype(F32)).astype(BF16)
    parts = jnp.concatenate([high, high, low], axis=0)
    out = jnp.dot(table_ref[...], parts, preferred_element_type=F32)
    return jnp.concatenate([out[:, :128], out[:, 128:]], axis=0)


def write_table(table, table_ref):
    sub = lax.broadcasted_iota(jnp.int32, (8, 128), 0)
    lane = lax.broadcasted_iota(jnp.int32, (8, 128), 1)
    base = jnp.zeros((8, 128), F32)
    for i in range(8):
        one_row = jnp.zeros((8, 128), F32)
        for q in range(8):
            one_row = jnp.where((lane & 7) == q, float(table[i, q]), one_row)
        base = jnp.where(sub == i, one_row, base)
    high = base.astype(BF16).astype(F32)
    block = lax.shift_right_logical(lane, 3)
    zero = jnp.zeros((8, 128), F32)
    empty = jnp.zeros((16, 128), F32)
    for a in range(0, 32, 2):
        parts = []
        for values in (high, base - high):
            pair = [jnp.where(block == (a + n) % 16, values, zero) for n in range(2)]
            pair = jnp.concatenate(pair, axis=0)
            parts.append([pair, empty] if a < 16 else [empty, pair])
        wide = jnp.concatenate(parts[0] + parts[1] + parts[0], axis=1)
        table_ref[pl.ds(8 * a, 16)] = wide.astype(BF16)


def lanes(block, index):
    wide = jnp.broadcast_to(index[None], (block.shape[0] // 8, 8, 128)).reshape(block.shape)
    return jnp.take_along_axis(block, wide, axis=1, mode="promise_in_bounds")


def set_mass(weight_ref, mass_ref):
    sub = lax.broadcasted_iota(jnp.int32, (8, 128), 0)
    along = jnp.zeros((8, 128), F32)
    for k in range(8):
        along = jnp.where(sub == k, float(WEIGHTS[k]), along)
    for i in range(8):
        for j in range(8):
            r = rows(i, j)
            mass_ref[r] = weight_ref[r] * (along * float(WEIGHTS[i] * WEIGHTS[j]))


def slope_k(source, table_ref, slope):
    slope[...] = along_k(table_ref, source[...])


def forward_k(carry_ref, weigh, turned_ref, slope, work):
    work[...] = carry_ref[2] * slope[...] + along_k(turned_ref, weigh[...] * slope[...])


def adjoint_k(source, carry_ref, weigh, turned_ref, slope, work):
    work[...] = along_k(turned_ref, carry_ref[2] * source[...] + weigh[...] * slope[...])


def forward_i(source, carry_ref, weigh, target):
    for j in range(8):
        slopes = line(DM, [source[rows(i, j)] for i in range(8)])
        back = line(DM.T, [weigh[rows(i, j)] * slopes[i] for i in range(8)])
        for i in range(8):
            r = rows(i, j)
            target[r] = carry_ref[0, r] * slopes[i] + back[i]


def forward_j(source, carry_ref, weigh, work, target):
    for i in range(8):
        slopes = line(DM, [source[rows(i, j)] for j in range(8)])
        back = line(DM.T, [weigh[rows(i, j)] * slopes[j] for j in range(8)])
        for j in range(8):
            r = rows(i, j)
            target[r] = target[r] + (carry_ref[1, r] * slopes[j] + (back[j] + work[r]))


def adjoint_lines(d, source, carry_ref, weigh, line_rows):
    for these in line_rows:
        values = [source[r] for r in these]
        slopes = line(DM, values)
        fluxes = [carry_ref[d, r] * v + weigh[r] * g for r, v, g in zip(these, values, slopes)]
        yield from zip(these, line(DM.T, fluxes))


def adjoint_i(source, base, carry_ref, weigh, target):
    lines = [[rows(i, j) for i in range(8)] for j in range(8)]
    for r, back in adjoint_lines(0, source, carry_ref, weigh, lines):
        target[r] = base[r] - back


def adjoint_j(source, carry_ref, weigh, work, target):
    lines = [[rows(i, j) for j in range(8)] for i in range(8)]
    for r, back in adjoint_lines(1, source, carry_ref, weigh, lines):
        target[r] = target[r] - (back + work[r])


def forward(sources, carry_ref, weigh_ref, table_ref, turned_ref, slope_ref, work_ref, target, finish):
    slope_k(sources.at[0], table_ref, slope_ref.at[0])
    for f in range(3):
        at = (carry_ref, weigh_ref.at[f])
        forward_i(sources.at[f], *at, target.at[f])
        forward_k(*at, turned_ref, slope_ref.at[f], work_ref.at[f])
        if f < 2:
            slope_k(sources.at[f + 1], table_ref, slope_ref.at[f + 1])
        forward_j(sources.at[f], *at, work_ref.at[f], target.at[f])
        finish(f)


def adjoint(
    sources, base, carry_ref, weigh_ref, table_ref, turned_ref, slope_ref, work_ref, target, finish
):
    slope_k(sources.at[0], table_ref, slope_ref.at[0])
    for f in range(3):
        at = (carry_ref, weigh_ref.at[f])
        adjoint_i(sources.at[f], base.at[f], *at, target.at[f])
        adjoint_k(sources.at[f], *at, turned_ref, slope_ref.at[f], work_ref.at[f])
        if f < 2:
            slope_k(sources.at[f + 1], table_ref, slope_ref.at[f + 1])
        adjoint_j(sources.at[f], *at, work_ref.at[f], target.at[f])
        finish(f)


def join_heights(ref, index):
    height, _, below, above = index
    lower = ref[pl.ds(0, 64, stride=8)]
    upper = ref[pl.ds(7, 64, stride=8)]
    tall = jnp.broadcast_to(height[None], (8, 8, 128)).reshape(64, 128)
    ref[pl.ds(0, 64, stride=8)] = lower + jnp.where(tall > 0, lanes(upper, below), 0.0)
    ref[pl.ds(7, 64, stride=8)] = upper + jnp.where(tall < 127, lanes(lower, above), 0.0)


def send_faces(c, ref, index, ends, out):
    inverse = index[1]
    for way in range(2):
        i_face = ref[pl.ds(pl.multiple_of(ends[0][way] * 64, 64), 64)]
        out[way][c] = lanes(i_face, inverse)
        for i in range(8):
            j_face = ref[pl.ds(pl.multiple_of(ends[1][way] * 8 + i * 64, 8), 8)]
            out[2 + way][c, pl.ds(i * 8, 8)] = lanes(j_face, inverse)


def add_faces(c, ref, index, ends, got):
    height = index[0]
    for way in range(2):
        r = pl.ds(pl.multiple_of(ends[0][way] * 64, 64), 64)
        part = lanes(got[way][c], height)
        ref[r] = ref[r] + (part * ends[2][0] if way else part)
    for way in range(2):
        for i in range(8):
            r = pl.ds(pl.multiple_of(ends[1][way] * 8 + i * 64, 8), 8)
            part = lanes(got[3 - way][c, pl.ds(i * 8, 8)], height)
            ref[r] = ref[r] + (part * ends[2][1] if way else part)


def ends_of(columns):
    column = lax.rem(lax.axis_index("elem") + columns // 2, columns * DA)
    row, place = lax.div(column, columns), lax.rem(column, columns)
    row_odd, place_odd = lax.rem(row, 2), lax.rem(place, 2)
    row_inside = jnp.where((row > 0) & (row < DA - 1), 1.0, 0.0)
    place_inside = jnp.where((place > 0) & (place < columns - 1), 1.0, 0.0)
    return (
        (7 - 7 * row_odd, 7 * row_odd),
        (7 - 7 * place_odd, 7 * place_odd),
        (row_inside, place_inside),
    )


def index_of(index_ref):
    return tuple(index_ref[n] for n in range(4))


def index_kernel(
    columns,
    moment_far,
    state_far,
    flow_far,
    weight_far,
    diff_far,
    numbers_far,
    moment_ref,
    state_ref,
    carry_ref,
    weigh_ref,
    table_ref,
    turned_ref,
    index_ref,
    joined_ref,
    ie_ref,
    io_ref,
    je_ref,
    jo_ref,
    weight_ref,
    mass_ref,
    flow_ref,
    numbers_ref,
    diff_ref,
    arrived,
):
    far = (numbers_far, weight_far, state_far, diff_far, moment_far, flow_far)
    near = (numbers_ref, weight_ref, state_ref, diff_ref, moment_ref, flow_ref)
    copies = [pltpu.make_async_copy(a, b, arrived.at[n]) for n, (a, b) in enumerate(zip(far, near))]
    for copy in copies:
        copy.start()
    write_table(DM, table_ref)
    write_table(DM.T, turned_ref)
    ends = ends_of(columns)
    copies[0].wait()
    height = jnp.broadcast_to(numbers_ref[...] & 127, (8, 128))
    square = jnp.broadcast_to(height[:1].astype(F32), (128, 128)).T
    lane = lax.broadcasted_iota(jnp.int32, (128, 128), 1).astype(F32)
    row = lax.broadcasted_iota(jnp.int32, (128, 128), 0).astype(F32)
    inverse = jnp.sum(jnp.where(square == lane, row, 0.0), axis=0, keepdims=True)
    inverse = jnp.broadcast_to(inverse, (8, 128)).astype(jnp.int32)
    index = (
        height,
        inverse,
        lanes(inverse, (height - 1) & 127),
        lanes(inverse, (height + 1) & 127),
    )
    for n in range(4):
        index_ref[n] = index[n]
    copies[1].wait()
    set_mass(weight_ref, mass_ref)
    joined_ref[3] = mass_ref[...]
    copies[2].wait()
    out = (ie_ref, io_ref, je_ref, jo_ref)
    for c in range(3):
        joined_ref[c] = state_ref[c]
    for c in range(4):
        join_heights(joined_ref.at[c], index)
        send_faces(c, joined_ref.at[c], index, ends, out)
    copies[3].wait()
    for f in range(3):
        weigh_ref[f] = mass_ref[...] * (DT * diff_ref[f])
    copies[5].wait()
    for d in range(3):
        carry_ref[d] = mass_ref[...] * (DT * flow_ref[d])
    copies[4].wait()


def moment_kernel(
    columns,
    moment_ref,
    carry_ref,
    weigh_ref,
    table_ref,
    turned_ref,
    index_ref,
    joined_ref,
    ie_ref,
    io_ref,
    je_ref,
    jo_ref,
    slope_ref,
    work_ref,
):
    ends = ends_of(columns)
    index = index_of(index_ref)
    out = (ie_ref, io_ref, je_ref, jo_ref)

    def finish(f):
        join_heights(joined_ref.at[f], index)
        send_faces(f, joined_ref.at[f], index, ends, out)

    at = (carry_ref, weigh_ref, table_ref, turned_ref, slope_ref, work_ref)
    forward(moment_ref, *at, joined_ref, finish)


def edge_kernel(columns, way, ie_ref, io_ref, face, *refs):
    ends, out = ends_of(columns), refs[-1]
    out[...] = face[...]
    r = pl.ds(pl.multiple_of(ends[1][way] * 8, 8), 8)
    for other, got in enumerate((ie_ref, io_ref)):
        w = pl.ds(pl.multiple_of(ends[0][other] * 8, 8), 8)
        part = got[:, r]
        out[:, w] = out[:, w] + (part * ends[2][0] if other else part)


def state_kernel(
    columns,
    first,
    state_ref,
    carry_ref,
    weigh_ref,
    table_ref,
    turned_ref,
    index_ref,
    joined_ref,
    *refs,
):
    ends = ends_of(columns)
    index = index_of(index_ref)
    if first:
        got, (inverse_ref, state_out, joined_out), refs = refs[:4], refs[4:7], refs[7:]
        out, (slope_ref, work_ref, hold_ref) = refs[:4], refs[4:]
        held = hold_ref.at[0]
        held[...] = joined_ref[3]
        add_faces(3, held, index, ends, got)
        inverse_ref[...] = 1.0 / held[...]
    else:
        inverse_ref, *got = refs[:5]
        state_far, token_ref, slope_ref, work_ref, hold_ref, state_out, sent = refs[5:]
        token_ref[...] = jnp.zeros_like(token_ref)
    for f in range(3):
        held = hold_ref.at[f]
        held[...] = joined_ref[f]
        add_faces(f, held, index, ends, got)
        held[...] = held[...] * inverse_ref[...]

    def finish(f):
        if first:
            joined_out[f] = state_out[f]
            join_heights(joined_out.at[f], index)
            send_faces(f, joined_out.at[f], index, ends, out)
        else:
            send_out(f, state_out, state_far, sent).start()

    at = (carry_ref, weigh_ref, table_ref, turned_ref, slope_ref, work_ref)
    adjoint(hold_ref, state_ref, *at, state_out, finish)
    if not first:
        for f in range(3):
            send_out(f, state_out, state_far, sent).wait()


def send_out(f, near, far, sent):
    return pltpu.make_async_copy(near.at[f], far.at[f], sent.at[f])


def moment_step(f, ends, index, moment_ref, joined_ref, inverse_ref, got, hold_ref, moment_out):
    held = hold_ref.at[f]
    held[...] = joined_ref[f]
    add_faces(f, held, index, ends, got)
    moment_out[f] = moment_ref[f] - held[...] * inverse_ref[...]


def middle_kernel(
    columns,
    moment_ref,
    carry_ref,
    weigh_ref,
    table_ref,
    turned_ref,
    index_ref,
    inverse_ref,
    joined_ref,
    gie_ref,
    gio_ref,
    gjo_ref,
    gje_ref,
    moment_out,
    joined_out,
    ie_ref,
    io_ref,
    je_ref,
    jo_ref,
    slope_ref,
    work_ref,
    hold_ref,
):
    ends = ends_of(columns)
    index = index_of(index_ref)
    out = (ie_ref, io_ref, je_ref, jo_ref)
    got = (gie_ref, gio_ref, gjo_ref, gje_ref)
    for f in range(3):
        moment_step(f, ends, index, moment_ref, joined_ref, inverse_ref, got, hold_ref, moment_out)

    def finish(f):
        join_heights(joined_out.at[f], index)
        send_faces(f, joined_out.at[f], index, ends, out)

    at = (carry_ref, weigh_ref, table_ref, turned_ref, slope_ref, work_ref)
    forward(moment_out, *at, joined_out, finish)


def last_kernel(
    columns,
    moment_ref,
    index_ref,
    inverse_ref,
    joined_ref,
    gie_ref,
    gio_ref,
    gjo_ref,
    gje_ref,
    moment_far,
    hold_ref,
    moment_out,
    sent,
):
    ends = ends_of(columns)
    index = index_of(index_ref)
    got = (gie_ref, gio_ref, gjo_ref, gje_ref)

    for f in range(3):
        moment_step(f, ends, index, moment_ref, joined_ref, inverse_ref, got, hold_ref, moment_out)
        send_out(f, moment_out, moment_far, sent).start()
    for f in range(3):
        send_out(f, moment_out, moment_far, sent).wait()


VMEM = pl.BlockSpec(memory_space=pltpu.VMEM)
FAR = pl.BlockSpec(memory_space=pltpu.HBM)


def call(kernel, specs, shapes, scratch, flops, *operands, first_out=VMEM):
    moved = sum(o.size * 4 for o in operands) + sum(int(np.prod(s)) * 4 for s, _ in shapes)
    return pl.pallas_call(
        kernel,
        out_shape=[jax.ShapeDtypeStruct(s, t) for s, t in shapes],
        in_specs=specs,
        out_specs=[first_out] + [VMEM] * (len(shapes) - 1),
        scratch_shapes=scratch,
        compiler_params=pltpu.CompilerParams(vmem_limit_bytes=32 * 1024 * 1024),
        cost_estimate=pl.CostEstimate(flops=flops, bytes_accessed=moved, transcendentals=0),
    )(*operands)


def pairings(devices):
    columns = devices // DA
    device = lambda row, place: (row % DA * columns + place - columns // 2) % devices

    def both(pairs):
        return pairs + [(b, a) for a, b in pairs]

    places, halves = range(columns), range(0, columns, 2)
    along_i = [
        [(device(r, s), device(r + 1, s)) for r in range(0, DA, 2) for s in places],
        [(device(r, s), device(r + 1, s)) for r in range(1, DA - 1, 2) for s in places]
        + [(device(r, s), device(r, s + 1)) for r in (0, DA - 1) for s in halves],
    ]
    along_j = [
        [(device(r, s), device(r, s + 1)) for r in range(DA) for s in halves],
        [(device(r, s - 1), device(r, s)) for r in range(DA) for s in halves if s]
        + [(device(r, columns - 1), device(r + 1, 0)) for r in range(DA)],
    ]
    return [both(p) for p in along_i], [both(p) for p in along_j]


def shards(moment_fields, adjoint_fields, velocity, mass_weights, diffusivity, numbering):
    devices = lax.axis_size("elem")
    columns = devices // DA
    along_i, along_j = pairings(devices)
    whole, block = ((3, 512, 128), F32), ((512, 128), F32)
    work = pltpu.VMEM((3, 512, 128), F32)

    def exchange(block, pairs):
        return lax.ppermute(block, "elem", pairs)

    def settle(block, *after):
        anywhere = pl.BlockSpec(memory_space=pl.ANY)
        return pl.pallas_call(
            lambda *refs: None,
            out_shape=jax.ShapeDtypeStruct(block.shape, block.dtype),
            in_specs=[anywhere] * (1 + len(after)),
            out_specs=anywhere,
            input_output_aliases={0: 0},
            compiler_params=pltpu.CompilerParams(vmem_limit_bytes=1024 * 1024),
        )(block, *after)

    def edge(count, way, *operands):
        return call(
            functools.partial(edge_kernel, columns, way),
            [VMEM] * len(operands),
            [((count, 64, 128), F32)],
            [],
            count * 64 * 128,
            *operands,
        )[0]

    def meet(count, faces):
        got_i = [exchange(faces[way], along_i[way]) for way in range(2)]
        far_face = edge(count, 1, *got_i, faces[3])
        near_face = edge(count, 0, *got_i, faces[2], far_face)
        return got_i + [exchange(far_face, along_j[1]), exchange(near_face, along_j[0])]

    def settled(got, *after):
        return got[:2] + [settle(got[2], *after), got[3]]

    def far(array):
        return pltpu.with_memory_space_constraint(array, pltpu.HBM)

    def faces_shape(count):
        return [((count, 64, 128), F32)] * 4

    moment, state, carry, weigh, table, turned, index, joined_state, *faces_state = call(
        functools.partial(index_kernel, columns),
        [FAR] * 6,
        [whole] * 4
        + [((256, 768), BF16)] * 2
        + [((4, 8, 128), jnp.int32), ((4, 512, 128), F32)]
        + faces_shape(4),
        [
            pltpu.VMEM((512, 128), F32),
            pltpu.VMEM((512, 128), F32),
            work,
            pltpu.VMEM((1, 128), jnp.int32),
            pltpu.SMEM((3,), F32),
            pltpu.SemaphoreType.DMA((6,)),
        ],
        1_000_000,
        *map(far, (moment_fields, adjoint_fields, velocity, mass_weights)),
        *map(far, (diffusivity, numbering.reshape(1, 128))),
    )
    tables = (carry, weigh, table, turned, index)
    got_state = meet(4, faces_state)
    joined_moment, *faces_moment = call(
        functools.partial(moment_kernel, columns),
        [VMEM] * 6,
        [whole] + faces_shape(3),
        [work] * 2,
        20_000_000,
        moment,
        *tables,
    )
    got_moment = meet(3, faces_moment)
    inverse, state, joined_state, *faces_state = call(
        functools.partial(state_kernel, columns, True),
        [VMEM] * 11,
        [block, whole, whole] + faces_shape(3),
        [work] * 3,
        20_000_000,
        state,
        *tables,
        joined_state,
        *settled(got_state),
    )
    got_state = meet(3, faces_state)
    moment, joined_moment, *faces_moment = call(
        functools.partial(middle_kernel, columns),
        [VMEM] * 12,
        [whole, whole] + faces_shape(3),
        [work] * 3,
        20_000_000,
        moment,
        *tables,
        inverse,
        joined_moment,
        *settled(got_moment, inverse),
    )
    got_moment = meet(3, faces_moment)
    state, token = call(
        functools.partial(state_kernel, columns, False),
        [VMEM] * 12,
        [whole, ((8, 128), F32)],
        [work] * 4 + [pltpu.SemaphoreType.DMA((3,))],
        20_000_000,
        state,
        *tables,
        joined_state,
        inverse,
        *settled(got_state),
        first_out=FAR,
    )
    (moment,) = call(
        functools.partial(last_kernel, columns),
        [VMEM] * 8,
        [whole],
        [work] * 2 + [pltpu.SemaphoreType.DMA((3,))],
        1_000_000,
        moment,
        index,
        inverse,
        joined_moment,
        *settled(got_moment, token),
        first_out=FAR,
    )
    return moment, state


def solution(mesh):
    in_specs = (
        P(None, None, "elem"),
        P(None, None, "elem"),
        P(None, None, "elem"),
        P(None, "elem"),
        P(),
        P("elem"),
    )
    out_specs = (P(None, None, "elem"), P(None, None, "elem"))
    return jax.shard_map(shards, mesh=mesh, in_specs=in_specs, out_specs=out_specs, check_vma=False)
```

```python
import functools

import jax
import jax.numpy as jnp
import numpy as np
from jax import lax
from jax.experimental import pallas as pl
from jax.experimental.pallas import tpu as pltpu
from jax.sharding import PartitionSpec as P

DA = 4
DT = 0.001
F32 = jnp.float32
BF16 = jnp.bfloat16


def gll_tables():
    points = [
        -1.0,
        -0.8717401485096066,
        -0.5917001814331423,
        -0.2092992179024789,
        0.2092992179024789,
        0.5917001814331423,
        0.8717401485096066,
        1.0,
    ]
    weights = [
        0.03571428571428571,
        0.21070422714350603,
        0.3411226924835044,
        0.4124587946587038,
        0.4124587946587038,
        0.3411226924835044,
        0.21070422714350603,
        0.03571428571428571,
    ]
    barycentric = []
    for left_index in range(8):
        product = 1.0
        for right_index in range(8):
            if right_index != left_index:
                product = product * (points[left_index] - points[right_index])
        barycentric.append(1.0 / product)
    derivative = np.zeros((8, 8))
    for left_index in range(8):
        row_total = 0.0
        for right_index in range(8):
            if left_index != right_index:
                entry = (
                    barycentric[right_index]
                    / barycentric[left_index]
                    / (points[left_index] - points[right_index])
                )
                derivative[left_index, right_index] = entry
                row_total = row_total + entry
        derivative[left_index, left_index] = -row_total
    return derivative, np.asarray(weights)


DM, WEIGHTS = gll_tables()


def line(table, values):
    sums = [values[q] + values[7 - q] for q in range(4)]
    differences = [values[q] - values[7 - q] for q in range(4)]
    out = [None] * 8
    for i in range(4):
        even = odd = None
        for q in range(4):
            on_sum = float(table[i, q] + table[i, 7 - q]) / 2
            on_difference = float(table[i, q] - table[i, 7 - q]) / 2
            even = sums[q] * on_sum if even is None else even + sums[q] * on_sum
            odd = (
                differences[q] * on_difference
                if odd is None
                else odd + differences[q] * on_difference
            )
        out[i] = odd + even
        out[7 - i] = odd - even
    return out


def rows(i, j):
    return pl.ds((8 * i + j) * 8, 8)


def along_k(table_ref, block):
    wide = jnp.concatenate([block[:256], block[256:]], axis=1)
    high = wide.astype(BF16)
    low = (wide - high.astype(F32)).astype(BF16)
    parts = jnp.concatenate([high, high, low], axis=0)
    out = jnp.dot(table_ref[...], parts, preferred_element_type=F32)
    return jnp.concatenate([out[:, :128], out[:, 128:]], axis=0)


def write_table(table, table_ref):
    sub = lax.broadcasted_iota(jnp.int32, (8, 128), 0)
    lane = lax.broadcasted_iota(jnp.int32, (8, 128), 1)
    base = jnp.zeros((8, 128), F32)
    for i in range(8):
        one_row = jnp.zeros((8, 128), F32)
        for q in range(8):
            one_row = jnp.where((lane & 7) == q, float(table[i, q]), one_row)
        base = jnp.where(sub == i, one_row, base)
    high = base.astype(BF16).astype(F32)
    block = lax.shift_right_logical(lane, 3)
    zero = jnp.zeros((8, 128), F32)
    empty = jnp.zeros((16, 128), F32)
    for a in range(0, 32, 2):
        parts = []
        for values in (high, base - high):
            pair = [jnp.where(block == (a + n) % 16, values, zero) for n in range(2)]
            pair = jnp.concatenate(pair, axis=0)
            parts.append([pair, empty] if a < 16 else [empty, pair])
        wide = jnp.concatenate(parts[0] + parts[1] + parts[0], axis=1)
        table_ref[pl.ds(8 * a, 16)] = wide.astype(BF16)


def lanes(block, index):
    wide = jnp.broadcast_to(index[None], (block.shape[0] // 8, 8, 128)).reshape(block.shape)
    return jnp.take_along_axis(block, wide, axis=1, mode="promise_in_bounds")


def set_mass(weight_ref, mass_ref):
    sub = lax.broadcasted_iota(jnp.int32, (8, 128), 0)
    along = jnp.zeros((8, 128), F32)
    for k in range(8):
        along = jnp.where(sub == k, float(WEIGHTS[k]), along)
    for i in range(8):
        for j in range(8):
            r = rows(i, j)
            mass_ref[r] = weight_ref[r] * (along * float(WEIGHTS[i] * WEIGHTS[j]))


def slope_k(source, table_ref, slope):
    slope[...] = along_k(table_ref, source[...])


def forward_k(carry_ref, weigh, turned_ref, slope, work):
    work[...] = carry_ref[2] * slope[...] + along_k(turned_ref, weigh[...] * slope[...])


def adjoint_k(source, carry_ref, weigh, turned_ref, slope, work):
    work[...] = along_k(turned_ref, carry_ref[2] * source[...] + weigh[...] * slope[...])


def forward_i(source, carry_ref, weigh, target):
    for j in range(8):
        slopes = line(DM, [source[rows(i, j)] for i in range(8)])
        back = line(DM.T, [weigh[rows(i, j)] * slopes[i] for i in range(8)])
        for i in range(8):
            r = rows(i, j)
            target[r] = carry_ref[0, r] * slopes[i] + back[i]


def forward_j(source, carry_ref, weigh, work, target):
    for i in range(8):
        slopes = line(DM, [source[rows(i, j)] for j in range(8)])
        back = line(DM.T, [weigh[rows(i, j)] * slopes[j] for j in range(8)])
        for j in range(8):
            r = rows(i, j)
            target[r] = target[r] + (carry_ref[1, r] * slopes[j] + (back[j] + work[r]))


def adjoint_lines(d, source, carry_ref, weigh, line_rows):
    for these in line_rows:
        values = [source[r] for r in these]
        slopes = line(DM, values)
        fluxes = [carry_ref[d, r] * v + weigh[r] * g for r, v, g in zip(these, values, slopes)]
        yield from zip(these, line(DM.T, fluxes))


def adjoint_i(source, base, carry_ref, weigh, target):
    lines = [[rows(i, j) for i in range(8)] for j in range(8)]
    for r, back in adjoint_lines(0, source, carry_ref, weigh, lines):
        target[r] = base[r] - back


def adjoint_j(source, carry_ref, weigh, work, target):
    lines = [[rows(i, j) for j in range(8)] for i in range(8)]
    for r, back in adjoint_lines(1, source, carry_ref, weigh, lines):
        target[r] = target[r] - (back + work[r])


def forward(sources, carry_ref, weigh_ref, table_ref, turned_ref, slope_ref, work_ref, target, finish):
    slope_k(sources.at[0], table_ref, slope_ref.at[0])
    for f in range(3):
        at = (carry_ref, weigh_ref.at[f])
        forward_i(sources.at[f], *at, target.at[f])
        forward_k(*at, turned_ref, slope_ref.at[f], work_ref.at[f])
        if f < 2:
            slope_k(sources.at[f + 1], table_ref, slope_ref.at[f + 1])
        forward_j(sources.at[f], *at, work_ref.at[f], target.at[f])
        finish(f)


def adjoint(
    sources, base, carry_ref, weigh_ref, table_ref, turned_ref, slope_ref, work_ref, target, finish
):
    slope_k(sources.at[0], table_ref, slope_ref.at[0])
    for f in range(3):
        at = (carry_ref, weigh_ref.at[f])
        adjoint_i(sources.at[f], base.at[f], *at, target.at[f])
        adjoint_k(sources.at[f], *at, turned_ref, slope_ref.at[f], work_ref.at[f])
        if f < 2:
            slope_k(sources.at[f + 1], table_ref, slope_ref.at[f + 1])
        adjoint_j(sources.at[f], *at, work_ref.at[f], target.at[f])
        finish(f)


def join_heights(ref, index):
    height, _, below, above = index
    lower = ref[pl.ds(0, 64, stride=8)]
    upper = ref[pl.ds(7, 64, stride=8)]
    tall = jnp.broadcast_to(height[None], (8, 8, 128)).reshape(64, 128)
    ref[pl.ds(0, 64, stride=8)] = lower + jnp.where(tall > 0, lanes(upper, below), 0.0)
    ref[pl.ds(7, 64, stride=8)] = upper + jnp.where(tall < 127, lanes(lower, above), 0.0)


def face_rows(ends, axis, way, k):
    end = ends[axis][way]
    return pl.ds(end * 8 + k, 8, stride=64) if axis else pl.ds(end * 64 + k, 8, stride=8)


def tile(c, k):
    return pl.ds((7 * c + k) * 8, 8)


def top_tile(ref):
    return pl.ds(ref.shape[0] - 8, 8)


def send_faces(c, ref, index, ends, out):
    inverse = index[1]
    top = jnp.broadcast_to(inverse[:, 127:], (8, 128))
    lane = lax.broadcasted_iota(jnp.int32, (8, 128), 1)
    for axis in range(2):
        for way in range(2):
            face = out[2 * axis + way]
            for k in range(7):
                face[tile(c, k)] = lanes(ref[face_rows(ends, axis, way, k)], inverse)
            last = lanes(ref[face_rows(ends, axis, way, 7)], top)
            others = face[top_tile(face)] if c else jnp.zeros((8, 128), F32)
            face[top_tile(face)] = jnp.where(lane == c, last, others)


def add_faces(c, ref, index, ends, got):
    height = index[0]
    above = (height + 1) & 127
    own = jnp.full((8, 128), c, jnp.int32)
    for axis in range(2):
        for way in range(2):
            face = got[3 - way if axis else way]
            last = jnp.where(
                height < 127, lanes(face[tile(c, 0)], above), lanes(face[top_tile(face)], own)
            )
            parts = [lanes(face[tile(c, k)], height) for k in range(7)] + [last]
            for k, part in enumerate(parts):
                r = face_rows(ends, axis, way, k)
                ref[r] = ref[r] + (part * ends[2][axis] if way else part)


def ends_of(columns):
    column = lax.rem(lax.axis_index("elem") + columns // 2, columns * DA)
    row, place = lax.div(column, columns), lax.rem(column, columns)
    row_odd, place_odd = lax.rem(row, 2), lax.rem(place, 2)
    row_inside = jnp.where((row > 0) & (row < DA - 1), 1.0, 0.0)
    place_inside = jnp.where((place > 0) & (place < columns - 1), 1.0, 0.0)
    return (
        (7 - 7 * row_odd, 7 * row_odd),
        (7 - 7 * place_odd, 7 * place_odd),
        (row_inside, place_inside),
    )


def index_of(index_ref):
    return tuple(index_ref[n] for n in range(4))


def index_kernel(
    columns,
    moment_far,
    state_far,
    flow_far,
    weight_far,
    diff_far,
    numbers_far,
    moment_ref,
    state_ref,
    carry_ref,
    weigh_ref,
    table_ref,
    turned_ref,
    index_ref,
    joined_ref,
    ie_ref,
    io_ref,
    je_ref,
    jo_ref,
    weight_ref,
    mass_ref,
    flow_ref,
    numbers_ref,
    diff_ref,
    arrived,
):
    far = (numbers_far, weight_far, state_far, diff_far, moment_far, flow_far)
    near = (numbers_ref, weight_ref, state_ref, diff_ref, moment_ref, flow_ref)
    copies = [pltpu.make_async_copy(a, b, arrived.at[n]) for n, (a, b) in enumerate(zip(far, near))]
    for copy in copies:
        copy.start()
    write_table(DM, table_ref)
    write_table(DM.T, turned_ref)
    ends = ends_of(columns)
    copies[0].wait()
    height = jnp.broadcast_to(numbers_ref[...] & 127, (8, 128))
    square = jnp.broadcast_to(height[:1].astype(F32), (128, 128)).T
    lane = lax.broadcasted_iota(jnp.int32, (128, 128), 1).astype(F32)
    row = lax.broadcasted_iota(jnp.int32, (128, 128), 0).astype(F32)
    inverse = jnp.sum(jnp.where(square == lane, row, 0.0), axis=0, keepdims=True)
    inverse = jnp.broadcast_to(inverse, (8, 128)).astype(jnp.int32)
    index = (
        height,
        inverse,
        lanes(inverse, (height - 1) & 127),
        lanes(inverse, (height + 1) & 127),
    )
    for n in range(4):
        index_ref[n] = index[n]
    copies[1].wait()
    set_mass(weight_ref, mass_ref)
    joined_ref[3] = mass_ref[...]
    copies[2].wait()
    out = (ie_ref, io_ref, je_ref, jo_ref)
    for c in range(3):
        joined_ref[c] = state_ref[c]
    for c in range(4):
        join_heights(joined_ref.at[c], index)
        send_faces(c, joined_ref.at[c], index, ends, out)
    copies[3].wait()
    for f in range(3):
        weigh_ref[f] = mass_ref[...] * (DT * diff_ref[f])
    copies[5].wait()
    for d in range(3):
        carry_ref[d] = mass_ref[...] * (DT * flow_ref[d])
    copies[4].wait()


def moment_kernel(
    columns,
    moment_ref,
    carry_ref,
    weigh_ref,
    table_ref,
    turned_ref,
    index_ref,
    joined_ref,
    ie_ref,
    io_ref,
    je_ref,
    jo_ref,
    slope_ref,
    work_ref,
):
    ends = ends_of(columns)
    index = index_of(index_ref)
    out = (ie_ref, io_ref, je_ref, jo_ref)

    def finish(f):
        join_heights(joined_ref.at[f], index)
        send_faces(f, joined_ref.at[f], index, ends, out)

    at = (carry_ref, weigh_ref, table_ref, turned_ref, slope_ref, work_ref)
    forward(moment_ref, *at, joined_ref, finish)


def edge_kernel(columns, way, ie_ref, io_ref, face, *refs):
    ends, out = ends_of(columns), refs[-1]
    out[...] = face[...]
    tiles = face.shape[0] // 8
    r = pl.ds(ends[1][way], tiles, stride=8)
    for other, got in enumerate((ie_ref, io_ref)):
        w = pl.ds(ends[0][other], tiles, stride=8)
        part = got[r]
        out[w] = out[w] + (part * ends[2][0] if other else part)


def state_kernel(
    columns,
    first,
    state_ref,
    carry_ref,
    weigh_ref,
    table_ref,
    turned_ref,
    index_ref,
    joined_ref,
    *refs,
):
    ends = ends_of(columns)
    index = index_of(index_ref)
    if first:
        got, (inverse_ref, state_out, joined_out), refs = refs[:4], refs[4:7], refs[7:]
        out, (slope_ref, work_ref, hold_ref) = refs[:4], refs[4:]
        held = hold_ref.at[0]
        held[...] = joined_ref[3]
        add_faces(3, held, index, ends, got)
        inverse_ref[...] = 1.0 / held[...]
    else:
        inverse_ref, *got = refs[:5]
        state_far, token_ref, slope_ref, work_ref, hold_ref, state_out, sent = refs[5:]
        token_ref[...] = jnp.zeros_like(token_ref)
    for f in range(3):
        held = hold_ref.at[f]
        held[...] = joined_ref[f]
        add_faces(f, held, index, ends, got)
        held[...] = held[...] * inverse_ref[...]

    def finish(f):
        if first:
            joined_out[f] = state_out[f]
            join_heights(joined_out.at[f], index)
            send_faces(f, joined_out.at[f], index, ends, out)
        else:
            send_out(f, state_out, state_far, sent).start()

    at = (carry_ref, weigh_ref, table_ref, turned_ref, slope_ref, work_ref)
    adjoint(hold_ref, state_ref, *at, state_out, finish)
    if not first:
        for f in range(3):
            send_out(f, state_out, state_far, sent).wait()


def send_out(f, near, far, sent):
    return pltpu.make_async_copy(near.at[f], far.at[f], sent.at[f])


def moment_step(f, ends, index, moment_ref, joined_ref, inverse_ref, got, hold_ref, moment_out):
    held = hold_ref.at[f]
    held[...] = joined_ref[f]
    add_faces(f, held, index, ends, got)
    moment_out[f] = moment_ref[f] - held[...] * inverse_ref[...]


def middle_kernel(
    columns,
    moment_ref,
    carry_ref,
    weigh_ref,
    table_ref,
    turned_ref,
    index_ref,
    inverse_ref,
    joined_ref,
    gie_ref,
    gio_ref,
    gjo_ref,
    gje_ref,
    moment_out,
    joined_out,
    ie_ref,
    io_ref,
    je_ref,
    jo_ref,
    slope_ref,
    work_ref,
    hold_ref,
):
    ends = ends_of(columns)
    index = index_of(index_ref)
    out = (ie_ref, io_ref, je_ref, jo_ref)
    got = (gie_ref, gio_ref, gjo_ref, gje_ref)
    for f in range(3):
        moment_step(f, ends, index, moment_ref, joined_ref, inverse_ref, got, hold_ref, moment_out)

    def finish(f):
        join_heights(joined_out.at[f], index)
        send_faces(f, joined_out.at[f], index, ends, out)

    at = (carry_ref, weigh_ref, table_ref, turned_ref, slope_ref, work_ref)
    forward(moment_out, *at, joined_out, finish)


def last_kernel(
    columns,
    moment_ref,
    index_ref,
    inverse_ref,
    joined_ref,
    gie_ref,
    gio_ref,
    gjo_ref,
    gje_ref,
    moment_far,
    hold_ref,
    moment_out,
    sent,
):
    ends = ends_of(columns)
    index = index_of(index_ref)
    got = (gie_ref, gio_ref, gjo_ref, gje_ref)

    for f in range(3):
        moment_step(f, ends, index, moment_ref, joined_ref, inverse_ref, got, hold_ref, moment_out)
        send_out(f, moment_out, moment_far, sent).start()
    for f in range(3):
        send_out(f, moment_out, moment_far, sent).wait()


VMEM = pl.BlockSpec(memory_space=pltpu.VMEM)
FAR = pl.BlockSpec(memory_space=pltpu.HBM)


def call(kernel, specs, shapes, scratch, flops, *operands, first_out=VMEM):
    moved = sum(o.size * 4 for o in operands) + sum(int(np.prod(s)) * 4 for s, _ in shapes)
    return pl.pallas_call(
        kernel,
        out_shape=[jax.ShapeDtypeStruct(s, t) for s, t in shapes],
        in_specs=specs,
        out_specs=[first_out] + [VMEM] * (len(shapes) - 1),
        scratch_shapes=scratch,
        compiler_params=pltpu.CompilerParams(vmem_limit_bytes=32 * 1024 * 1024),
        cost_estimate=pl.CostEstimate(flops=flops, bytes_accessed=moved, transcendentals=0),
    )(*operands)


def pairings(devices):
    columns = devices // DA
    device = lambda row, place: (row % DA * columns + place - columns // 2) % devices

    def both(pairs):
        return pairs + [(b, a) for a, b in pairs]

    places, halves = range(columns), range(0, columns, 2)
    along_i = [
        [(device(r, s), device(r + 1, s)) for r in range(0, DA, 2) for s in places],
        [(device(r, s), device(r + 1, s)) for r in range(1, DA - 1, 2) for s in places]
        + [(device(r, s), device(r, s + 1)) for r in (0, DA - 1) for s in halves],
    ]
    along_j = [
        [(device(r, s), device(r, s + 1)) for r in range(DA) for s in halves],
        [(device(r, s - 1), device(r, s)) for r in range(DA) for s in halves if s]
        + [(device(r, columns - 1), device(r + 1, 0)) for r in range(DA)],
    ]
    return [both(p) for p in along_i], [both(p) for p in along_j]


def shards(moment_fields, adjoint_fields, velocity, mass_weights, diffusivity, numbering):
    devices = lax.axis_size("elem")
    columns = devices // DA
    along_i, along_j = pairings(devices)
    whole, block = ((3, 512, 128), F32), ((512, 128), F32)
    work = pltpu.VMEM((3, 512, 128), F32)

    def exchange(block, pairs):
        return lax.ppermute(block, "elem", pairs)

    def settle(block, *after):
        anywhere = pl.BlockSpec(memory_space=pl.ANY)
        return pl.pallas_call(
            lambda *refs: None,
            out_shape=jax.ShapeDtypeStruct(block.shape, block.dtype),
            in_specs=[anywhere] * (1 + len(after)),
            out_specs=anywhere,
            input_output_aliases={0: 0},
            compiler_params=pltpu.CompilerParams(vmem_limit_bytes=1024 * 1024),
        )(block, *after)

    def edge(count, way, *operands):
        return call(
            functools.partial(edge_kernel, columns, way),
            [VMEM] * len(operands),
            [(face_shape(count), F32)],
            [],
            count * 64 * 128,
            *operands,
        )[0]

    def meet(count, faces):
        got_i = [exchange(faces[way], along_i[way]) for way in range(2)]
        far_face = edge(count, 1, *got_i, faces[3])
        near_face = edge(count, 0, *got_i, faces[2], far_face)
        return got_i + [exchange(far_face, along_j[1]), exchange(near_face, along_j[0])]

    def settled(got, *after):
        return got[:2] + [settle(got[2], *after), got[3]]

    def far(array):
        return pltpu.with_memory_space_constraint(array, pltpu.HBM)

    def face_shape(count):
        return ((7 * count + 1) * 8, 128)

    def faces_shape(count):
        return [(face_shape(count), F32)] * 4

    moment, state, carry, weigh, table, turned, index, joined_state, *faces_state = call(
        functools.partial(index_kernel, columns),
        [FAR] * 6,
        [whole] * 4
        + [((256, 768), BF16)] * 2
        + [((4, 8, 128), jnp.int32), ((4, 512, 128), F32)]
        + faces_shape(4),
        [
            pltpu.VMEM((512, 128), F32),
            pltpu.VMEM((512, 128), F32),
            work,
            pltpu.VMEM((1, 128), jnp.int32),
            pltpu.SMEM((3,), F32),
            pltpu.SemaphoreType.DMA((6,)),
        ],
        1_000_000,
        *map(far, (moment_fields, adjoint_fields, velocity, mass_weights)),
        *map(far, (diffusivity, numbering.reshape(1, 128))),
    )
    tables = (carry, weigh, table, turned, index)
    got_state = meet(4, faces_state)
    joined_moment, *faces_moment = call(
        functools.partial(moment_kernel, columns),
        [VMEM] * 6,
        [whole] + faces_shape(3),
        [work] * 2,
        20_000_000,
        moment,
        *tables,
    )
    got_moment = meet(3, faces_moment)
    inverse, state, joined_state, *faces_state = call(
        functools.partial(state_kernel, columns, True),
        [VMEM] * 11,
        [block, whole, whole] + faces_shape(3),
        [work] * 3,
        20_000_000,
        state,
        *tables,
        joined_state,
        *settled(got_state),
    )
    got_state = meet(3, faces_state)
    moment, joined_moment, *faces_moment = call(
        functools.partial(middle_kernel, columns),
        [VMEM] * 12,
        [whole, whole] + faces_shape(3),
        [work] * 3,
        20_000_000,
        moment,
        *tables,
        inverse,
        joined_moment,
        *settled(got_moment, inverse),
    )
    got_moment = meet(3, faces_moment)
    state, token = call(
        functools.partial(state_kernel, columns, False),
        [VMEM] * 12,
        [whole, ((8, 128), F32)],
        [work] * 4 + [pltpu.SemaphoreType.DMA((3,))],
        20_000_000,
        state,
        *tables,
        joined_state,
        inverse,
        *settled(got_state),
        first_out=FAR,
    )
    (moment,) = call(
        functools.partial(last_kernel, columns),
        [VMEM] * 8,
        [whole],
        [work] * 2 + [pltpu.SemaphoreType.DMA((3,))],
        1_000_000,
        moment,
        index,
        inverse,
        joined_moment,
        *settled(got_moment, token),
        first_out=FAR,
    )
    return moment, state


def solution(mesh):
    in_specs = (
        P(None, None, "elem"),
        P(None, None, "elem"),
        P(None, None, "elem"),
        P(None, "elem"),
        P(),
        P("elem"),
    )
    out_specs = (P(None, None, "elem"), P(None, None, "elem"))
    return jax.shard_map(shards, mesh=mesh, in_specs=in_specs, out_specs=out_specs, check_vma=False)
```

```python
import functools

import jax
import jax.numpy as jnp
import numpy as np
from jax import lax
from jax.experimental import pallas as pl
from jax.experimental.pallas import tpu as pltpu
from jax.sharding import PartitionSpec as P

DA = 4
DT = 0.001
F32 = jnp.float32
BF16 = jnp.bfloat16


def gll_tables():
    points = [
        -1.0,
        -0.8717401485096066,
        -0.5917001814331423,
        -0.2092992179024789,
        0.2092992179024789,
        0.5917001814331423,
        0.8717401485096066,
        1.0,
    ]
    weights = [
        0.03571428571428571,
        0.21070422714350603,
        0.3411226924835044,
        0.4124587946587038,
        0.4124587946587038,
        0.3411226924835044,
        0.21070422714350603,
        0.03571428571428571,
    ]
    barycentric = []
    for left_index in range(8):
        product = 1.0
        for right_index in range(8):
            if right_index != left_index:
                product = product * (points[left_index] - points[right_index])
        barycentric.append(1.0 / product)
    derivative = np.zeros((8, 8))
    for left_index in range(8):
        row_total = 0.0
        for right_index in range(8):
            if left_index != right_index:
                entry = (
                    barycentric[right_index]
                    / barycentric[left_index]
                    / (points[left_index] - points[right_index])
                )
                derivative[left_index, right_index] = entry
                row_total = row_total + entry
        derivative[left_index, left_index] = -row_total
    return derivative, np.asarray(weights)


DM, WEIGHTS = gll_tables()


def line(table, values):
    sums = [values[q] + values[7 - q] for q in range(4)]
    differences = [values[q] - values[7 - q] for q in range(4)]
    out = [None] * 8
    for i in range(4):
        even = odd = None
        for q in range(4):
            on_sum = float(table[i, q] + table[i, 7 - q]) / 2
            on_difference = float(table[i, q] - table[i, 7 - q]) / 2
            even = sums[q] * on_sum if even is None else even + sums[q] * on_sum
            odd = (
                differences[q] * on_difference
                if odd is None
                else odd + differences[q] * on_difference
            )
        out[i] = odd + even
        out[7 - i] = odd - even
    return out


def rows(i, j):
    return pl.ds((8 * i + j) * 8, 8)


def along_k(table_ref, block):
    wide = jnp.concatenate([block[:256], block[256:]], axis=1)
    high = wide.astype(BF16)
    low = (wide - high.astype(F32)).astype(BF16)
    parts = jnp.concatenate([high, high, low], axis=0)
    out = jnp.dot(table_ref[...], parts, preferred_element_type=F32)
    return jnp.concatenate([out[:, :128], out[:, 128:]], axis=0)


def write_table(table, table_ref):
    sub = lax.broadcasted_iota(jnp.int32, (8, 128), 0)
    lane = lax.broadcasted_iota(jnp.int32, (8, 128), 1)
    base = jnp.zeros((8, 128), F32)
    for i in range(8):
        one_row = jnp.zeros((8, 128), F32)
        for q in range(8):
            one_row = jnp.where((lane & 7) == q, float(table[i, q]), one_row)
        base = jnp.where(sub == i, one_row, base)
    high = base.astype(BF16).astype(F32)
    block = lax.shift_right_logical(lane, 3)
    zero = jnp.zeros((8, 128), F32)
    empty = jnp.zeros((16, 128), F32)
    for a in range(0, 32, 2):
        parts = []
        for values in (high, base - high):
            pair = [jnp.where(block == (a + n) % 16, values, zero) for n in range(2)]
            pair = jnp.concatenate(pair, axis=0)
            parts.append([pair, empty] if a < 16 else [empty, pair])
        wide = jnp.concatenate(parts[0] + parts[1] + parts[0], axis=1)
        table_ref[pl.ds(8 * a, 16)] = wide.astype(BF16)


def lanes(block, index):
    wide = jnp.broadcast_to(index[None], (block.shape[0] // 8, 8, 128)).reshape(block.shape)
    return jnp.take_along_axis(block, wide, axis=1, mode="promise_in_bounds")


def set_mass(weight_ref, mass_ref):
    sub = lax.broadcasted_iota(jnp.int32, (8, 128), 0)
    along = jnp.zeros((8, 128), F32)
    for k in range(8):
        along = jnp.where(sub == k, float(WEIGHTS[k]), along)
    for i in range(8):
        for j in range(8):
            r = rows(i, j)
            mass_ref[r] = weight_ref[r] * (along * float(WEIGHTS[i] * WEIGHTS[j]))


def slope_k(source, table_ref, slope):
    slope[...] = along_k(table_ref, source[...])


def forward_k(carry_ref, weigh, turned_ref, slope, work):
    work[...] = carry_ref[2] * slope[...] + along_k(turned_ref, weigh[...] * slope[...])


def adjoint_k(source, carry_ref, weigh, turned_ref, slope, work):
    work[...] = along_k(turned_ref, carry_ref[2] * source[...] + weigh[...] * slope[...])


def forward_i(source, carry_ref, weigh, target):
    for j in range(8):
        slopes = line(DM, [source[rows(i, j)] for i in range(8)])
        back = line(DM.T, [weigh[rows(i, j)] * slopes[i] for i in range(8)])
        for i in range(8):
            r = rows(i, j)
            target[r] = carry_ref[0, r] * slopes[i] + back[i]


def forward_j(source, carry_ref, weigh, work, target):
    for i in range(8):
        slopes = line(DM, [source[rows(i, j)] for j in range(8)])
        back = line(DM.T, [weigh[rows(i, j)] * slopes[j] for j in range(8)])
        for j in range(8):
            r = rows(i, j)
            target[r] = target[r] + (carry_ref[1, r] * slopes[j] + (back[j] + work[r]))


def adjoint_lines(d, source, carry_ref, weigh, line_rows):
    for these in line_rows:
        values = [source[r] for r in these]
        slopes = line(DM, values)
        fluxes = [carry_ref[d, r] * v + weigh[r] * g for r, v, g in zip(these, values, slopes)]
        yield from zip(these, line(DM.T, fluxes))


def adjoint_i(source, base, carry_ref, weigh, target):
    lines = [[rows(i, j) for i in range(8)] for j in range(8)]
    for r, back in adjoint_lines(0, source, carry_ref, weigh, lines):
        target[r] = base[r] - back


def adjoint_j(source, carry_ref, weigh, work, target):
    lines = [[rows(i, j) for j in range(8)] for i in range(8)]
    for r, back in adjoint_lines(1, source, carry_ref, weigh, lines):
        target[r] = target[r] - (back + work[r])


def forward(sources, carry_ref, weigh_ref, table_ref, turned_ref, slope_ref, work_ref, target, finish):
    slope_k(sources.at[0], table_ref, slope_ref.at[0])
    for f in range(3):
        at = (carry_ref, weigh_ref.at[f])
        forward_i(sources.at[f], *at, target.at[f])
        forward_k(*at, turned_ref, slope_ref.at[f], work_ref.at[f])
        if f < 2:
            slope_k(sources.at[f + 1], table_ref, slope_ref.at[f + 1])
        forward_j(sources.at[f], *at, work_ref.at[f], target.at[f])
        finish(f)


def adjoint(
    sources, base, carry_ref, weigh_ref, table_ref, turned_ref, slope_ref, work_ref, target, finish
):
    slope_k(sources.at[0], table_ref, slope_ref.at[0])
    for f in range(3):
        at = (carry_ref, weigh_ref.at[f])
        adjoint_i(sources.at[f], base.at[f], *at, target.at[f])
        adjoint_k(sources.at[f], *at, turned_ref, slope_ref.at[f], work_ref.at[f])
        if f < 2:
            slope_k(sources.at[f + 1], table_ref, slope_ref.at[f + 1])
        adjoint_j(sources.at[f], *at, work_ref.at[f], target.at[f])
        finish(f)


def join_heights(ref, index):
    height, _, below, above = index
    lower = ref[pl.ds(0, 64, stride=8)]
    upper = ref[pl.ds(7, 64, stride=8)]
    tall = jnp.broadcast_to(height[None], (8, 8, 128)).reshape(64, 128)
    ref[pl.ds(0, 64, stride=8)] = lower + jnp.where(tall > 0, lanes(upper, below), 0.0)
    ref[pl.ds(7, 64, stride=8)] = upper + jnp.where(tall < 127, lanes(lower, above), 0.0)


def face_rows(ends, axis, way, k):
    end = ends[axis][way]
    return pl.ds(end * 8 + k, 8, stride=64) if axis else pl.ds(end * 64 + k, 8, stride=8)


def tile(c, k):
    return pl.ds((7 * c + k) * 8, 8)


def top_tile(ref):
    return pl.ds(ref.shape[0] - 8, 8)


def send_faces(c, ref, index, ends, out):
    inverse = index[1]
    top = jnp.broadcast_to(inverse[:, 127:], (8, 128))
    lane = lax.broadcasted_iota(jnp.int32, (8, 128), 1)
    for axis in range(2):
        for way in range(2):
            face = out[2 * axis + way]
            for k in range(7):
                face[tile(c, k)] = lanes(ref[face_rows(ends, axis, way, k)], inverse)
            last = lanes(ref[face_rows(ends, axis, way, 7)], top)
            others = face[top_tile(face)] if c else jnp.zeros((8, 128), F32)
            face[top_tile(face)] = jnp.where(lane == c, last, others)


def take_faces(c, index, ends, got, spread_ref):
    height = index[0]
    above = (height + 1) & 127
    own = jnp.full((8, 128), c, jnp.int32)
    for axis in range(2):
        for way in range(2):
            face = got[3 - way if axis else way]
            last = jnp.where(
                height < 127, lanes(face[tile(c, 0)], above), lanes(face[top_tile(face)], own)
            )
            parts = [lanes(face[tile(c, k)], height) for k in range(7)] + [last]
            slot = 2 * axis + jnp.minimum(ends[axis][way], 1)
            for k, part in enumerate(parts):
                spread_ref[c, slot, pl.ds(8 * k, 8)] = part * ends[2][axis] if way else part


def assembled(c, i, j, joined, spread_ref):
    total = joined[rows(i, j)]
    for axis, (end, place) in enumerate(((i, j), (j, i))):
        if end in (0, 7):
            total = total + spread_ref[c, 2 * axis + end // 7, pl.ds(place, 8, stride=8)]
    return total


def ends_of(columns):
    column = lax.rem(lax.axis_index("elem") + columns // 2, columns * DA)
    row, place = lax.div(column, columns), lax.rem(column, columns)
    row_odd, place_odd = lax.rem(row, 2), lax.rem(place, 2)
    row_inside = jnp.where((row > 0) & (row < DA - 1), 1.0, 0.0)
    place_inside = jnp.where((place > 0) & (place < columns - 1), 1.0, 0.0)
    return (
        (7 - 7 * row_odd, 7 * row_odd),
        (7 - 7 * place_odd, 7 * place_odd),
        (row_inside, place_inside),
    )


def index_of(index_ref):
    return tuple(index_ref[n] for n in range(4))


def index_kernel(
    columns,
    moment_far,
    state_far,
    flow_far,
    weight_far,
    diff_far,
    numbers_far,
    moment_ref,
    state_ref,
    carry_ref,
    weigh_ref,
    table_ref,
    turned_ref,
    index_ref,
    joined_ref,
    ie_ref,
    io_ref,
    je_ref,
    jo_ref,
    weight_ref,
    mass_ref,
    flow_ref,
    numbers_ref,
    diff_ref,
    arrived,
):
    far = (numbers_far, weight_far, state_far, diff_far, moment_far, flow_far)
    near = (numbers_ref, weight_ref, state_ref, diff_ref, moment_ref, flow_ref)
    copies = [pltpu.make_async_copy(a, b, arrived.at[n]) for n, (a, b) in enumerate(zip(far, near))]
    for copy in copies:
        copy.start()
    write_table(DM, table_ref)
    write_table(DM.T, turned_ref)
    ends = ends_of(columns)
    copies[0].wait()
    height = jnp.broadcast_to(numbers_ref[...] & 127, (8, 128))
    square = jnp.broadcast_to(height[:1].astype(F32), (128, 128)).T
    lane = lax.broadcasted_iota(jnp.int32, (128, 128), 1).astype(F32)
    row = lax.broadcasted_iota(jnp.int32, (128, 128), 0).astype(F32)
    inverse = jnp.sum(jnp.where(square == lane, row, 0.0), axis=0, keepdims=True)
    inverse = jnp.broadcast_to(inverse, (8, 128)).astype(jnp.int32)
    index = (
        height,
        inverse,
        lanes(inverse, (height - 1) & 127),
        lanes(inverse, (height + 1) & 127),
    )
    for n in range(4):
        index_ref[n] = index[n]
    copies[1].wait()
    set_mass(weight_ref, mass_ref)
    joined_ref[3] = mass_ref[...]
    copies[2].wait()
    out = (ie_ref, io_ref, je_ref, jo_ref)
    for c in range(3):
        joined_ref[c] = state_ref[c]
    for c in range(4):
        join_heights(joined_ref.at[c], index)
        send_faces(c, joined_ref.at[c], index, ends, out)
    copies[3].wait()
    for f in range(3):
        weigh_ref[f] = mass_ref[...] * (DT * diff_ref[f])
    copies[5].wait()
    for d in range(3):
        carry_ref[d] = mass_ref[...] * (DT * flow_ref[d])
    copies[4].wait()


def moment_kernel(
    columns,
    moment_ref,
    carry_ref,
    weigh_ref,
    table_ref,
    turned_ref,
    index_ref,
    joined_ref,
    ie_ref,
    io_ref,
    je_ref,
    jo_ref,
    slope_ref,
    work_ref,
):
    ends = ends_of(columns)
    index = index_of(index_ref)
    out = (ie_ref, io_ref, je_ref, jo_ref)

    def finish(f):
        join_heights(joined_ref.at[f], index)
        send_faces(f, joined_ref.at[f], index, ends, out)

    at = (carry_ref, weigh_ref, table_ref, turned_ref, slope_ref, work_ref)
    forward(moment_ref, *at, joined_ref, finish)


def edge_kernel(columns, way, ie_ref, io_ref, face, *refs):
    ends, out = ends_of(columns), refs[-1]
    out[...] = face[...]
    tiles = face.shape[0] // 8
    r = pl.ds(ends[1][way], tiles, stride=8)
    for other, got in enumerate((ie_ref, io_ref)):
        w = pl.ds(ends[0][other], tiles, stride=8)
        part = got[r]
        out[w] = out[w] + (part * ends[2][0] if other else part)


def state_kernel(
    columns,
    first,
    state_ref,
    carry_ref,
    weigh_ref,
    table_ref,
    turned_ref,
    index_ref,
    joined_ref,
    *refs,
):
    ends = ends_of(columns)
    index = index_of(index_ref)
    if first:
        got, (inverse_ref, state_out, joined_out), refs = refs[:4], refs[4:7], refs[7:]
        out, (slope_ref, work_ref, hold_ref, spread_ref) = refs[:4], refs[4:]
        take_faces(3, index, ends, got, spread_ref)
        for i in range(8):
            for j in range(8):
                inverse_ref[rows(i, j)] = 1.0 / assembled(3, i, j, joined_ref.at[3], spread_ref)
    else:
        inverse_ref, *got = refs[:5]
        state_far, token_ref, slope_ref, work_ref, hold_ref, spread_ref, state_out, sent = refs[5:]
        token_ref[...] = jnp.zeros_like(token_ref)
    for f in range(3):
        take_faces(f, index, ends, got, spread_ref)
        for i in range(8):
            for j in range(8):
                total = assembled(f, i, j, joined_ref.at[f], spread_ref)
                hold_ref[f, rows(i, j)] = total * inverse_ref[rows(i, j)]

    def finish(f):
        if first:
            joined_out[f] = state_out[f]
            join_heights(joined_out.at[f], index)
            send_faces(f, joined_out.at[f], index, ends, out)
        else:
            send_out(f, state_out, state_far, sent).start()

    at = (carry_ref, weigh_ref, table_ref, turned_ref, slope_ref, work_ref)
    adjoint(hold_ref, state_ref, *at, state_out, finish)
    if not first:
        for f in range(3):
            send_out(f, state_out, state_far, sent).wait()


def send_out(f, near, far, sent):
    return pltpu.make_async_copy(near.at[f], far.at[f], sent.at[f])


def moment_step(f, ends, index, moment_ref, joined_ref, inverse_ref, got, spread_ref, moment_out):
    take_faces(f, index, ends, got, spread_ref)
    for i in range(8):
        for j in range(8):
            r = rows(i, j)
            total = assembled(f, i, j, joined_ref.at[f], spread_ref)
            moment_out[f, r] = moment_ref[f, r] - total * inverse_ref[r]


def middle_kernel(
    columns,
    moment_ref,
    carry_ref,
    weigh_ref,
    table_ref,
    turned_ref,
    index_ref,
    inverse_ref,
    joined_ref,
    gie_ref,
    gio_ref,
    gjo_ref,
    gje_ref,
    moment_out,
    joined_out,
    ie_ref,
    io_ref,
    je_ref,
    jo_ref,
    slope_ref,
    work_ref,
    spread_ref,
):
    ends = ends_of(columns)
    index = index_of(index_ref)
    out = (ie_ref, io_ref, je_ref, jo_ref)
    got = (gie_ref, gio_ref, gjo_ref, gje_ref)
    for f in range(3):
        moment_step(f, ends, index, moment_ref, joined_ref, inverse_ref, got, spread_ref, moment_out)

    def finish(f):
        join_heights(joined_out.at[f], index)
        send_faces(f, joined_out.at[f], index, ends, out)

    at = (carry_ref, weigh_ref, table_ref, turned_ref, slope_ref, work_ref)
    forward(moment_out, *at, joined_out, finish)


def last_kernel(
    columns,
    moment_ref,
    index_ref,
    inverse_ref,
    joined_ref,
    gie_ref,
    gio_ref,
    gjo_ref,
    gje_ref,
    moment_far,
    spread_ref,
    moment_out,
    sent,
):
    ends = ends_of(columns)
    index = index_of(index_ref)
    got = (gie_ref, gio_ref, gjo_ref, gje_ref)

    for f in range(3):
        moment_step(f, ends, index, moment_ref, joined_ref, inverse_ref, got, spread_ref, moment_out)
        send_out(f, moment_out, moment_far, sent).start()
    for f in range(3):
        send_out(f, moment_out, moment_far, sent).wait()


VMEM = pl.BlockSpec(memory_space=pltpu.VMEM)
FAR = pl.BlockSpec(memory_space=pltpu.HBM)


def call(kernel, specs, shapes, scratch, flops, *operands, first_out=VMEM):
    moved = sum(o.size * 4 for o in operands) + sum(int(np.prod(s)) * 4 for s, _ in shapes)
    return pl.pallas_call(
        kernel,
        out_shape=[jax.ShapeDtypeStruct(s, t) for s, t in shapes],
        in_specs=specs,
        out_specs=[first_out] + [VMEM] * (len(shapes) - 1),
        scratch_shapes=scratch,
        compiler_params=pltpu.CompilerParams(vmem_limit_bytes=32 * 1024 * 1024),
        cost_estimate=pl.CostEstimate(flops=flops, bytes_accessed=moved, transcendentals=0),
    )(*operands)


def pairings(devices):
    columns = devices // DA
    device = lambda row, place: (row % DA * columns + place - columns // 2) % devices

    def both(pairs):
        return pairs + [(b, a) for a, b in pairs]

    places, halves = range(columns), range(0, columns, 2)
    along_i = [
        [(device(r, s), device(r + 1, s)) for r in range(0, DA, 2) for s in places],
        [(device(r, s), device(r + 1, s)) for r in range(1, DA - 1, 2) for s in places]
        + [(device(r, s), device(r, s + 1)) for r in (0, DA - 1) for s in halves],
    ]
    along_j = [
        [(device(r, s), device(r, s + 1)) for r in range(DA) for s in halves],
        [(device(r, s - 1), device(r, s)) for r in range(DA) for s in halves if s]
        + [(device(r, columns - 1), device(r + 1, 0)) for r in range(DA)],
    ]
    return [both(p) for p in along_i], [both(p) for p in along_j]


def shards(moment_fields, adjoint_fields, velocity, mass_weights, diffusivity, numbering):
    devices = lax.axis_size("elem")
    columns = devices // DA
    along_i, along_j = pairings(devices)
    whole, block = ((3, 512, 128), F32), ((512, 128), F32)
    work = pltpu.VMEM((3, 512, 128), F32)

    def spread(count):
        return pltpu.VMEM((count, 4, 64, 128), F32)

    def exchange(block, pairs):
        return lax.ppermute(block, "elem", pairs)

    def settle(block, *after):
        anywhere = pl.BlockSpec(memory_space=pl.ANY)
        return pl.pallas_call(
            lambda *refs: None,
            out_shape=jax.ShapeDtypeStruct(block.shape, block.dtype),
            in_specs=[anywhere] * (1 + len(after)),
            out_specs=anywhere,
            input_output_aliases={0: 0},
            compiler_params=pltpu.CompilerParams(vmem_limit_bytes=1024 * 1024),
        )(block, *after)

    def edge(count, way, *operands):
        return call(
            functools.partial(edge_kernel, columns, way),
            [VMEM] * len(operands),
            [(face_shape(count), F32)],
            [],
            count * 64 * 128,
            *operands,
        )[0]

    def meet(count, faces):
        got_i = [exchange(faces[way], along_i[way]) for way in range(2)]
        far_face = edge(count, 1, *got_i, faces[3])
        near_face = edge(count, 0, *got_i, faces[2], far_face)
        return got_i + [exchange(far_face, along_j[1]), exchange(near_face, along_j[0])]

    def settled(got, *after):
        return got[:2] + [settle(got[2], *after), got[3]]

    def far(array):
        return pltpu.with_memory_space_constraint(array, pltpu.HBM)

    def face_shape(count):
        return ((7 * count + 1) * 8, 128)

    def faces_shape(count):
        return [(face_shape(count), F32)] * 4

    moment, state, carry, weigh, table, turned, index, joined_state, *faces_state = call(
        functools.partial(index_kernel, columns),
        [FAR] * 6,
        [whole] * 4
        + [((256, 768), BF16)] * 2
        + [((4, 8, 128), jnp.int32), ((4, 512, 128), F32)]
        + faces_shape(4),
        [
            pltpu.VMEM((512, 128), F32),
            pltpu.VMEM((512, 128), F32),
            work,
            pltpu.VMEM((1, 128), jnp.int32),
            pltpu.SMEM((3,), F32),
            pltpu.SemaphoreType.DMA((6,)),
        ],
        1_000_000,
        *map(far, (moment_fields, adjoint_fields, velocity, mass_weights)),
        *map(far, (diffusivity, numbering.reshape(1, 128))),
    )
    tables = (carry, weigh, table, turned, index)
    got_state = meet(4, faces_state)
    joined_moment, *faces_moment = call(
        functools.partial(moment_kernel, columns),
        [VMEM] * 6,
        [whole] + faces_shape(3),
        [work] * 2,
        20_000_000,
        moment,
        *tables,
    )
    got_moment = meet(3, faces_moment)
    inverse, state, joined_state, *faces_state = call(
        functools.partial(state_kernel, columns, True),
        [VMEM] * 11,
        [block, whole, whole] + faces_shape(3),
        [work] * 3 + [spread(4)],
        20_000_000,
        state,
        *tables,
        joined_state,
        *settled(got_state),
    )
    got_state = meet(3, faces_state)
    moment, joined_moment, *faces_moment = call(
        functools.partial(middle_kernel, columns),
        [VMEM] * 12,
        [whole, whole] + faces_shape(3),
        [work] * 2 + [spread(3)],
        20_000_000,
        moment,
        *tables,
        inverse,
        joined_moment,
        *settled(got_moment, inverse),
    )
    got_moment = meet(3, faces_moment)
    state, token = call(
        functools.partial(state_kernel, columns, False),
        [VMEM] * 12,
        [whole, ((8, 128), F32)],
        [work] * 3 + [spread(3), work] + [pltpu.SemaphoreType.DMA((3,))],
        20_000_000,
        state,
        *tables,
        joined_state,
        inverse,
        *settled(got_state),
        first_out=FAR,
    )
    (moment,) = call(
        functools.partial(last_kernel, columns),
        [VMEM] * 8,
        [whole],
        [spread(3), work] + [pltpu.SemaphoreType.DMA((3,))],
        1_000_000,
        moment,
        index,
        inverse,
        joined_moment,
        *settled(got_moment, token),
        first_out=FAR,
    )
    return moment, state


def solution(mesh):
    in_specs = (
        P(None, None, "elem"),
        P(None, None, "elem"),
        P(None, None, "elem"),
        P(None, "elem"),
        P(),
        P("elem"),
    )
    out_specs = (P(None, None, "elem"), P(None, None, "elem"))
    return jax.shard_map(shards, mesh=mesh, in_specs=in_specs, out_specs=out_specs, check_vma=False)
```

```python
import functools

import jax
import jax.numpy as jnp
import numpy as np
from jax import lax
from jax.experimental import pallas as pl
from jax.experimental.pallas import tpu as pltpu
from jax.sharding import PartitionSpec as P

DA = 4
DT = 0.001
F32 = jnp.float32
BF16 = jnp.bfloat16


def gll_tables():
    points = [
        -1.0,
        -0.8717401485096066,
        -0.5917001814331423,
        -0.2092992179024789,
        0.2092992179024789,
        0.5917001814331423,
        0.8717401485096066,
        1.0,
    ]
    weights = [
        0.03571428571428571,
        0.21070422714350603,
        0.3411226924835044,
        0.4124587946587038,
        0.4124587946587038,
        0.3411226924835044,
        0.21070422714350603,
        0.03571428571428571,
    ]
    barycentric = []
    for left_index in range(8):
        product = 1.0
        for right_index in range(8):
            if right_index != left_index:
                product = product * (points[left_index] - points[right_index])
        barycentric.append(1.0 / product)
    derivative = np.zeros((8, 8))
    for left_index in range(8):
        row_total = 0.0
        for right_index in range(8):
            if left_index != right_index:
                entry = (
                    barycentric[right_index]
                    / barycentric[left_index]
                    / (points[left_index] - points[right_index])
                )
                derivative[left_index, right_index] = entry
                row_total = row_total + entry
        derivative[left_index, left_index] = -row_total
    return derivative, np.asarray(weights)


DM, WEIGHTS = gll_tables()


def line(table, values):
    sums = [values[q] + values[7 - q] for q in range(4)]
    differences = [values[q] - values[7 - q] for q in range(4)]
    out = [None] * 8
    for i in range(4):
        even = odd = None
        for q in range(4):
            on_sum = float(table[i, q] + table[i, 7 - q]) / 2
            on_difference = float(table[i, q] - table[i, 7 - q]) / 2
            even = sums[q] * on_sum if even is None else even + sums[q] * on_sum
            odd = (
                differences[q] * on_difference
                if odd is None
                else odd + differences[q] * on_difference
            )
        out[i] = odd + even
        out[7 - i] = odd - even
    return out


def rows(i, j):
    return pl.ds((8 * i + j) * 8, 8)


def split(block):
    wide = jnp.concatenate([block[:256], block[256:]], axis=1)
    high = wide.astype(BF16)
    low = (wide - high.astype(F32)).astype(BF16)
    return [high, high, low]


def tall(wide):
    return jnp.concatenate([wide[:, :128], wide[:, 128:]], axis=0)


def slopes_jk(table_ref, block):
    parts = jnp.concatenate(split(block), axis=0)
    out = jnp.dot(table_ref[...], parts, preferred_element_type=F32)
    return tall(out[:256]), tall(out[256:])


def back_jk(turned_ref, flux_k, flux_j):
    parts = jnp.concatenate(split(flux_k) + split(flux_j), axis=0)
    return tall(jnp.dot(turned_ref[...], parts, preferred_element_type=F32))


def write_table(table, axis, table_ref, start, column):
    sub = lax.broadcasted_iota(jnp.int32, (8, 128), 0)
    lane = lax.broadcasted_iota(jnp.int32, (8, 128), 1)
    zero = jnp.zeros((8, 128), F32)
    place = lax.shift_right_logical(lane, 3)
    entry = place & 7 if axis else lane & 7
    bases = []
    for n in range(8):
        one_row = zero
        for q in range(8):
            one_row = jnp.where(entry == q, float(table[n, q]), one_row)
        bases.append(one_row)
    if axis:
        bases = [jnp.where((lane & 7) == sub, one_row, zero) for one_row in bases]
        place = lax.shift_right_logical(lane, 6)
    else:
        base = zero
        for n in range(8):
            base = jnp.where(sub == n, bases[n], base)
        bases = [base]
    highs = [base.astype(BF16).astype(F32) for base in bases]
    lows = [base - high for base, high in zip(bases, highs)]
    empty = jnp.zeros((16, 128), F32)
    for a in range(0, 32, 2):
        parts = []
        for values in (highs, lows):
            pair = []
            for block in (a, a + 1):
                own = place == (block // 8 % 2 if axis else block % 16)
                pair.append(jnp.where(own, values[block % 8 if axis else 0], zero))
            pair = jnp.concatenate(pair, axis=0)
            parts.append([pair, empty] if a < 16 else [empty, pair])
        wide = jnp.concatenate(parts[0] + parts[1] + parts[0], axis=1)
        table_ref[pl.ds(start + 8 * a, 16), column : column + 768] = wide.astype(BF16)


def lanes(block, index):
    wide = jnp.broadcast_to(index[None], (block.shape[0] // 8, 8, 128)).reshape(block.shape)
    return jnp.take_along_axis(block, wide, axis=1, mode="promise_in_bounds")


def set_mass(weight_ref, mass_ref):
    sub = lax.broadcasted_iota(jnp.int32, (8, 128), 0)
    along = jnp.zeros((8, 128), F32)
    for k in range(8):
        along = jnp.where(sub == k, float(WEIGHTS[k]), along)
    for i in range(8):
        for j in range(8):
            r = rows(i, j)
            mass_ref[r] = weight_ref[r] * (along * float(WEIGHTS[i] * WEIGHTS[j]))


def forward_jk(carry_ref, weigh, turned_ref, slope, work):
    fluxes = weigh[...] * slope[0], weigh[...] * slope[1]
    carried = carry_ref[2] * slope[0] + carry_ref[1] * slope[1]
    work[...] = carried + back_jk(turned_ref, *fluxes)


def adjoint_jk(source, carry_ref, weigh, turned_ref, slope, work):
    flux_k = carry_ref[2] * source[...] + weigh[...] * slope[0]
    flux_j = carry_ref[1] * source[...] + weigh[...] * slope[1]
    work[...] = back_jk(turned_ref, flux_k, flux_j)


def forward_i(source, carry_ref, weigh, work, target):
    for j in range(8):
        slopes = line(DM, [source[rows(i, j)] for i in range(8)])
        back = line(DM.T, [weigh[rows(i, j)] * slopes[i] for i in range(8)])
        for i in range(8):
            r = rows(i, j)
            target[r] = work[r] + (carry_ref[0, r] * slopes[i] + back[i])


def adjoint_i(source, base, carry_ref, weigh, work, target):
    for j in range(8):
        these = [rows(i, j) for i in range(8)]
        values = [source[r] for r in these]
        slopes = line(DM, values)
        fluxes = [carry_ref[0, r] * v + weigh[r] * g for r, v, g in zip(these, values, slopes)]
        for r, back in zip(these, line(DM.T, fluxes)):
            target[r] = base[r] - (back + work[r])


def set_slopes(source, table_ref, slope):
    slope[0], slope[1] = slopes_jk(table_ref, source[...])


def forward(sources, carry_ref, weigh_ref, table_ref, turned_ref, slope_ref, work_ref, target, finish):
    for f in range(3):
        set_slopes(sources.at[f], table_ref, slope_ref.at[f])
    for f in range(3):
        at = (carry_ref, weigh_ref.at[f])
        forward_jk(*at, turned_ref, slope_ref.at[f], work_ref.at[f])
    for f in range(3):
        at = (carry_ref, weigh_ref.at[f])
        forward_i(sources.at[f], *at, work_ref.at[f], target.at[f])
        finish(f)


def adjoint(
    sources, base, carry_ref, weigh_ref, table_ref, turned_ref, slope_ref, work_ref, target, finish
):
    for f in range(3):
        set_slopes(sources.at[f], table_ref, slope_ref.at[f])
    for f in range(3):
        at = (carry_ref, weigh_ref.at[f])
        adjoint_jk(sources.at[f], *at, turned_ref, slope_ref.at[f], work_ref.at[f])
    for f in range(3):
        at = (carry_ref, weigh_ref.at[f])
        adjoint_i(sources.at[f], base.at[f], *at, work_ref.at[f], target.at[f])
        finish(f)


def join_heights(ref, index):
    height, _, below, above = index
    lower = ref[pl.ds(0, 64, stride=8)]
    upper = ref[pl.ds(7, 64, stride=8)]
    tall = jnp.broadcast_to(height[None], (8, 8, 128)).reshape(64, 128)
    ref[pl.ds(0, 64, stride=8)] = lower + jnp.where(tall > 0, lanes(upper, below), 0.0)
    ref[pl.ds(7, 64, stride=8)] = upper + jnp.where(tall < 127, lanes(lower, above), 0.0)


def face_rows(ends, axis, way, k):
    end = ends[axis][way]
    return pl.ds(end * 8 + k, 8, stride=64) if axis else pl.ds(end * 64 + k, 8, stride=8)


def tile(c, k):
    return pl.ds((7 * c + k) * 8, 8)


def top_tile(ref):
    return pl.ds(ref.shape[0] - 8, 8)


def send_faces(c, ref, index, ends, out):
    inverse = index[1]
    top = jnp.broadcast_to(inverse[:, 127:], (8, 128))
    lane = lax.broadcasted_iota(jnp.int32, (8, 128), 1)
    for axis in range(2):
        for way in range(2):
            face = out[2 * axis + way]
            for k in range(7):
                face[tile(c, k)] = lanes(ref[face_rows(ends, axis, way, k)], inverse)
            last = lanes(ref[face_rows(ends, axis, way, 7)], top)
            others = face[top_tile(face)] if c else jnp.zeros((8, 128), F32)
            face[top_tile(face)] = jnp.where(lane == c, last, others)


def take_faces(c, index, ends, got, spread_ref):
    height = index[0]
    above = (height + 1) & 127
    own = jnp.full((8, 128), c, jnp.int32)
    for axis in range(2):
        for way in range(2):
            face = got[2 * axis + way]
            last = jnp.where(
                height < 127, lanes(face[tile(c, 0)], above), lanes(face[top_tile(face)], own)
            )
            parts = [lanes(face[tile(c, k)], height) for k in range(7)] + [last]
            slot = 2 * axis + jnp.minimum(ends[axis][way], 1)
            for k, part in enumerate(parts):
                spread_ref[c, slot, pl.ds(8 * k, 8)] = part * ends[2][axis] if way else part


def assembled(c, i, j, joined, spread_ref):
    total = joined[rows(i, j)]
    for axis, (end, place) in enumerate(((i, j), (j, i))):
        if end in (0, 7):
            total = total + spread_ref[c, 2 * axis + end // 7, pl.ds(place, 8, stride=8)]
    return total


def ends_of(columns):
    column = lax.rem(lax.axis_index("elem") + columns // 2, columns * DA)
    row, place = lax.div(column, columns), lax.rem(column, columns)
    row_odd, place_odd = lax.rem(row, 2), lax.rem(place, 2)
    row_inside = jnp.where((row > 0) & (row < DA - 1), 1.0, 0.0)
    place_inside = jnp.where((place > 0) & (place < columns - 1), 1.0, 0.0)
    return (
        (7 - 7 * row_odd, 7 * row_odd),
        (7 - 7 * place_odd, 7 * place_odd),
        (row_inside, place_inside),
    )


def index_of(index_ref):
    return tuple(index_ref[n] for n in range(4))


def index_kernel(
    columns,
    moment_far,
    state_far,
    flow_far,
    weight_far,
    diff_far,
    numbers_far,
    moment_ref,
    state_ref,
    carry_ref,
    weigh_ref,
    table_ref,
    turned_ref,
    index_ref,
    joined_ref,
    ie_ref,
    io_ref,
    je_ref,
    jo_ref,
    weight_ref,
    mass_ref,
    flow_ref,
    numbers_ref,
    diff_ref,
    arrived,
):
    far = (numbers_far, weight_far, state_far, diff_far, moment_far, flow_far)
    near = (numbers_ref, weight_ref, state_ref, diff_ref, moment_ref, flow_ref)
    copies = [pltpu.make_async_copy(a, b, arrived.at[n]) for n, (a, b) in enumerate(zip(far, near))]
    for copy in copies:
        copy.start()
    for axis in range(2):
        write_table(DM, axis, table_ref, 256 * axis, 0)
        write_table(DM.T, axis, turned_ref, 0, 768 * axis)
    ends = ends_of(columns)
    copies[0].wait()
    height = jnp.broadcast_to(numbers_ref[...] & 127, (8, 128))
    square = jnp.broadcast_to(height[:1].astype(F32), (128, 128)).T
    lane = lax.broadcasted_iota(jnp.int32, (128, 128), 1).astype(F32)
    row = lax.broadcasted_iota(jnp.int32, (128, 128), 0).astype(F32)
    inverse = jnp.sum(jnp.where(square == lane, row, 0.0), axis=0, keepdims=True)
    inverse = jnp.broadcast_to(inverse, (8, 128)).astype(jnp.int32)
    index = (
        height,
        inverse,
        lanes(inverse, (height - 1) & 127),
        lanes(inverse, (height + 1) & 127),
    )
    for n in range(4):
        index_ref[n] = index[n]
    copies[1].wait()
    set_mass(weight_ref, mass_ref)
    joined_ref[3] = mass_ref[...]
    copies[2].wait()
    out = (ie_ref, io_ref, je_ref, jo_ref)
    for c in range(3):
        joined_ref[c] = state_ref[c]
    for c in range(4):
        join_heights(joined_ref.at[c], index)
        send_faces(c, joined_ref.at[c], index, ends, out)
    copies[3].wait()
    for f in range(3):
        weigh_ref[f] = mass_ref[...] * (DT * diff_ref[f])
    copies[5].wait()
    for d in range(3):
        carry_ref[d] = mass_ref[...] * (DT * flow_ref[d])
    copies[4].wait()


def moment_kernel(
    columns,
    moment_ref,
    carry_ref,
    weigh_ref,
    table_ref,
    turned_ref,
    index_ref,
    joined_ref,
    ie_ref,
    io_ref,
    je_ref,
    jo_ref,
    slope_ref,
    work_ref,
):
    ends = ends_of(columns)
    index = index_of(index_ref)
    out = (ie_ref, io_ref, je_ref, jo_ref)

    def finish(f):
        join_heights(joined_ref.at[f], index)
        send_faces(f, joined_ref.at[f], index, ends, out)

    at = (carry_ref, weigh_ref, table_ref, turned_ref, slope_ref, work_ref)
    forward(moment_ref, *at, joined_ref, finish)


def edge_kernel(columns, axis, way, e_ref, o_ref, face, *refs):
    ends, out = ends_of(columns), refs[-1]
    out[...] = face[...]
    tiles = face.shape[0] // 8
    r = pl.ds(ends[axis][way], tiles, stride=8)
    for other, got in enumerate((e_ref, o_ref)):
        w = pl.ds(ends[1 - axis][other], tiles, stride=8)
        part = got[r]
        out[w] = out[w] + (part * ends[2][1 - axis] if other else part)


def state_kernel(
    columns,
    first,
    state_ref,
    carry_ref,
    weigh_ref,
    table_ref,
    turned_ref,
    index_ref,
    joined_ref,
    *refs,
):
    ends = ends_of(columns)
    index = index_of(index_ref)
    if first:
        got, (inverse_ref, state_out, joined_out), refs = refs[:4], refs[4:7], refs[7:]
        out, (slope_ref, work_ref, hold_ref, spread_ref) = refs[:4], refs[4:]
        take_faces(3, index, ends, got, spread_ref)
        for i in range(8):
            for j in range(8):
                inverse_ref[rows(i, j)] = 1.0 / assembled(3, i, j, joined_ref.at[3], spread_ref)
    else:
        inverse_ref, *got = refs[:5]
        state_far, slope_ref, work_ref, hold_ref, spread_ref, state_out, sent = refs[5:]
    for f in range(3):
        take_faces(f, index, ends, got, spread_ref)
        for i in range(8):
            for j in range(8):
                total = assembled(f, i, j, joined_ref.at[f], spread_ref)
                hold_ref[f, rows(i, j)] = total * inverse_ref[rows(i, j)]

    def finish(f):
        if first:
            joined_out[f] = state_out[f]
            join_heights(joined_out.at[f], index)
            send_faces(f, joined_out.at[f], index, ends, out)
        else:
            send_out(f, state_out, state_far, sent).start()

    at = (carry_ref, weigh_ref, table_ref, turned_ref, slope_ref, work_ref)
    adjoint(hold_ref, state_ref, *at, state_out, finish)
    if not first:
        for f in range(3):
            send_out(f, state_out, state_far, sent).wait()


def send_out(f, near, far, sent):
    return pltpu.make_async_copy(near.at[f], far.at[f], sent.at[f])


def moment_step(f, ends, index, moment_ref, joined_ref, inverse_ref, got, spread_ref, moment_out):
    take_faces(f, index, ends, got, spread_ref)
    for i in range(8):
        for j in range(8):
            r = rows(i, j)
            total = assembled(f, i, j, joined_ref.at[f], spread_ref)
            moment_out[f, r] = moment_ref[f, r] - total * inverse_ref[r]


def middle_kernel(
    columns,
    moment_ref,
    carry_ref,
    weigh_ref,
    table_ref,
    turned_ref,
    index_ref,
    inverse_ref,
    joined_ref,
    gie_ref,
    gio_ref,
    gje_ref,
    gjo_ref,
    moment_out,
    joined_out,
    ie_ref,
    io_ref,
    je_ref,
    jo_ref,
    slope_ref,
    work_ref,
    spread_ref,
):
    ends = ends_of(columns)
    index = index_of(index_ref)
    out = (ie_ref, io_ref, je_ref, jo_ref)
    got = (gie_ref, gio_ref, gje_ref, gjo_ref)
    for f in range(3):
        moment_step(f, ends, index, moment_ref, joined_ref, inverse_ref, got, spread_ref, moment_out)

    def finish(f):
        join_heights(joined_out.at[f], index)
        send_faces(f, joined_out.at[f], index, ends, out)

    at = (carry_ref, weigh_ref, table_ref, turned_ref, slope_ref, work_ref)
    forward(moment_out, *at, joined_out, finish)


def last_kernel(
    columns,
    moment_ref,
    index_ref,
    inverse_ref,
    joined_ref,
    gie_ref,
    gio_ref,
    gje_ref,
    gjo_ref,
    moment_far,
    spread_ref,
    moment_out,
    sent,
):
    ends = ends_of(columns)
    index = index_of(index_ref)
    got = (gie_ref, gio_ref, gje_ref, gjo_ref)

    for f in range(3):
        moment_step(f, ends, index, moment_ref, joined_ref, inverse_ref, got, spread_ref, moment_out)
        send_out(f, moment_out, moment_far, sent).start()
    for f in range(3):
        send_out(f, moment_out, moment_far, sent).wait()


VMEM = pl.BlockSpec(memory_space=pltpu.VMEM)
FAR = pl.BlockSpec(memory_space=pltpu.HBM)


def call(kernel, specs, shapes, scratch, flops, *operands, first_out=VMEM):
    moved = sum(o.size * 4 for o in operands) + sum(int(np.prod(s)) * 4 for s, _ in shapes)
    return pl.pallas_call(
        kernel,
        out_shape=[jax.ShapeDtypeStruct(s, t) for s, t in shapes],
        in_specs=specs,
        out_specs=[first_out] + [VMEM] * (len(shapes) - 1),
        scratch_shapes=scratch,
        compiler_params=pltpu.CompilerParams(vmem_limit_bytes=32 * 1024 * 1024),
        cost_estimate=pl.CostEstimate(flops=flops, bytes_accessed=moved, transcendentals=0),
    )(*operands)


def pairings(devices):
    columns = devices // DA
    device = lambda row, place: (row % DA * columns + place - columns // 2) % devices

    def both(pairs):
        return pairs + [(b, a) for a, b in pairs]

    places, halves = range(columns), range(0, columns, 2)
    along_i = [
        [(device(r, s), device(r + 1, s)) for r in range(0, DA, 2) for s in places],
        [(device(r, s), device(r + 1, s)) for r in range(1, DA - 1, 2) for s in places]
        + [(device(r, s), device(r, s + 1)) for r in (0, DA - 1) for s in halves],
    ]
    along_j = [
        [(device(r, s), device(r, s + 1)) for r in range(DA) for s in halves],
        [(device(r, s - 1), device(r, s)) for r in range(DA) for s in halves if s]
        + [(device(r, columns - 1), device(r + 1, 0)) for r in range(DA)],
    ]
    return [both(p) for p in along_i], [both(p) for p in along_j]


def shards(moment_fields, adjoint_fields, velocity, mass_weights, diffusivity, numbering):
    devices = lax.axis_size("elem")
    columns = devices // DA
    along_i, along_j = pairings(devices)
    whole, block = ((3, 512, 128), F32), ((512, 128), F32)
    work = pltpu.VMEM((3, 512, 128), F32)
    slopes = pltpu.VMEM((3, 2, 512, 128), F32)

    def spread(count):
        return pltpu.VMEM((count, 4, 64, 128), F32)

    def exchange(block, pairs):
        return lax.ppermute(block, "elem", pairs)

    def settle(block):
        anywhere = pl.BlockSpec(memory_space=pl.ANY)
        return pl.pallas_call(
            lambda *refs: None,
            out_shape=jax.ShapeDtypeStruct(block.shape, block.dtype),
            in_specs=[anywhere],
            out_specs=anywhere,
            input_output_aliases={0: 0},
            compiler_params=pltpu.CompilerParams(vmem_limit_bytes=1024 * 1024),
        )(block)

    def edge(count, axis, way, *operands):
        return call(
            functools.partial(edge_kernel, columns, axis, way),
            [VMEM] * len(operands),
            [(face_shape(count), F32)],
            [],
            count * 64 * 128,
            *operands,
        )[0]

    def meet_ij(count, faces):
        got = [exchange(faces[way], along_i[way]) for way in range(2)]
        far_face = edge(count, 1, 1, *got, faces[3])
        near_face = edge(count, 1, 0, *got, faces[2], far_face)
        far_face, near_face = exchange(far_face, along_j[1]), exchange(near_face, along_j[0])
        return got + [near_face, settle(far_face)]

    def meet_ji(count, faces):
        got = [exchange(faces[2 + way], along_j[way]) for way in range(2)]
        got[1] = settle(got[1])
        face_e = edge(count, 0, 0, *got, faces[0])
        face_o = edge(count, 0, 1, *got, faces[1])
        return [exchange(face_e, along_i[0]), exchange(face_o, along_i[1])] + got

    def far(array):
        return pltpu.with_memory_space_constraint(array, pltpu.HBM)

    def face_shape(count):
        return ((7 * count + 1) * 8, 128)

    def faces_shape(count):
        return [(face_shape(count), F32)] * 4

    moment, state, carry, weigh, table, turned, index, joined_state, *faces_state = call(
        functools.partial(index_kernel, columns),
        [FAR] * 6,
        [whole] * 4
        + [((512, 768), BF16), ((256, 1536), BF16)]
        + [((4, 8, 128), jnp.int32), ((4, 512, 128), F32)]
        + faces_shape(4),
        [
            pltpu.VMEM((512, 128), F32),
            pltpu.VMEM((512, 128), F32),
            work,
            pltpu.VMEM((1, 128), jnp.int32),
            pltpu.SMEM((3,), F32),
            pltpu.SemaphoreType.DMA((6,)),
        ],
        1_000_000,
        *map(far, (moment_fields, adjoint_fields, velocity, mass_weights)),
        *map(far, (diffusivity, numbering.reshape(1, 128))),
    )
    tables = (carry, weigh, table, turned, index)
    got_state = meet_ij(4, faces_state)
    joined_moment, *faces_moment = call(
        functools.partial(moment_kernel, columns),
        [VMEM] * 6,
        [whole] + faces_shape(3),
        [slopes, work],
        20_000_000,
        moment,
        *tables,
    )
    got_moment = meet_ji(3, faces_moment)
    inverse, state, joined_state, *faces_state = call(
        functools.partial(state_kernel, columns, True),
        [VMEM] * 11,
        [block, whole, whole] + faces_shape(3),
        [slopes, work, work, spread(4)],
        20_000_000,
        state,
        *tables,
        joined_state,
        *got_state,
    )
    got_state = meet_ij(3, faces_state)
    moment, joined_moment, *faces_moment = call(
        functools.partial(middle_kernel, columns),
        [VMEM] * 12,
        [whole, whole] + faces_shape(3),
        [slopes, work, spread(3)],
        20_000_000,
        moment,
        *tables,
        inverse,
        joined_moment,
        *got_moment,
    )
    got_moment = meet_ji(3, faces_moment)
    (state,) = call(
        functools.partial(state_kernel, columns, False),
        [VMEM] * 12,
        [whole],
        [slopes, work, work, spread(3), work] + [pltpu.SemaphoreType.DMA((3,))],
        20_000_000,
        state,
        *tables,
        joined_state,
        inverse,
        *got_state,
        first_out=FAR,
    )
    (moment,) = call(
        functools.partial(last_kernel, columns),
        [VMEM] * 8,
        [whole],
        [spread(3), work] + [pltpu.SemaphoreType.DMA((3,))],
        1_000_000,
        moment,
        index,
        inverse,
        joined_moment,
        *got_moment,
        first_out=FAR,
    )
    return moment, state


def solution(mesh):
    in_specs = (
        P(None, None, "elem"),
        P(None, None, "elem"),
        P(None, None, "elem"),
        P(None, "elem"),
        P(),
        P("elem"),
    )
    out_specs = (P(None, None, "elem"), P(None, None, "elem"))
    return jax.shard_map(shards, mesh=mesh, in_specs=in_specs, out_specs=out_specs, check_vma=False)
```

```python
import functools

import jax
import jax.numpy as jnp
import numpy as np
from jax import lax
from jax.experimental import pallas as pl
from jax.experimental.pallas import tpu as pltpu
from jax.sharding import PartitionSpec as P

DA = 4
DT = 0.001
F32 = jnp.float32
BF16 = jnp.bfloat16


def gll_tables():
    points = [
        -1.0,
        -0.8717401485096066,
        -0.5917001814331423,
        -0.2092992179024789,
        0.2092992179024789,
        0.5917001814331423,
        0.8717401485096066,
        1.0,
    ]
    weights = [
        0.03571428571428571,
        0.21070422714350603,
        0.3411226924835044,
        0.4124587946587038,
        0.4124587946587038,
        0.3411226924835044,
        0.21070422714350603,
        0.03571428571428571,
    ]
    barycentric = []
    for left_index in range(8):
        product = 1.0
        for right_index in range(8):
            if right_index != left_index:
                product = product * (points[left_index] - points[right_index])
        barycentric.append(1.0 / product)
    derivative = np.zeros((8, 8))
    for left_index in range(8):
        row_total = 0.0
        for right_index in range(8):
            if left_index != right_index:
                entry = (
                    barycentric[right_index]
                    / barycentric[left_index]
                    / (points[left_index] - points[right_index])
                )
                derivative[left_index, right_index] = entry
                row_total = row_total + entry
        derivative[left_index, left_index] = -row_total
    return derivative, np.asarray(weights)


DM, WEIGHTS = gll_tables()


def line(table, values):
    sums = [values[q] + values[7 - q] for q in range(4)]
    differences = [values[q] - values[7 - q] for q in range(4)]
    out = [None] * 8
    for i in range(4):
        even = odd = None
        for q in range(4):
            on_sum = float(table[i, q] + table[i, 7 - q]) / 2
            on_difference = float(table[i, q] - table[i, 7 - q]) / 2
            even = sums[q] * on_sum if even is None else even + sums[q] * on_sum
            odd = (
                differences[q] * on_difference
                if odd is None
                else odd + differences[q] * on_difference
            )
        out[i] = odd + even
        out[7 - i] = odd - even
    return out


def rows(i, j):
    return pl.ds((8 * i + j) * 8, 8)


def split(block):
    wide = jnp.concatenate([block[128 * n : 128 * (n + 1)] for n in range(4)], axis=1)
    high = wide.astype(BF16)
    low = (wide - high.astype(F32)).astype(BF16)
    return [high, high, low]


def tall(wide):
    return jnp.concatenate([wide[:, 128 * n : 128 * (n + 1)] for n in range(4)], axis=0)


def slopes_jk(table_ref, block):
    parts = jnp.concatenate(split(block), axis=0)
    out = jnp.dot(table_ref[...], parts, preferred_element_type=F32)
    return tall(out[:128]), tall(out[128:])


def back_jk(turned_ref, flux_k, flux_j):
    parts = jnp.concatenate(split(flux_k) + split(flux_j), axis=0)
    return tall(jnp.dot(turned_ref[...], parts, preferred_element_type=F32))


def write_table(table, axis, table_ref, start, column):
    sub = lax.broadcasted_iota(jnp.int32, (8, 128), 0)
    lane = lax.broadcasted_iota(jnp.int32, (8, 128), 1)
    zero = jnp.zeros((8, 128), F32)
    place = lax.shift_right_logical(lane, 3)
    entry = place & 7 if axis else lane & 7
    bases = []
    for n in range(8):
        one_row = zero
        for q in range(8):
            one_row = jnp.where(entry == q, float(table[n, q]), one_row)
        bases.append(one_row)
    if axis:
        bases = [jnp.where((lane & 7) == sub, one_row, zero) for one_row in bases]
        place = lax.shift_right_logical(lane, 6)
    else:
        base = zero
        for n in range(8):
            base = jnp.where(sub == n, bases[n], base)
        bases = [base]
    highs = [base.astype(BF16).astype(F32) for base in bases]
    lows = [base - high for base, high in zip(bases, highs)]
    for a in range(0, 16, 2):
        parts = []
        for values in (highs, lows):
            pair = []
            for block in (a, a + 1):
                own = place == (block // 8 if axis else block)
                pair.append(jnp.where(own, values[block % 8 if axis else 0], zero))
            parts.append(jnp.concatenate(pair, axis=0))
        wide = jnp.concatenate([parts[0], parts[1], parts[0]], axis=1)
        table_ref[pl.ds(start + 8 * a, 16), column : column + 384] = wide.astype(BF16)


def lanes(block, index):
    wide = jnp.broadcast_to(index[None], (block.shape[0] // 8, 8, 128)).reshape(block.shape)
    return jnp.take_along_axis(block, wide, axis=1, mode="promise_in_bounds")


def set_mass(weight_ref, mass_ref):
    sub = lax.broadcasted_iota(jnp.int32, (8, 128), 0)
    along = jnp.zeros((8, 128), F32)
    for k in range(8):
        along = jnp.where(sub == k, float(WEIGHTS[k]), along)
    for i in range(8):
        for j in range(8):
            r = rows(i, j)
            mass_ref[r] = weight_ref[r] * (along * float(WEIGHTS[i] * WEIGHTS[j]))


def forward_jk(carry_ref, weigh, turned_ref, slope, work):
    fluxes = weigh[...] * slope[0], weigh[...] * slope[1]
    carried = carry_ref[2] * slope[0] + carry_ref[1] * slope[1]
    work[...] = carried + back_jk(turned_ref, *fluxes)


def adjoint_jk(source, carry_ref, weigh, turned_ref, slope, work):
    flux_k = carry_ref[2] * source[...] + weigh[...] * slope[0]
    flux_j = carry_ref[1] * source[...] + weigh[...] * slope[1]
    work[...] = back_jk(turned_ref, flux_k, flux_j)


def forward_i(source, carry_ref, weigh, work, target):
    for j in range(8):
        slopes = line(DM, [source[rows(i, j)] for i in range(8)])
        back = line(DM.T, [weigh[rows(i, j)] * slopes[i] for i in range(8)])
        for i in range(8):
            r = rows(i, j)
            target[r] = work[r] + (carry_ref[0, r] * slopes[i] + back[i])


def adjoint_i(source, base, carry_ref, weigh, work, target):
    for j in range(8):
        these = [rows(i, j) for i in range(8)]
        values = [source[r] for r in these]
        slopes = line(DM, values)
        fluxes = [carry_ref[0, r] * v + weigh[r] * g for r, v, g in zip(these, values, slopes)]
        for r, back in zip(these, line(DM.T, fluxes)):
            target[r] = base[r] - (back + work[r])


def set_slopes(source, table_ref, slope):
    slope[0], slope[1] = slopes_jk(table_ref, source[...])


def forward(sources, carry_ref, weigh_ref, table_ref, turned_ref, slope_ref, work_ref, target, finish):
    for f in range(3):
        set_slopes(sources.at[f], table_ref, slope_ref.at[f])
    for f in range(3):
        at = (carry_ref, weigh_ref.at[f])
        forward_jk(*at, turned_ref, slope_ref.at[f], work_ref.at[f])
    for f in range(3):
        at = (carry_ref, weigh_ref.at[f])
        forward_i(sources.at[f], *at, work_ref.at[f], target.at[f])
        finish(f)


def adjoint(
    sources, base, carry_ref, weigh_ref, table_ref, turned_ref, slope_ref, work_ref, target, finish
):
    for f in range(3):
        set_slopes(sources.at[f], table_ref, slope_ref.at[f])
    for f in range(3):
        at = (carry_ref, weigh_ref.at[f])
        adjoint_jk(sources.at[f], *at, turned_ref, slope_ref.at[f], work_ref.at[f])
    for f in range(3):
        at = (carry_ref, weigh_ref.at[f])
        adjoint_i(sources.at[f], base.at[f], *at, work_ref.at[f], target.at[f])
        finish(f)


def join_heights(ref, index):
    height, _, below, above = index
    lower = ref[pl.ds(0, 64, stride=8)]
    upper = ref[pl.ds(7, 64, stride=8)]
    tall = jnp.broadcast_to(height[None], (8, 8, 128)).reshape(64, 128)
    ref[pl.ds(0, 64, stride=8)] = lower + jnp.where(tall > 0, lanes(upper, below), 0.0)
    ref[pl.ds(7, 64, stride=8)] = upper + jnp.where(tall < 127, lanes(lower, above), 0.0)


def face_rows(ends, axis, way, k):
    end = ends[axis][way]
    return pl.ds(end * 8 + k, 8, stride=64) if axis else pl.ds(end * 64 + k, 8, stride=8)


def tile(c, k):
    return pl.ds((7 * c + k) * 8, 8)


def top_tile(ref):
    return pl.ds(ref.shape[0] - 8, 8)


def send_faces(c, ref, index, ends, out):
    inverse = index[1]
    top = jnp.broadcast_to(inverse[:, 127:], (8, 128))
    lane = lax.broadcasted_iota(jnp.int32, (8, 128), 1)
    for axis in range(2):
        for way in range(2):
            face = out[2 * axis + way]
            for k in range(7):
                face[tile(c, k)] = lanes(ref[face_rows(ends, axis, way, k)], inverse)
            last = lanes(ref[face_rows(ends, axis, way, 7)], top)
            others = face[top_tile(face)] if c else jnp.zeros((8, 128), F32)
            face[top_tile(face)] = jnp.where(lane == c, last, others)


def take_faces(c, index, ends, got, spread_ref):
    height = index[0]
    above = (height + 1) & 127
    own = jnp.full((8, 128), c, jnp.int32)
    for axis in range(2):
        for way in range(2):
            face = got[3 - way if axis else way]
            last = jnp.where(
                height < 127, lanes(face[tile(c, 0)], above), lanes(face[top_tile(face)], own)
            )
            parts = [lanes(face[tile(c, k)], height) for k in range(7)] + [last]
            slot = 2 * axis + jnp.minimum(ends[axis][way], 1)
            for k, part in enumerate(parts):
                spread_ref[c, slot, pl.ds(8 * k, 8)] = part * ends[2][axis] if way else part


def assembled(c, i, j, joined, spread_ref):
    total = joined[rows(i, j)]
    for axis, (end, place) in enumerate(((i, j), (j, i))):
        if end in (0, 7):
            total = total + spread_ref[c, 2 * axis + end // 7, pl.ds(place, 8, stride=8)]
    return total


def ends_of(columns):
    column = lax.rem(lax.axis_index("elem") + columns // 2, columns * DA)
    row, place = lax.div(column, columns), lax.rem(column, columns)
    row_odd, place_odd = lax.rem(row, 2), lax.rem(place, 2)
    row_inside = jnp.where((row > 0) & (row < DA - 1), 1.0, 0.0)
    place_inside = jnp.where((place > 0) & (place < columns - 1), 1.0, 0.0)
    return (
        (7 - 7 * row_odd, 7 * row_odd),
        (7 - 7 * place_odd, 7 * place_odd),
        (row_inside, place_inside),
    )


def index_of(index_ref):
    return tuple(index_ref[n] for n in range(4))


def index_kernel(
    columns,
    moment_far,
    state_far,
    flow_far,
    weight_far,
    diff_far,
    numbers_far,
    moment_ref,
    state_ref,
    carry_ref,
    weigh_ref,
    table_ref,
    turned_ref,
    index_ref,
    joined_ref,
    ie_ref,
    io_ref,
    je_ref,
    jo_ref,
    weight_ref,
    mass_ref,
    flow_ref,
    numbers_ref,
    diff_ref,
    arrived,
):
    far = (numbers_far, weight_far, state_far, diff_far, moment_far, flow_far)
    near = (numbers_ref, weight_ref, state_ref, diff_ref, moment_ref, flow_ref)
    copies = [pltpu.make_async_copy(a, b, arrived.at[n]) for n, (a, b) in enumerate(zip(far, near))]
    for copy in copies:
        copy.start()
    for axis in range(2):
        write_table(DM, axis, table_ref, 128 * axis, 0)
        write_table(DM.T, axis, turned_ref, 0, 384 * axis)
    ends = ends_of(columns)
    copies[0].wait()
    height = jnp.broadcast_to(numbers_ref[...] & 127, (8, 128))
    square = jnp.broadcast_to(height[:1].astype(F32), (128, 128)).T
    lane = lax.broadcasted_iota(jnp.int32, (128, 128), 1).astype(F32)
    row = lax.broadcasted_iota(jnp.int32, (128, 128), 0).astype(F32)
    inverse = jnp.sum(jnp.where(square == lane, row, 0.0), axis=0, keepdims=True)
    inverse = jnp.broadcast_to(inverse, (8, 128)).astype(jnp.int32)
    index = (
        height,
        inverse,
        lanes(inverse, (height - 1) & 127),
        lanes(inverse, (height + 1) & 127),
    )
    for n in range(4):
        index_ref[n] = index[n]
    copies[1].wait()
    set_mass(weight_ref, mass_ref)
    joined_ref[3] = mass_ref[...]
    copies[2].wait()
    out = (ie_ref, io_ref, je_ref, jo_ref)
    for c in range(3):
        joined_ref[c] = state_ref[c]
    for c in range(4):
        join_heights(joined_ref.at[c], index)
        send_faces(c, joined_ref.at[c], index, ends, out)
    copies[3].wait()
    for f in range(3):
        weigh_ref[f] = mass_ref[...] * (DT * diff_ref[f])
    copies[5].wait()
    for d in range(3):
        carry_ref[d] = mass_ref[...] * (DT * flow_ref[d])
    copies[4].wait()


def moment_kernel(
    columns,
    moment_ref,
    carry_ref,
    weigh_ref,
    table_ref,
    turned_ref,
    index_ref,
    joined_ref,
    ie_ref,
    io_ref,
    je_ref,
    jo_ref,
    slope_ref,
    work_ref,
):
    ends = ends_of(columns)
    index = index_of(index_ref)
    out = (ie_ref, io_ref, je_ref, jo_ref)

    def finish(f):
        join_heights(joined_ref.at[f], index)
        send_faces(f, joined_ref.at[f], index, ends, out)

    at = (carry_ref, weigh_ref, table_ref, turned_ref, slope_ref, work_ref)
    forward(moment_ref, *at, joined_ref, finish)


def edge_kernel(columns, way, ie_ref, io_ref, face, *refs):
    ends, out = ends_of(columns), refs[-1]
    out[...] = face[...]
    tiles = face.shape[0] // 8
    r = pl.ds(ends[1][way], tiles, stride=8)
    for other, got in enumerate((ie_ref, io_ref)):
        w = pl.ds(ends[0][other], tiles, stride=8)
        part = got[r]
        out[w] = out[w] + (part * ends[2][0] if other else part)


def state_kernel(
    columns,
    first,
    state_ref,
    carry_ref,
    weigh_ref,
    table_ref,
    turned_ref,
    index_ref,
    joined_ref,
    *refs,
):
    ends = ends_of(columns)
    index = index_of(index_ref)
    if first:
        got, (inverse_ref, state_out, joined_out), refs = refs[:4], refs[4:7], refs[7:]
        out, (slope_ref, work_ref, hold_ref, spread_ref) = refs[:4], refs[4:]
        take_faces(3, index, ends, got, spread_ref)
        for i in range(8):
            for j in range(8):
                inverse_ref[rows(i, j)] = 1.0 / assembled(3, i, j, joined_ref.at[3], spread_ref)
    else:
        inverse_ref, *got = refs[:5]
        state_far, token_ref, slope_ref, work_ref, hold_ref, spread_ref, state_out, sent = refs[5:]
        token_ref[...] = jnp.zeros_like(token_ref)
    for f in range(3):
        take_faces(f, index, ends, got, spread_ref)
        for i in range(8):
            for j in range(8):
                total = assembled(f, i, j, joined_ref.at[f], spread_ref)
                hold_ref[f, rows(i, j)] = total * inverse_ref[rows(i, j)]

    def finish(f):
        if first:
            joined_out[f] = state_out[f]
            join_heights(joined_out.at[f], index)
            send_faces(f, joined_out.at[f], index, ends, out)
        else:
            send_out(f, state_out, state_far, sent).start()

    at = (carry_ref, weigh_ref, table_ref, turned_ref, slope_ref, work_ref)
    adjoint(hold_ref, state_ref, *at, state_out, finish)
    if not first:
        for f in range(3):
            send_out(f, state_out, state_far, sent).wait()


def send_out(f, near, far, sent):
    return pltpu.make_async_copy(near.at[f], far.at[f], sent.at[f])


def moment_step(f, ends, index, moment_ref, joined_ref, inverse_ref, got, spread_ref, moment_out):
    take_faces(f, index, ends, got, spread_ref)
    for i in range(8):
        for j in range(8):
            r = rows(i, j)
            total = assembled(f, i, j, joined_ref.at[f], spread_ref)
            moment_out[f, r] = moment_ref[f, r] - total * inverse_ref[r]


def middle_kernel(
    columns,
    moment_ref,
    carry_ref,
    weigh_ref,
    table_ref,
    turned_ref,
    index_ref,
    inverse_ref,
    joined_ref,
    gie_ref,
    gio_ref,
    gjo_ref,
    gje_ref,
    moment_out,
    joined_out,
    ie_ref,
    io_ref,
    je_ref,
    jo_ref,
    slope_ref,
    work_ref,
    spread_ref,
):
    ends = ends_of(columns)
    index = index_of(index_ref)
    out = (ie_ref, io_ref, je_ref, jo_ref)
    got = (gie_ref, gio_ref, gjo_ref, gje_ref)
    for f in range(3):
        moment_step(f, ends, index, moment_ref, joined_ref, inverse_ref, got, spread_ref, moment_out)

    def finish(f):
        join_heights(joined_out.at[f], index)
        send_faces(f, joined_out.at[f], index, ends, out)

    at = (carry_ref, weigh_ref, table_ref, turned_ref, slope_ref, work_ref)
    forward(moment_out, *at, joined_out, finish)


def last_kernel(
    columns,
    moment_ref,
    index_ref,
    inverse_ref,
    joined_ref,
    gie_ref,
    gio_ref,
    gjo_ref,
    gje_ref,
    moment_far,
    spread_ref,
    moment_out,
    sent,
):
    ends = ends_of(columns)
    index = index_of(index_ref)
    got = (gie_ref, gio_ref, gjo_ref, gje_ref)

    for f in range(3):
        moment_step(f, ends, index, moment_ref, joined_ref, inverse_ref, got, spread_ref, moment_out)
        send_out(f, moment_out, moment_far, sent).start()
    for f in range(3):
        send_out(f, moment_out, moment_far, sent).wait()


VMEM = pl.BlockSpec(memory_space=pltpu.VMEM)
FAR = pl.BlockSpec(memory_space=pltpu.HBM)


def call(kernel, specs, shapes, scratch, flops, *operands, first_out=VMEM):
    moved = sum(o.size * 4 for o in operands) + sum(int(np.prod(s)) * 4 for s, _ in shapes)
    return pl.pallas_call(
        kernel,
        out_shape=[jax.ShapeDtypeStruct(s, t) for s, t in shapes],
        in_specs=specs,
        out_specs=[first_out] + [VMEM] * (len(shapes) - 1),
        scratch_shapes=scratch,
        compiler_params=pltpu.CompilerParams(vmem_limit_bytes=32 * 1024 * 1024),
        cost_estimate=pl.CostEstimate(flops=flops, bytes_accessed=moved, transcendentals=0),
    )(*operands)


def pairings(devices):
    columns = devices // DA
    device = lambda row, place: (row % DA * columns + place - columns // 2) % devices

    def both(pairs):
        return pairs + [(b, a) for a, b in pairs]

    places, halves = range(columns), range(0, columns, 2)
    along_i = [
        [(device(r, s), device(r + 1, s)) for r in range(0, DA, 2) for s in places],
        [(device(r, s), device(r + 1, s)) for r in range(1, DA - 1, 2) for s in places]
        + [(device(r, s), device(r, s + 1)) for r in (0, DA - 1) for s in halves],
    ]
    along_j = [
        [(device(r, s), device(r, s + 1)) for r in range(DA) for s in halves],
        [(device(r, s - 1), device(r, s)) for r in range(DA) for s in halves if s]
        + [(device(r, columns - 1), device(r + 1, 0)) for r in range(DA)],
    ]
    return [both(p) for p in along_i], [both(p) for p in along_j]


def shards(moment_fields, adjoint_fields, velocity, mass_weights, diffusivity, numbering):
    devices = lax.axis_size("elem")
    columns = devices // DA
    along_i, along_j = pairings(devices)
    whole, block = ((3, 512, 128), F32), ((512, 128), F32)
    work = pltpu.VMEM((3, 512, 128), F32)
    slopes = pltpu.VMEM((3, 2, 512, 128), F32)

    def spread(count):
        return pltpu.VMEM((count, 4, 64, 128), F32)

    def exchange(block, pairs):
        return lax.ppermute(block, "elem", pairs)

    def settle(block, *after):
        anywhere = pl.BlockSpec(memory_space=pl.ANY)
        return pl.pallas_call(
            lambda *refs: None,
            out_shape=jax.ShapeDtypeStruct(block.shape, block.dtype),
            in_specs=[anywhere] * (1 + len(after)),
            out_specs=anywhere,
            input_output_aliases={0: 0},
            compiler_params=pltpu.CompilerParams(vmem_limit_bytes=1024 * 1024),
        )(block, *after)

    def edge(count, way, *operands):
        return call(
            functools.partial(edge_kernel, columns, way),
            [VMEM] * len(operands),
            [(face_shape(count), F32)],
            [],
            count * 64 * 128,
            *operands,
        )[0]

    def meet(count, faces):
        got_i = [exchange(faces[way], along_i[way]) for way in range(2)]
        far_face = edge(count, 1, *got_i, faces[3])
        near_face = edge(count, 0, *got_i, faces[2], far_face)
        return got_i + [exchange(far_face, along_j[1]), exchange(near_face, along_j[0])]

    def settled(got, *after):
        return got[:2] + [settle(got[2], *after), got[3]]

    def far(array):
        return pltpu.with_memory_space_constraint(array, pltpu.HBM)

    def face_shape(count):
        return ((7 * count + 1) * 8, 128)

    def faces_shape(count):
        return [(face_shape(count), F32)] * 4

    moment, state, carry, weigh, table, turned, index, joined_state, *faces_state = call(
        functools.partial(index_kernel, columns),
        [FAR] * 6,
        [whole] * 4
        + [((256, 384), BF16), ((128, 768), BF16)]
        + [((4, 8, 128), jnp.int32), ((4, 512, 128), F32)]
        + faces_shape(4),
        [
            pltpu.VMEM((512, 128), F32),
            pltpu.VMEM((512, 128), F32),
            work,
            pltpu.VMEM((1, 128), jnp.int32),
            pltpu.SMEM((3,), F32),
            pltpu.SemaphoreType.DMA((6,)),
        ],
        1_000_000,
        *map(far, (moment_fields, adjoint_fields, velocity, mass_weights)),
        *map(far, (diffusivity, numbering.reshape(1, 128))),
    )
    tables = (carry, weigh, table, turned, index)
    got_state = meet(4, faces_state)
    joined_moment, *faces_moment = call(
        functools.partial(moment_kernel, columns),
        [VMEM] * 6,
        [whole] + faces_shape(3),
        [slopes, work],
        20_000_000,
        moment,
        *tables,
    )
    got_moment = meet(3, faces_moment)
    inverse, state, joined_state, *faces_state = call(
        functools.partial(state_kernel, columns, True),
        [VMEM] * 11,
        [block, whole, whole] + faces_shape(3),
        [slopes, work, work, spread(4)],
        20_000_000,
        state,
        *tables,
        joined_state,
        *settled(got_state),
    )
    got_state = meet(3, faces_state)
    moment, joined_moment, *faces_moment = call(
        functools.partial(middle_kernel, columns),
        [VMEM] * 12,
        [whole, whole] + faces_shape(3),
        [slopes, work, spread(3)],
        20_000_000,
        moment,
        *tables,
        inverse,
        joined_moment,
        *settled(got_moment, inverse),
    )
    got_moment = meet(3, faces_moment)
    state, token = call(
        functools.partial(state_kernel, columns, False),
        [VMEM] * 12,
        [whole, ((8, 128), F32)],
        [slopes, work, work, spread(3), work] + [pltpu.SemaphoreType.DMA((3,))],
        20_000_000,
        state,
        *tables,
        joined_state,
        inverse,
        *settled(got_state),
        first_out=FAR,
    )
    (moment,) = call(
        functools.partial(last_kernel, columns),
        [VMEM] * 8,
        [whole],
        [spread(3), work] + [pltpu.SemaphoreType.DMA((3,))],
        1_000_000,
        moment,
        index,
        inverse,
        joined_moment,
        *settled(got_moment, token),
        first_out=FAR,
    )
    return moment, state


def solution(mesh):
    in_specs = (
        P(None, None, "elem"),
        P(None, None, "elem"),
        P(None, None, "elem"),
        P(None, "elem"),
        P(),
        P("elem"),
    )
    out_specs = (P(None, None, "elem"), P(None, None, "elem"))
    return jax.shard_map(shards, mesh=mesh, in_specs=in_specs, out_specs=out_specs, check_vma=False)
```

```python
import functools

import jax
import jax.numpy as jnp
import numpy as np
from jax import lax
from jax.experimental import pallas as pl
from jax.experimental.pallas import tpu as pltpu
from jax.sharding import PartitionSpec as P

DA = 4
DT = 0.001
F32 = jnp.float32
BF16 = jnp.bfloat16


def gll_tables():
    points = [
        -1.0,
        -0.8717401485096066,
        -0.5917001814331423,
        -0.2092992179024789,
        0.2092992179024789,
        0.5917001814331423,
        0.8717401485096066,
        1.0,
    ]
    weights = [
        0.03571428571428571,
        0.21070422714350603,
        0.3411226924835044,
        0.4124587946587038,
        0.4124587946587038,
        0.3411226924835044,
        0.21070422714350603,
        0.03571428571428571,
    ]
    barycentric = []
    for left_index in range(8):
        product = 1.0
        for right_index in range(8):
            if right_index != left_index:
                product = product * (points[left_index] - points[right_index])
        barycentric.append(1.0 / product)
    derivative = np.zeros((8, 8))
    for left_index in range(8):
        row_total = 0.0
        for right_index in range(8):
            if left_index != right_index:
                entry = (
                    barycentric[right_index]
                    / barycentric[left_index]
                    / (points[left_index] - points[right_index])
                )
                derivative[left_index, right_index] = entry
                row_total = row_total + entry
        derivative[left_index, left_index] = -row_total
    return derivative, np.asarray(weights)


DM, WEIGHTS = gll_tables()


def line(table, values):
    sums = [values[q] + values[7 - q] for q in range(4)]
    differences = [values[q] - values[7 - q] for q in range(4)]
    out = [None] * 8
    for i in range(4):
        even = odd = None
        for q in range(4):
            on_sum = float(table[i, q] + table[i, 7 - q]) / 2
            on_difference = float(table[i, q] - table[i, 7 - q]) / 2
            even = sums[q] * on_sum if even is None else even + sums[q] * on_sum
            odd = (
                differences[q] * on_difference
                if odd is None
                else odd + differences[q] * on_difference
            )
        out[i] = odd + even
        out[7 - i] = odd - even
    return out


def rows(i, j):
    return pl.ds((8 * i + j) * 8, 8)


def split(block):
    wide = jnp.concatenate([block[128 * n : 128 * (n + 1)] for n in range(4)], axis=1)
    high = wide.astype(BF16)
    low = (wide - high.astype(F32)).astype(BF16)
    return [high, high, low]


def tall(wide):
    return jnp.concatenate([wide[:, 128 * n : 128 * (n + 1)] for n in range(4)], axis=0)


def slopes_jk(table_ref, block):
    parts = jnp.concatenate(split(block), axis=0)
    out = jnp.dot(table_ref[...], parts, preferred_element_type=F32)
    return tall(out[:128]), tall(out[128:])


def back_jk(turned_ref, flux_k, flux_j):
    parts = jnp.concatenate(split(flux_k) + split(flux_j), axis=0)
    return tall(jnp.dot(turned_ref[...], parts, preferred_element_type=F32))


def write_table(table, axis, table_ref, start, column):
    sub = lax.broadcasted_iota(jnp.int32, (8, 128), 0)
    lane = lax.broadcasted_iota(jnp.int32, (8, 128), 1)
    zero = jnp.zeros((8, 128), F32)
    place = lax.shift_right_logical(lane, 3)
    entry = place & 7 if axis else lane & 7
    bases = []
    for n in range(8):
        one_row = zero
        for q in range(8):
            one_row = jnp.where(entry == q, float(table[n, q]), one_row)
        bases.append(one_row)
    if axis:
        bases = [jnp.where((lane & 7) == sub, one_row, zero) for one_row in bases]
        place = lax.shift_right_logical(lane, 6)
    else:
        base = zero
        for n in range(8):
            base = jnp.where(sub == n, bases[n], base)
        bases = [base]
    highs = [base.astype(BF16).astype(F32) for base in bases]
    lows = [base - high for base, high in zip(bases, highs)]
    for a in range(0, 16, 2):
        parts = []
        for values in (highs, lows):
            pair = []
            for block in (a, a + 1):
                own = place == (block // 8 if axis else block)
                pair.append(jnp.where(own, values[block % 8 if axis else 0], zero))
            parts.append(jnp.concatenate(pair, axis=0))
        wide = jnp.concatenate([parts[0], parts[1], parts[0]], axis=1)
        table_ref[pl.ds(start + 8 * a, 16), column : column + 384] = wide.astype(BF16)


def lanes(block, index):
    wide = jnp.broadcast_to(index[None], (block.shape[0] // 8, 8, 128)).reshape(block.shape)
    return jnp.take_along_axis(block, wide, axis=1, mode="promise_in_bounds")


def set_mass(weight_ref, mass_ref):
    sub = lax.broadcasted_iota(jnp.int32, (8, 128), 0)
    along = jnp.zeros((8, 128), F32)
    for k in range(8):
        along = jnp.where(sub == k, float(WEIGHTS[k]), along)
    for i in range(8):
        for j in range(8):
            r = rows(i, j)
            mass_ref[r] = weight_ref[r] * (along * float(WEIGHTS[i] * WEIGHTS[j]))


def set_slopes(source, table_ref, slope):
    slope[0], slope[1] = slopes_jk(table_ref, source[...])


def forward_i(source, carry_ref, weigh, target):
    for j in range(8):
        slopes = line(DM, [source[rows(i, j)] for i in range(8)])
        back = line(DM.T, [weigh[rows(i, j)] * slopes[i] for i in range(8)])
        for i in range(8):
            r = rows(i, j)
            target[r] = carry_ref[0, r] * slopes[i] + back[i]


def forward_jk(carry_ref, weigh, turned_ref, slope, target):
    fluxes = weigh[...] * slope[0], weigh[...] * slope[1]
    carried = carry_ref[2] * slope[0] + carry_ref[1] * slope[1]
    target[...] = target[...] + (carried + back_jk(turned_ref, *fluxes))


def adjoint_i(source, base, carry_ref, weigh, target):
    for j in range(8):
        these = [rows(i, j) for i in range(8)]
        values = [source[r] for r in these]
        slopes = line(DM, values)
        fluxes = [carry_ref[0, r] * v + weigh[r] * g for r, v, g in zip(these, values, slopes)]
        for r, back in zip(these, line(DM.T, fluxes)):
            target[r] = base[r] - back


def adjoint_jk(source, carry_ref, weigh, turned_ref, slope, target):
    flux_k = carry_ref[2] * source[...] + weigh[...] * slope[0]
    flux_j = carry_ref[1] * source[...] + weigh[...] * slope[1]
    target[...] = target[...] - back_jk(turned_ref, flux_k, flux_j)


def forward(sources, carry_ref, weigh_ref, table_ref, turned_ref, slope_ref, target, finish):
    set_slopes(sources.at[0], table_ref, slope_ref.at[0])
    for f in range(3):
        at = (carry_ref, weigh_ref.at[f])
        forward_i(sources.at[f], *at, target.at[f])
        if f < 2:
            set_slopes(sources.at[f + 1], table_ref, slope_ref.at[f + 1])
        forward_jk(*at, turned_ref, slope_ref.at[f], target.at[f])
        finish(f)


def adjoint(sources, base, carry_ref, weigh_ref, table_ref, turned_ref, slope_ref, target, finish):
    set_slopes(sources.at[0], table_ref, slope_ref.at[0])
    for f in range(3):
        at = (carry_ref, weigh_ref.at[f])
        adjoint_i(sources.at[f], base.at[f], *at, target.at[f])
        if f < 2:
            set_slopes(sources.at[f + 1], table_ref, slope_ref.at[f + 1])
        adjoint_jk(sources.at[f], *at, turned_ref, slope_ref.at[f], target.at[f])
        finish(f)


def join_heights(ref, index):
    height, _, below, above = index
    lower = ref[pl.ds(0, 64, stride=8)]
    upper = ref[pl.ds(7, 64, stride=8)]
    tall = jnp.broadcast_to(height[None], (8, 8, 128)).reshape(64, 128)
    ref[pl.ds(0, 64, stride=8)] = lower + jnp.where(tall > 0, lanes(upper, below), 0.0)
    ref[pl.ds(7, 64, stride=8)] = upper + jnp.where(tall < 127, lanes(lower, above), 0.0)


def face_rows(ends, axis, way, k):
    end = ends[axis][way]
    return pl.ds(end * 8 + k, 8, stride=64) if axis else pl.ds(end * 64 + k, 8, stride=8)


def tile(c, k):
    return pl.ds((7 * c + k) * 8, 8)


def top_tile(ref):
    return pl.ds(ref.shape[0] - 8, 8)


def send_faces(c, ref, index, ends, out):
    inverse = index[1]
    top = jnp.broadcast_to(inverse[:, 127:], (8, 128))
    lane = lax.broadcasted_iota(jnp.int32, (8, 128), 1)
    for axis in range(2):
        for way in range(2):
            face = out[2 * axis + way]
            for k in range(7):
                face[tile(c, k)] = lanes(ref[face_rows(ends, axis, way, k)], inverse)
            last = lanes(ref[face_rows(ends, axis, way, 7)], top)
            others = face[top_tile(face)] if c else jnp.zeros((8, 128), F32)
            face[top_tile(face)] = jnp.where(lane == c, last, others)


def take_faces(c, index, ends, got, spread_ref, axes=(0, 1)):
    height = index[0]
    above = (height + 1) & 127
    own = jnp.full((8, 128), c, jnp.int32)
    for axis in axes:
        for way in range(2):
            face = got[3 - way if axis else way]
            last = jnp.where(
                height < 127, lanes(face[tile(c, 0)], above), lanes(face[top_tile(face)], own)
            )
            parts = [lanes(face[tile(c, k)], height) for k in range(7)] + [last]
            slot = 2 * axis + jnp.minimum(ends[axis][way], 1)
            for k, part in enumerate(parts):
                spread_ref[c, slot, pl.ds(8 * k, 8)] = part * ends[2][axis] if way else part


def assembled(c, i, j, joined, spread_ref, axes=(0, 1)):
    total = joined[rows(i, j)]
    for axis, (end, place) in enumerate(((i, j), (j, i))):
        if end in (0, 7) and axis in axes:
            total = total + spread_ref[c, 2 * axis + end // 7, pl.ds(place, 8, stride=8)]
    return total


def ends_of(columns):
    column = lax.rem(lax.axis_index("elem") + columns // 2, columns * DA)
    row, place = lax.div(column, columns), lax.rem(column, columns)
    row_odd, place_odd = lax.rem(row, 2), lax.rem(place, 2)
    row_inside = jnp.where((row > 0) & (row < DA - 1), 1.0, 0.0)
    place_inside = jnp.where((place > 0) & (place < columns - 1), 1.0, 0.0)
    return (
        (7 - 7 * row_odd, 7 * row_odd),
        (7 - 7 * place_odd, 7 * place_odd),
        (row_inside, place_inside),
    )


def index_of(index_ref):
    return tuple(index_ref[n] for n in range(4))


def index_kernel(
    columns,
    moment_far,
    state_far,
    flow_far,
    weight_far,
    diff_far,
    numbers_far,
    moment_ref,
    state_ref,
    carry_ref,
    weigh_ref,
    table_ref,
    turned_ref,
    index_ref,
    joined_ref,
    ie_ref,
    io_ref,
    je_ref,
    jo_ref,
    weight_ref,
    mass_ref,
    flow_ref,
    numbers_ref,
    diff_ref,
    arrived,
):
    far = (numbers_far, weight_far, state_far, diff_far, moment_far, flow_far)
    near = (numbers_ref, weight_ref, state_ref, diff_ref, moment_ref, flow_ref)
    copies = [pltpu.make_async_copy(a, b, arrived.at[n]) for n, (a, b) in enumerate(zip(far, near))]
    for copy in copies:
        copy.start()
    for axis in range(2):
        write_table(DM, axis, table_ref, 128 * axis, 0)
        write_table(DM.T, axis, turned_ref, 0, 384 * axis)
    ends = ends_of(columns)
    copies[0].wait()
    height = jnp.broadcast_to(numbers_ref[...] & 127, (8, 128))
    square = jnp.broadcast_to(height[:1].astype(F32), (128, 128)).T
    lane = lax.broadcasted_iota(jnp.int32, (128, 128), 1).astype(F32)
    row = lax.broadcasted_iota(jnp.int32, (128, 128), 0).astype(F32)
    inverse = jnp.sum(jnp.where(square == lane, row, 0.0), axis=0, keepdims=True)
    inverse = jnp.broadcast_to(inverse, (8, 128)).astype(jnp.int32)
    index = (
        height,
        inverse,
        lanes(inverse, (height - 1) & 127),
        lanes(inverse, (height + 1) & 127),
    )
    for n in range(4):
        index_ref[n] = index[n]
    copies[1].wait()
    set_mass(weight_ref, mass_ref)
    joined_ref[3] = mass_ref[...]
    copies[2].wait()
    out = (ie_ref, io_ref, je_ref, jo_ref)
    for c in range(3):
        joined_ref[c] = state_ref[c]
    for c in range(4):
        join_heights(joined_ref.at[c], index)
        send_faces(c, joined_ref.at[c], index, ends, out)
    copies[3].wait()
    for f in range(3):
        weigh_ref[f] = mass_ref[...] * (DT * diff_ref[f])
    copies[5].wait()
    for d in range(3):
        carry_ref[d] = mass_ref[...] * (DT * flow_ref[d])
    copies[4].wait()


def moment_kernel(
    columns,
    moment_ref,
    carry_ref,
    weigh_ref,
    table_ref,
    turned_ref,
    index_ref,
    joined_ref,
    ie_ref,
    io_ref,
    je_ref,
    jo_ref,
    slope_ref,
):
    ends = ends_of(columns)
    index = index_of(index_ref)
    out = (ie_ref, io_ref, je_ref, jo_ref)

    def finish(f):
        join_heights(joined_ref.at[f], index)
        send_faces(f, joined_ref.at[f], index, ends, out)

    at = (carry_ref, weigh_ref, table_ref, turned_ref, slope_ref)
    forward(moment_ref, *at, joined_ref, finish)


def edge_kernel(columns, way, ie_ref, io_ref, face, *refs):
    ends, out = ends_of(columns), refs[-1]
    out[...] = face[...]
    tiles = face.shape[0] // 8
    r = pl.ds(ends[1][way], tiles, stride=8)
    for other, got in enumerate((ie_ref, io_ref)):
        w = pl.ds(ends[0][other], tiles, stride=8)
        part = got[r]
        out[w] = out[w] + (part * ends[2][0] if other else part)


def state_kernel(
    columns,
    first,
    state_ref,
    carry_ref,
    weigh_ref,
    table_ref,
    turned_ref,
    index_ref,
    joined_ref,
    *refs,
):
    ends = ends_of(columns)
    index = index_of(index_ref)
    if first:
        got, (inverse_ref, state_out, joined_out), refs = refs[:4], refs[4:7], refs[7:]
        out, (slope_ref, hold_ref, spread_ref) = refs[:4], refs[4:]
        take_faces(3, index, ends, got, spread_ref)
        for i in range(8):
            for j in range(8):
                inverse_ref[rows(i, j)] = 1.0 / assembled(3, i, j, joined_ref.at[3], spread_ref)
    else:
        inverse_ref, *got = refs[:5]
        state_far, token_ref, slope_ref, hold_ref, spread_ref, state_out, sent = refs[5:]
        token_ref[...] = jnp.zeros_like(token_ref)
    for f in range(3):
        take_faces(f, index, ends, got, spread_ref)
        for i in range(8):
            for j in range(8):
                total = assembled(f, i, j, joined_ref.at[f], spread_ref)
                hold_ref[f, rows(i, j)] = total * inverse_ref[rows(i, j)]

    def finish(f):
        if first:
            joined_out[f] = state_out[f]
            join_heights(joined_out.at[f], index)
            send_faces(f, joined_out.at[f], index, ends, out)
        else:
            send_out(f, state_out, state_far, sent).start()

    at = (carry_ref, weigh_ref, table_ref, turned_ref, slope_ref)
    adjoint(hold_ref, state_ref, *at, state_out, finish)
    if not first:
        for f in range(3):
            send_out(f, state_out, state_far, sent).wait()


def send_out(f, near, far, sent):
    return pltpu.make_async_copy(near.at[f], far.at[f], sent.at[f])


def moment_step(f, ends, index, moment_ref, joined_ref, inverse_ref, got, spread_ref, moment_out):
    take_faces(f, index, ends, got, spread_ref)
    for i in range(8):
        for j in range(8):
            r = rows(i, j)
            total = assembled(f, i, j, joined_ref.at[f], spread_ref)
            moment_out[f, r] = moment_ref[f, r] - total * inverse_ref[r]


def middle_kernel(
    columns,
    moment_ref,
    carry_ref,
    weigh_ref,
    table_ref,
    turned_ref,
    index_ref,
    inverse_ref,
    joined_ref,
    gie_ref,
    gio_ref,
    gjo_ref,
    gje_ref,
    moment_out,
    joined_out,
    ie_ref,
    io_ref,
    je_ref,
    jo_ref,
    slope_ref,
    spread_ref,
):
    ends = ends_of(columns)
    index = index_of(index_ref)
    out = (ie_ref, io_ref, je_ref, jo_ref)
    got = (gie_ref, gio_ref, gjo_ref, gje_ref)
    for f in range(3):
        moment_step(f, ends, index, moment_ref, joined_ref, inverse_ref, got, spread_ref, moment_out)

    def finish(f):
        join_heights(joined_out.at[f], index)
        send_faces(f, joined_out.at[f], index, ends, out)

    at = (carry_ref, weigh_ref, table_ref, turned_ref, slope_ref)
    forward(moment_out, *at, joined_out, finish)


def inner_kernel(
    columns,
    moment_ref,
    index_ref,
    inverse_ref,
    joined_ref,
    gie_ref,
    gio_ref,
    token_ref,
    moment_far,
    moment_out,
    spread_ref,
    sent,
):
    ends = ends_of(columns)
    index = index_of(index_ref)
    for f in range(3):
        take_faces(f, index, ends, (gie_ref, gio_ref), spread_ref, (0,))
        for i in range(8):
            for j in range(8):
                r = rows(i, j)
                total = assembled(f, i, j, joined_ref.at[f], spread_ref, (0,))
                moment_out[f, i, j] = moment_ref[f, r] - total * inverse_ref[r]
        send_out(f, moment_out, moment_far, sent).start()
    for f in range(3):
        send_out(f, moment_out, moment_far, sent).wait()


def outer_kernel(
    columns,
    inner_far,
    moment_ref,
    index_ref,
    inverse_ref,
    gjo_ref,
    gje_ref,
    moment_far,
    spread_ref,
    rows_ref,
    sent,
):
    ends = ends_of(columns)
    index = index_of(index_ref)
    got = (None, None, gjo_ref, gje_ref)
    copies = []
    for f in range(3):
        take_faces(f, index, ends, got, spread_ref, (1,))
        for end in range(2):
            for i in range(8):
                part = spread_ref[f, 2 + end, pl.ds(i, 8, stride=8)]
                kept = moment_ref[f, i, 7 * end]
                rows_ref[f, end, i] = kept - part * inverse_ref[rows(i, 7 * end)]
            copy = pltpu.make_async_copy(
                rows_ref.at[f, end], moment_far.at[f, :, 7 * end], sent.at[2 * f + end]
            )
            copy.start()
            copies.append(copy)
    for copy in copies:
        copy.wait()


VMEM = pl.BlockSpec(memory_space=pltpu.VMEM)
FAR = pl.BlockSpec(memory_space=pltpu.HBM)


def call(kernel, specs, shapes, scratch, flops, *operands, first_out=VMEM, aliases={}):
    moved = sum(o.size * 4 for o in operands) + sum(int(np.prod(s)) * 4 for s, _ in shapes)
    return pl.pallas_call(
        kernel,
        out_shape=[jax.ShapeDtypeStruct(s, t) for s, t in shapes],
        in_specs=specs,
        out_specs=[first_out] + [VMEM] * (len(shapes) - 1),
        scratch_shapes=scratch,
        input_output_aliases=aliases,
        compiler_params=pltpu.CompilerParams(vmem_limit_bytes=32 * 1024 * 1024),
        cost_estimate=pl.CostEstimate(flops=flops, bytes_accessed=moved, transcendentals=0),
    )(*operands)


def pairings(devices):
    columns = devices // DA
    device = lambda row, place: (row % DA * columns + place - columns // 2) % devices

    def both(pairs):
        return pairs + [(b, a) for a, b in pairs]

    places, halves = range(columns), range(0, columns, 2)
    along_i = [
        [(device(r, s), device(r + 1, s)) for r in range(0, DA, 2) for s in places],
        [(device(r, s), device(r + 1, s)) for r in range(1, DA - 1, 2) for s in places]
        + [(device(r, s), device(r, s + 1)) for r in (0, DA - 1) for s in halves],
    ]
    along_j = [
        [(device(r, s), device(r, s + 1)) for r in range(DA) for s in halves],
        [(device(r, s - 1), device(r, s)) for r in range(DA) for s in halves if s]
        + [(device(r, columns - 1), device(r + 1, 0)) for r in range(DA)],
    ]
    return [both(p) for p in along_i], [both(p) for p in along_j]


def shards(moment_fields, adjoint_fields, velocity, mass_weights, diffusivity, numbering):
    devices = lax.axis_size("elem")
    columns = devices // DA
    along_i, along_j = pairings(devices)
    whole, block = ((3, 512, 128), F32), ((512, 128), F32)
    work = pltpu.VMEM((3, 512, 128), F32)
    slopes = pltpu.VMEM((3, 2, 512, 128), F32)

    def spread(count):
        return pltpu.VMEM((count, 4, 64, 128), F32)

    def exchange(block, pairs):
        return lax.ppermute(block, "elem", pairs)

    def settle(block, *after):
        anywhere = pl.BlockSpec(memory_space=pl.ANY)
        return pl.pallas_call(
            lambda *refs: None,
            out_shape=jax.ShapeDtypeStruct(block.shape, block.dtype),
            in_specs=[anywhere] * (1 + len(after)),
            out_specs=anywhere,
            input_output_aliases={0: 0},
            compiler_params=pltpu.CompilerParams(vmem_limit_bytes=1024 * 1024),
        )(block, *after)

    def edge(count, way, *operands):
        return call(
            functools.partial(edge_kernel, columns, way),
            [VMEM] * len(operands),
            [(face_shape(count), F32)],
            [],
            count * 64 * 128,
            *operands,
        )[0]

    def meet(count, faces):
        got_i = [exchange(faces[way], along_i[way]) for way in range(2)]
        far_face = edge(count, 1, *got_i, faces[3])
        near_face = edge(count, 0, *got_i, faces[2], far_face)
        return got_i + [exchange(far_face, along_j[1]), exchange(near_face, along_j[0])]

    def settled(got, *after):
        return got[:2] + [settle(got[2], *after), got[3]]

    def far(array):
        return pltpu.with_memory_space_constraint(array, pltpu.HBM)

    def face_shape(count):
        return ((7 * count + 1) * 8, 128)

    def faces_shape(count):
        return [(face_shape(count), F32)] * 4

    moment, state, carry, weigh, table, turned, index, joined_state, *faces_state = call(
        functools.partial(index_kernel, columns),
        [FAR] * 6,
        [whole] * 4
        + [((256, 384), BF16), ((128, 768), BF16)]
        + [((4, 8, 128), jnp.int32), ((4, 512, 128), F32)]
        + faces_shape(4),
        [
            pltpu.VMEM((512, 128), F32),
            pltpu.VMEM((512, 128), F32),
            work,
            pltpu.VMEM((1, 128), jnp.int32),
            pltpu.SMEM((3,), F32),
            pltpu.SemaphoreType.DMA((6,)),
        ],
        1_000_000,
        *map(far, (moment_fields, adjoint_fields, velocity, mass_weights)),
        *map(far, (diffusivity, numbering.reshape(1, 128))),
    )
    tables = (carry, weigh, table, turned, index)
    got_state = meet(4, faces_state)
    joined_moment, *faces_moment = call(
        functools.partial(moment_kernel, columns),
        [VMEM] * 6,
        [whole] + faces_shape(3),
        [slopes],
        20_000_000,
        moment,
        *tables,
    )
    got_moment = meet(3, faces_moment)
    inverse, state, joined_state, *faces_state = call(
        functools.partial(state_kernel, columns, True),
        [VMEM] * 11,
        [block, whole, whole] + faces_shape(3),
        [slopes, work, spread(4)],
        20_000_000,
        state,
        *tables,
        joined_state,
        *settled(got_state),
    )
    got_state = meet(3, faces_state)
    moment, joined_moment, *faces_moment = call(
        functools.partial(middle_kernel, columns),
        [VMEM] * 12,
        [whole, whole] + faces_shape(3),
        [slopes, spread(3)],
        20_000_000,
        moment,
        *tables,
        inverse,
        joined_moment,
        *settled(got_moment, inverse),
    )
    got_moment = meet(3, faces_moment)
    state, token = call(
        functools.partial(state_kernel, columns, False),
        [VMEM] * 12,
        [whole, ((8, 128), F32)],
        [slopes, work, spread(3), work] + [pltpu.SemaphoreType.DMA((3,))],
        20_000_000,
        state,
        *tables,
        joined_state,
        inverse,
        *settled(got_state),
        first_out=FAR,
    )
    cube = ((3, 8, 8, 8, 128), F32)
    inner, kept = call(
        functools.partial(inner_kernel, columns),
        [VMEM] * 7,
        [cube, cube],
        [spread(3), pltpu.SemaphoreType.DMA((3,))],
        1_000_000,
        moment,
        index,
        inverse,
        joined_moment,
        *got_moment[:2],
        token,
        first_out=FAR,
    )
    far_face, near_face = got_moment[2:]
    (moment,) = call(
        functools.partial(outer_kernel, columns),
        [FAR] + [VMEM] * 5,
        [cube],
        [
            spread(3),
            pltpu.VMEM((3, 2, 8, 8, 128), F32),
            pltpu.SemaphoreType.DMA((6,)),
        ],
        1_000_000,
        far(inner),
        kept,
        index,
        inverse,
        settle(far_face, kept),
        near_face,
        first_out=FAR,
        aliases={0: 0},
    )
    moment = moment.reshape(whole[0])
    return moment, state


def solution(mesh):
    in_specs = (
        P(None, None, "elem"),
        P(None, None, "elem"),
        P(None, None, "elem"),
        P(None, "elem"),
        P(),
        P("elem"),
    )
    out_specs = (P(None, None, "elem"), P(None, None, "elem"))
    return jax.shard_map(shards, mesh=mesh, in_specs=in_specs, out_specs=out_specs, check_vma=False)
```

```python
import functools

import jax
import jax.numpy as jnp
import numpy as np
from jax import lax
from jax.experimental import pallas as pl
from jax.experimental.pallas import tpu as pltpu
from jax.sharding import PartitionSpec as P

DA = 4
DT = 0.001
F32 = jnp.float32
BF16 = jnp.bfloat16


def gll_tables():
    points = [
        -1.0,
        -0.8717401485096066,
        -0.5917001814331423,
        -0.2092992179024789,
        0.2092992179024789,
        0.5917001814331423,
        0.8717401485096066,
        1.0,
    ]
    weights = [
        0.03571428571428571,
        0.21070422714350603,
        0.3411226924835044,
        0.4124587946587038,
        0.4124587946587038,
        0.3411226924835044,
        0.21070422714350603,
        0.03571428571428571,
    ]
    barycentric = []
    for left_index in range(8):
        product = 1.0
        for right_index in range(8):
            if right_index != left_index:
                product = product * (points[left_index] - points[right_index])
        barycentric.append(1.0 / product)
    derivative = np.zeros((8, 8))
    for left_index in range(8):
        row_total = 0.0
        for right_index in range(8):
            if left_index != right_index:
                entry = (
                    barycentric[right_index]
                    / barycentric[left_index]
                    / (points[left_index] - points[right_index])
                )
                derivative[left_index, right_index] = entry
                row_total = row_total + entry
        derivative[left_index, left_index] = -row_total
    return derivative, np.asarray(weights)


DM, WEIGHTS = gll_tables()


def line(table, values):
    sums = [values[q] + values[7 - q] for q in range(4)]
    differences = [values[q] - values[7 - q] for q in range(4)]
    out = [None] * 8
    for i in range(4):
        even = odd = None
        for q in range(4):
            on_sum = float(table[i, q] + table[i, 7 - q]) / 2
            on_difference = float(table[i, q] - table[i, 7 - q]) / 2
            even = sums[q] * on_sum if even is None else even + sums[q] * on_sum
            odd = (
                differences[q] * on_difference
                if odd is None
                else odd + differences[q] * on_difference
            )
        out[i] = odd + even
        out[7 - i] = odd - even
    return out


def rows(i, j):
    return pl.ds((8 * i + j) * 8, 8)


def split(block):
    wide = jnp.concatenate([block[128 * n : 128 * (n + 1)] for n in range(4)], axis=1)
    high = wide.astype(BF16)
    low = (wide - high.astype(F32)).astype(BF16)
    return [high, high, low]


def tall(wide):
    return jnp.concatenate([wide[:, 128 * n : 128 * (n + 1)] for n in range(4)], axis=0)


def slopes_jk(table_ref, block):
    parts = jnp.concatenate(split(block), axis=0)
    out = jnp.dot(table_ref[...], parts, preferred_element_type=F32)
    return tall(out[:128]), tall(out[128:])


def back_jk(turned_ref, flux_k, flux_j):
    parts = jnp.concatenate(split(flux_k) + split(flux_j), axis=0)
    return tall(jnp.dot(turned_ref[...], parts, preferred_element_type=F32))


def write_table(table, axis, table_ref, start, column):
    sub = lax.broadcasted_iota(jnp.int32, (8, 128), 0)
    lane = lax.broadcasted_iota(jnp.int32, (8, 128), 1)
    zero = jnp.zeros((8, 128), F32)
    place = lax.shift_right_logical(lane, 3)
    entry = place & 7 if axis else lane & 7
    bases = []
    for n in range(8):
        one_row = zero
        for q in range(8):
            one_row = jnp.where(entry == q, float(table[n, q]), one_row)
        bases.append(one_row)
    if axis:
        bases = [jnp.where((lane & 7) == sub, one_row, zero) for one_row in bases]
        place = lax.shift_right_logical(lane, 6)
    else:
        base = zero
        for n in range(8):
            base = jnp.where(sub == n, bases[n], base)
        bases = [base]
    highs = [base.astype(BF16).astype(F32) for base in bases]
    lows = [base - high for base, high in zip(bases, highs)]
    for a in range(0, 16, 2):
        parts = []
        for values in (highs, lows):
            pair = []
            for block in (a, a + 1):
                own = place == (block // 8 if axis else block)
                pair.append(jnp.where(own, values[block % 8 if axis else 0], zero))
            parts.append(jnp.concatenate(pair, axis=0))
        wide = jnp.concatenate([parts[0], parts[1], parts[0]], axis=1)
        table_ref[pl.ds(start + 8 * a, 16), column : column + 384] = wide.astype(BF16)


def lanes(block, index):
    wide = jnp.broadcast_to(index[None], (block.shape[0] // 8, 8, 128)).reshape(block.shape)
    return jnp.take_along_axis(block, wide, axis=1, mode="promise_in_bounds")


def set_mass(weight_ref, mass_ref):
    sub = lax.broadcasted_iota(jnp.int32, (8, 128), 0)
    along = jnp.zeros((8, 128), F32)
    for k in range(8):
        along = jnp.where(sub == k, float(WEIGHTS[k]), along)
    for i in range(8):
        for j in range(8):
            r = rows(i, j)
            mass_ref[r] = weight_ref[r] * (along * float(WEIGHTS[i] * WEIGHTS[j]))


def set_slopes(source, table_ref, slope):
    slope[0], slope[1] = slopes_jk(table_ref, source[...])


def forward_i(source, carry_ref, weigh, target):
    for j in range(8):
        slopes = line(DM, [source[rows(i, j)] for i in range(8)])
        back = line(DM.T, [weigh[rows(i, j)] * slopes[i] for i in range(8)])
        for i in range(8):
            r = rows(i, j)
            target[r] = carry_ref[0, r] * slopes[i] + back[i]


def forward_jk(carry_ref, weigh, turned_ref, slope, target):
    fluxes = weigh[...] * slope[0], weigh[...] * slope[1]
    carried = carry_ref[2] * slope[0] + carry_ref[1] * slope[1]
    target[...] = target[...] + (carried + back_jk(turned_ref, *fluxes))


def adjoint_i(source, base, carry_ref, weigh, target):
    for j in range(8):
        these = [rows(i, j) for i in range(8)]
        values = [source[r] for r in these]
        slopes = line(DM, values)
        fluxes = [carry_ref[0, r] * v + weigh[r] * g for r, v, g in zip(these, values, slopes)]
        for r, back in zip(these, line(DM.T, fluxes)):
            target[r] = base[r] - back


def adjoint_jk(source, carry_ref, weigh, turned_ref, slope, target):
    flux_k = carry_ref[2] * source[...] + weigh[...] * slope[0]
    flux_j = carry_ref[1] * source[...] + weigh[...] * slope[1]
    target[...] = target[...] - back_jk(turned_ref, flux_k, flux_j)


def forward(sources, carry_ref, weigh_ref, table_ref, turned_ref, slope_ref, target, finish):
    set_slopes(sources.at[0], table_ref, slope_ref.at[0])
    for f in range(3):
        at = (carry_ref, weigh_ref.at[f])
        forward_i(sources.at[f], *at, target.at[f])
        if f < 2:
            set_slopes(sources.at[f + 1], table_ref, slope_ref.at[f + 1])
        forward_jk(*at, turned_ref, slope_ref.at[f], target.at[f])
        finish(f)


def adjoint(sources, base, carry_ref, weigh_ref, table_ref, turned_ref, slope_ref, target, finish):
    set_slopes(sources.at[0], table_ref, slope_ref.at[0])
    for f in range(3):
        at = (carry_ref, weigh_ref.at[f])
        adjoint_i(sources.at[f], base.at[f], *at, target.at[f])
        if f < 2:
            set_slopes(sources.at[f + 1], table_ref, slope_ref.at[f + 1])
        adjoint_jk(sources.at[f], *at, turned_ref, slope_ref.at[f], target.at[f])
        finish(f)


def join_heights(ref, index):
    height, _, below, above = index
    lower = ref[pl.ds(0, 64, stride=8)]
    upper = ref[pl.ds(7, 64, stride=8)]
    tall = jnp.broadcast_to(height[None], (8, 8, 128)).reshape(64, 128)
    ref[pl.ds(0, 64, stride=8)] = lower + jnp.where(tall > 0, lanes(upper, below), 0.0)
    ref[pl.ds(7, 64, stride=8)] = upper + jnp.where(tall < 127, lanes(lower, above), 0.0)


def face_rows(ends, axis, way, k):
    end = ends[axis][way]
    return pl.ds(end * 8 + k, 8, stride=64) if axis else pl.ds(end * 64 + k, 8, stride=8)


def tile(c, k):
    return pl.ds((7 * c + k) * 8, 8)


def top_tile(ref):
    return pl.ds(ref.shape[0] - 8, 8)


def send_faces(c, ref, index, ends, out):
    inverse = index[1]
    top = jnp.broadcast_to(inverse[:, 127:], (8, 128))
    lane = lax.broadcasted_iota(jnp.int32, (8, 128), 1)
    for axis in range(2):
        for way in range(2):
            face = out[2 * axis + way]
            for k in range(7):
                face[tile(c, k)] = lanes(ref[face_rows(ends, axis, way, k)], inverse)
            last = lanes(ref[face_rows(ends, axis, way, 7)], top)
            others = face[top_tile(face)] if c else jnp.zeros((8, 128), F32)
            face[top_tile(face)] = jnp.where(lane == c, last, others)


def take_faces(c, index, ends, got, spread_ref, axes=(0, 1)):
    height = index[0]
    above = (height + 1) & 127
    own = jnp.full((8, 128), c, jnp.int32)
    for axis in axes:
        for way in range(2):
            face = got[3 - way if axis else way]
            last = jnp.where(
                height < 127, lanes(face[tile(c, 0)], above), lanes(face[top_tile(face)], own)
            )
            parts = [lanes(face[tile(c, k)], height) for k in range(7)] + [last]
            slot = 2 * axis + jnp.minimum(ends[axis][way], 1)
            for k, part in enumerate(parts):
                spread_ref[c, slot, pl.ds(8 * k, 8)] = part * ends[2][axis] if way else part


def assembled(c, i, j, joined, spread_ref, axes=(0, 1)):
    total = joined[rows(i, j)]
    for axis, (end, place) in enumerate(((i, j), (j, i))):
        if end in (0, 7) and axis in axes:
            total = total + spread_ref[c, 2 * axis + end // 7, pl.ds(place, 8, stride=8)]
    return total


def ends_of(columns):
    column = lax.rem(lax.axis_index("elem") + columns // 2, columns * DA)
    row, place = lax.div(column, columns), lax.rem(column, columns)
    row_odd, place_odd = lax.rem(row, 2), lax.rem(place, 2)
    row_inside = jnp.where((row > 0) & (row < DA - 1), 1.0, 0.0)
    place_inside = jnp.where((place > 0) & (place < columns - 1), 1.0, 0.0)
    return (
        (7 - 7 * row_odd, 7 * row_odd),
        (7 - 7 * place_odd, 7 * place_odd),
        (row_inside, place_inside),
    )


def index_of(index_ref):
    return tuple(index_ref[n] for n in range(4))


def index_kernel(
    columns,
    moment_far,
    state_far,
    weight_far,
    diff_far,
    numbers_far,
    moment_ref,
    state_ref,
    mass_ref,
    weigh_ref,
    table_ref,
    turned_ref,
    index_ref,
    joined_ref,
    ie_ref,
    io_ref,
    je_ref,
    jo_ref,
    weight_ref,
    numbers_ref,
    diff_ref,
    arrived,
):
    far = (numbers_far, weight_far, state_far, diff_far, moment_far)
    near = (numbers_ref, weight_ref, state_ref, diff_ref, moment_ref)
    copies = [pltpu.make_async_copy(a, b, arrived.at[n]) for n, (a, b) in enumerate(zip(far, near))]
    for copy in copies:
        copy.start()
    for axis in range(2):
        write_table(DM, axis, table_ref, 128 * axis, 0)
        write_table(DM.T, axis, turned_ref, 0, 384 * axis)
    ends = ends_of(columns)
    copies[0].wait()
    height = jnp.broadcast_to(numbers_ref[...] & 127, (8, 128))
    square = jnp.broadcast_to(height[:1].astype(F32), (128, 128)).T
    lane = lax.broadcasted_iota(jnp.int32, (128, 128), 1).astype(F32)
    row = lax.broadcasted_iota(jnp.int32, (128, 128), 0).astype(F32)
    inverse = jnp.sum(jnp.where(square == lane, row, 0.0), axis=0, keepdims=True)
    inverse = jnp.broadcast_to(inverse, (8, 128)).astype(jnp.int32)
    index = (
        height,
        inverse,
        lanes(inverse, (height - 1) & 127),
        lanes(inverse, (height + 1) & 127),
    )
    for n in range(4):
        index_ref[n] = index[n]
    copies[1].wait()
    set_mass(weight_ref, mass_ref)
    joined_ref[3] = mass_ref[...]
    copies[2].wait()
    out = (ie_ref, io_ref, je_ref, jo_ref)
    for c in range(3):
        joined_ref[c] = state_ref[c]
    for c in range(4):
        join_heights(joined_ref.at[c], index)
        send_faces(c, joined_ref.at[c], index, ends, out)
    copies[3].wait()
    for f in range(3):
        weigh_ref[f] = mass_ref[...] * (DT * diff_ref[f])
    copies[4].wait()


def moment_kernel(
    columns,
    moment_ref,
    flow_ref,
    mass_ref,
    weigh_ref,
    table_ref,
    turned_ref,
    index_ref,
    carry_ref,
    joined_ref,
    ie_ref,
    io_ref,
    je_ref,
    jo_ref,
    slope_ref,
):
    ends = ends_of(columns)
    index = index_of(index_ref)
    out = (ie_ref, io_ref, je_ref, jo_ref)
    for d in range(3):
        carry_ref[d] = mass_ref[...] * (DT * flow_ref[d])

    def finish(f):
        join_heights(joined_ref.at[f], index)
        send_faces(f, joined_ref.at[f], index, ends, out)

    at = (carry_ref, weigh_ref, table_ref, turned_ref, slope_ref)
    forward(moment_ref, *at, joined_ref, finish)


def edge_kernel(columns, way, ie_ref, io_ref, face, *refs):
    ends, out = ends_of(columns), refs[-1]
    out[...] = face[...]
    tiles = face.shape[0] // 8
    r = pl.ds(ends[1][way], tiles, stride=8)
    for other, got in enumerate((ie_ref, io_ref)):
        w = pl.ds(ends[0][other], tiles, stride=8)
        part = got[r]
        out[w] = out[w] + (part * ends[2][0] if other else part)


def state_kernel(
    columns,
    first,
    state_ref,
    carry_ref,
    weigh_ref,
    table_ref,
    turned_ref,
    index_ref,
    joined_ref,
    *refs,
):
    ends = ends_of(columns)
    index = index_of(index_ref)
    if first:
        got, (inverse_ref, state_out, joined_out), refs = refs[:4], refs[4:7], refs[7:]
        out, (slope_ref, hold_ref, spread_ref) = refs[:4], refs[4:]
        take_faces(3, index, ends, got, spread_ref)
        for i in range(8):
            for j in range(8):
                inverse_ref[rows(i, j)] = 1.0 / assembled(3, i, j, joined_ref.at[3], spread_ref)
    else:
        inverse_ref, *got = refs[:5]
        state_far, token_ref, slope_ref, hold_ref, spread_ref, state_out, sent = refs[5:]
        token_ref[...] = jnp.zeros_like(token_ref)
    for f in range(3):
        take_faces(f, index, ends, got, spread_ref)
        for i in range(8):
            for j in range(8):
                total = assembled(f, i, j, joined_ref.at[f], spread_ref)
                hold_ref[f, rows(i, j)] = total * inverse_ref[rows(i, j)]

    def finish(f):
        if first:
            joined_out[f] = state_out[f]
            join_heights(joined_out.at[f], index)
            send_faces(f, joined_out.at[f], index, ends, out)
        else:
            send_out(f, state_out, state_far, sent).start()

    at = (carry_ref, weigh_ref, table_ref, turned_ref, slope_ref)
    adjoint(hold_ref, state_ref, *at, state_out, finish)
    if not first:
        for f in range(3):
            send_out(f, state_out, state_far, sent).wait()


def send_out(f, near, far, sent):
    return pltpu.make_async_copy(near.at[f], far.at[f], sent.at[f])


def moment_step(f, ends, index, moment_ref, joined_ref, inverse_ref, got, spread_ref, moment_out):
    take_faces(f, index, ends, got, spread_ref)
    for i in range(8):
        for j in range(8):
            r = rows(i, j)
            total = assembled(f, i, j, joined_ref.at[f], spread_ref)
            moment_out[f, r] = moment_ref[f, r] - total * inverse_ref[r]


def middle_kernel(
    columns,
    moment_ref,
    carry_ref,
    weigh_ref,
    table_ref,
    turned_ref,
    index_ref,
    inverse_ref,
    joined_ref,
    gie_ref,
    gio_ref,
    gjo_ref,
    gje_ref,
    moment_out,
    joined_out,
    ie_ref,
    io_ref,
    je_ref,
    jo_ref,
    slope_ref,
    spread_ref,
):
    ends = ends_of(columns)
    index = index_of(index_ref)
    out = (ie_ref, io_ref, je_ref, jo_ref)
    got = (gie_ref, gio_ref, gjo_ref, gje_ref)
    for f in range(3):
        moment_step(f, ends, index, moment_ref, joined_ref, inverse_ref, got, spread_ref, moment_out)

    def finish(f):
        join_heights(joined_out.at[f], index)
        send_faces(f, joined_out.at[f], index, ends, out)

    at = (carry_ref, weigh_ref, table_ref, turned_ref, slope_ref)
    forward(moment_out, *at, joined_out, finish)


def inner_kernel(
    columns,
    moment_ref,
    index_ref,
    inverse_ref,
    joined_ref,
    gie_ref,
    gio_ref,
    token_ref,
    moment_far,
    moment_out,
    spread_ref,
    sent,
):
    ends = ends_of(columns)
    index = index_of(index_ref)
    for f in range(3):
        take_faces(f, index, ends, (gie_ref, gio_ref), spread_ref, (0,))
        for i in range(8):
            for j in range(8):
                r = rows(i, j)
                total = assembled(f, i, j, joined_ref.at[f], spread_ref, (0,))
                moment_out[f, i, j] = moment_ref[f, r] - total * inverse_ref[r]
        send_out(f, moment_out, moment_far, sent).start()
    for f in range(3):
        send_out(f, moment_out, moment_far, sent).wait()


def outer_kernel(
    columns,
    inner_far,
    moment_ref,
    index_ref,
    inverse_ref,
    gjo_ref,
    gje_ref,
    moment_far,
    spread_ref,
    rows_ref,
    sent,
):
    ends = ends_of(columns)
    index = index_of(index_ref)
    got = (None, None, gjo_ref, gje_ref)
    copies = []
    for f in range(3):
        take_faces(f, index, ends, got, spread_ref, (1,))
        for end in range(2):
            for i in range(8):
                part = spread_ref[f, 2 + end, pl.ds(i, 8, stride=8)]
                kept = moment_ref[f, i, 7 * end]
                rows_ref[f, end, i] = kept - part * inverse_ref[rows(i, 7 * end)]
            copy = pltpu.make_async_copy(
                rows_ref.at[f, end], moment_far.at[f, :, 7 * end], sent.at[2 * f + end]
            )
            copy.start()
            copies.append(copy)
    for copy in copies:
        copy.wait()


VMEM = pl.BlockSpec(memory_space=pltpu.VMEM)
FAR = pl.BlockSpec(memory_space=pltpu.HBM)


def call(kernel, specs, shapes, scratch, flops, *operands, first_out=VMEM, aliases={}):
    moved = sum(o.size * 4 for o in operands) + sum(int(np.prod(s)) * 4 for s, _ in shapes)
    return pl.pallas_call(
        kernel,
        out_shape=[jax.ShapeDtypeStruct(s, t) for s, t in shapes],
        in_specs=specs,
        out_specs=[first_out] + [VMEM] * (len(shapes) - 1),
        scratch_shapes=scratch,
        input_output_aliases=aliases,
        compiler_params=pltpu.CompilerParams(vmem_limit_bytes=32 * 1024 * 1024),
        cost_estimate=pl.CostEstimate(flops=flops, bytes_accessed=moved, transcendentals=0),
    )(*operands)


def pairings(devices):
    columns = devices // DA
    device = lambda row, place: (row % DA * columns + place - columns // 2) % devices

    def both(pairs):
        return pairs + [(b, a) for a, b in pairs]

    places, halves = range(columns), range(0, columns, 2)
    along_i = [
        [(device(r, s), device(r + 1, s)) for r in range(0, DA, 2) for s in places],
        [(device(r, s), device(r + 1, s)) for r in range(1, DA - 1, 2) for s in places]
        + [(device(r, s), device(r, s + 1)) for r in (0, DA - 1) for s in halves],
    ]
    along_j = [
        [(device(r, s), device(r, s + 1)) for r in range(DA) for s in halves],
        [(device(r, s - 1), device(r, s)) for r in range(DA) for s in halves if s]
        + [(device(r, columns - 1), device(r + 1, 0)) for r in range(DA)],
    ]
    return [both(p) for p in along_i], [both(p) for p in along_j]


def shards(moment_fields, adjoint_fields, velocity, mass_weights, diffusivity, numbering):
    devices = lax.axis_size("elem")
    columns = devices // DA
    along_i, along_j = pairings(devices)
    whole, block = ((3, 512, 128), F32), ((512, 128), F32)
    work = pltpu.VMEM((3, 512, 128), F32)
    slopes = pltpu.VMEM((3, 2, 512, 128), F32)

    def spread(count):
        return pltpu.VMEM((count, 4, 64, 128), F32)

    def exchange(block, pairs):
        return lax.ppermute(block, "elem", pairs)

    def settle(block, *after):
        anywhere = pl.BlockSpec(memory_space=pl.ANY)
        return pl.pallas_call(
            lambda *refs: None,
            out_shape=jax.ShapeDtypeStruct(block.shape, block.dtype),
            in_specs=[anywhere] * (1 + len(after)),
            out_specs=anywhere,
            input_output_aliases={0: 0},
            compiler_params=pltpu.CompilerParams(vmem_limit_bytes=1024 * 1024),
        )(block, *after)

    def edge(count, way, *operands):
        return call(
            functools.partial(edge_kernel, columns, way),
            [VMEM] * len(operands),
            [(face_shape(count), F32)],
            [],
            count * 64 * 128,
            *operands,
        )[0]

    def meet(count, faces):
        got_i = [exchange(faces[way], along_i[way]) for way in range(2)]
        far_face = edge(count, 1, *got_i, faces[3])
        near_face = edge(count, 0, *got_i, faces[2], far_face)
        return got_i + [exchange(far_face, along_j[1]), exchange(near_face, along_j[0])]

    def settled(got, *after):
        return got[:2] + [settle(got[2], *after), got[3]]

    def far(array):
        return pltpu.with_memory_space_constraint(array, pltpu.HBM)

    def face_shape(count):
        return ((7 * count + 1) * 8, 128)

    def faces_shape(count):
        return [(face_shape(count), F32)] * 4

    moment, state, mass, weigh, table, turned, index, joined_state, *faces_state = call(
        functools.partial(index_kernel, columns),
        [FAR] * 5,
        [whole, whole, block, whole]
        + [((256, 384), BF16), ((128, 768), BF16)]
        + [((4, 8, 128), jnp.int32), ((4, 512, 128), F32)]
        + faces_shape(4),
        [
            pltpu.VMEM((512, 128), F32),
            pltpu.VMEM((1, 128), jnp.int32),
            pltpu.SMEM((3,), F32),
            pltpu.SemaphoreType.DMA((5,)),
        ],
        1_000_000,
        *map(far, (moment_fields, adjoint_fields, mass_weights, diffusivity)),
        far(numbering.reshape(1, 128)),
    )
    got_state = meet(4, faces_state)
    carry, joined_moment, *faces_moment = call(
        functools.partial(moment_kernel, columns),
        [VMEM] * 7,
        [whole, whole] + faces_shape(3),
        [slopes],
        20_000_000,
        moment,
        velocity,
        mass,
        weigh,
        table,
        turned,
        index,
    )
    tables = (carry, weigh, table, turned, index)
    got_moment = meet(3, faces_moment)
    inverse, state, joined_state, *faces_state = call(
        functools.partial(state_kernel, columns, True),
        [VMEM] * 11,
        [block, whole, whole] + faces_shape(3),
        [slopes, work, spread(4)],
        20_000_000,
        state,
        *tables,
        joined_state,
        *settled(got_state),
    )
    got_state = meet(3, faces_state)
    moment, joined_moment, *faces_moment = call(
        functools.partial(middle_kernel, columns),
        [VMEM] * 12,
        [whole, whole] + faces_shape(3),
        [slopes, spread(3)],
        20_000_000,
        moment,
        *tables,
        inverse,
        joined_moment,
        *settled(got_moment, inverse),
    )
    got_moment = meet(3, faces_moment)
    state, token = call(
        functools.partial(state_kernel, columns, False),
        [VMEM] * 12,
        [whole, ((8, 128), F32)],
        [slopes, work, spread(3), work] + [pltpu.SemaphoreType.DMA((3,))],
        20_000_000,
        state,
        *tables,
        joined_state,
        inverse,
        *settled(got_state),
        first_out=FAR,
    )
    cube = ((3, 8, 8, 8, 128), F32)
    inner, kept = call(
        functools.partial(inner_kernel, columns),
        [VMEM] * 7,
        [cube, cube],
        [spread(3), pltpu.SemaphoreType.DMA((3,))],
        1_000_000,
        moment,
        index,
        inverse,
        joined_moment,
        *got_moment[:2],
        token,
        first_out=FAR,
    )
    far_face, near_face = got_moment[2:]
    (moment,) = call(
        functools.partial(outer_kernel, columns),
        [FAR] + [VMEM] * 5,
        [cube],
        [
            spread(3),
            pltpu.VMEM((3, 2, 8, 8, 128), F32),
            pltpu.SemaphoreType.DMA((6,)),
        ],
        1_000_000,
        far(inner),
        kept,
        index,
        inverse,
        settle(far_face, kept),
        near_face,
        first_out=FAR,
        aliases={0: 0},
    )
    moment = moment.reshape(whole[0])
    return moment, state


def solution(mesh):
    in_specs = (
        P(None, None, "elem"),
        P(None, None, "elem"),
        P(None, None, "elem"),
        P(None, "elem"),
        P(),
        P("elem"),
    )
    out_specs = (P(None, None, "elem"), P(None, None, "elem"))
    return jax.shard_map(shards, mesh=mesh, in_specs=in_specs, out_specs=out_specs, check_vma=False)
```

```python
import functools

import jax
import jax.numpy as jnp
import numpy as np
from jax import lax
from jax.experimental import pallas as pl
from jax.experimental.pallas import tpu as pltpu
from jax.sharding import PartitionSpec as P

DA = 4
DT = 0.001
F32 = jnp.float32
BF16 = jnp.bfloat16


def gll_tables():
    points = [
        -1.0,
        -0.8717401485096066,
        -0.5917001814331423,
        -0.2092992179024789,
        0.2092992179024789,
        0.5917001814331423,
        0.8717401485096066,
        1.0,
    ]
    weights = [
        0.03571428571428571,
        0.21070422714350603,
        0.3411226924835044,
        0.4124587946587038,
        0.4124587946587038,
        0.3411226924835044,
        0.21070422714350603,
        0.03571428571428571,
    ]
    barycentric = []
    for left_index in range(8):
        product = 1.0
        for right_index in range(8):
            if right_index != left_index:
                product = product * (points[left_index] - points[right_index])
        barycentric.append(1.0 / product)
    derivative = np.zeros((8, 8))
    for left_index in range(8):
        row_total = 0.0
        for right_index in range(8):
            if left_index != right_index:
                entry = (
                    barycentric[right_index]
                    / barycentric[left_index]
                    / (points[left_index] - points[right_index])
                )
                derivative[left_index, right_index] = entry
                row_total = row_total + entry
        derivative[left_index, left_index] = -row_total
    return derivative, np.asarray(weights)


DM, WEIGHTS = gll_tables()


def line(table, values):
    sums = [values[q] + values[7 - q] for q in range(4)]
    differences = [values[q] - values[7 - q] for q in range(4)]
    out = [None] * 8
    for i in range(4):
        even = odd = None
        for q in range(4):
            on_sum = float(table[i, q] + table[i, 7 - q]) / 2
            on_difference = float(table[i, q] - table[i, 7 - q]) / 2
            even = sums[q] * on_sum if even is None else even + sums[q] * on_sum
            odd = (
                differences[q] * on_difference
                if odd is None
                else odd + differences[q] * on_difference
            )
        out[i] = odd + even
        out[7 - i] = odd - even
    return out


def rows(i, j):
    return pl.ds((8 * i + j) * 8, 8)


def split(block):
    wide = jnp.concatenate([block[128 * n : 128 * (n + 1)] for n in range(4)], axis=1)
    high = wide.astype(BF16)
    low = (wide - high.astype(F32)).astype(BF16)
    return [high, high, low]


def tall(wide):
    return jnp.concatenate([wide[:, 128 * n : 128 * (n + 1)] for n in range(4)], axis=0)


def slopes_jk(table_ref, block):
    parts = jnp.concatenate(split(block), axis=0)
    out = jnp.dot(table_ref[...], parts, preferred_element_type=F32)
    return tall(out[:128]), tall(out[128:])


def back_jk(turned_ref, flux_k, flux_j):
    parts = jnp.concatenate(split(flux_k) + split(flux_j), axis=0)
    return tall(jnp.dot(turned_ref[...], parts, preferred_element_type=F32))


def write_table(table, axis, table_ref, start, column):
    sub = lax.broadcasted_iota(jnp.int32, (8, 128), 0)
    lane = lax.broadcasted_iota(jnp.int32, (8, 128), 1)
    zero = jnp.zeros((8, 128), F32)
    place = lax.shift_right_logical(lane, 3)
    entry = place & 7 if axis else lane & 7
    bases = []
    for n in range(8):
        one_row = zero
        for q in range(8):
            one_row = jnp.where(entry == q, float(table[n, q]), one_row)
        bases.append(one_row)
    if axis:
        bases = [jnp.where((lane & 7) == sub, one_row, zero) for one_row in bases]
        place = lax.shift_right_logical(lane, 6)
    else:
        base = zero
        for n in range(8):
            base = jnp.where(sub == n, bases[n], base)
        bases = [base]
    highs = [base.astype(BF16).astype(F32) for base in bases]
    lows = [base - high for base, high in zip(bases, highs)]
    for a in range(0, 16, 2):
        parts = []
        for values in (highs, lows):
            pair = []
            for block in (a, a + 1):
                own = place == (block // 8 if axis else block)
                pair.append(jnp.where(own, values[block % 8 if axis else 0], zero))
            parts.append(jnp.concatenate(pair, axis=0))
        wide = jnp.concatenate([parts[0], parts[1], parts[0]], axis=1)
        table_ref[pl.ds(start + 8 * a, 16), column : column + 384] = wide.astype(BF16)


def lanes(block, index):
    wide = jnp.broadcast_to(index[None], (block.shape[0] // 8, 8, 128)).reshape(block.shape)
    return jnp.take_along_axis(block, wide, axis=1, mode="promise_in_bounds")


def set_mass(weight_ref, mass_ref):
    sub = lax.broadcasted_iota(jnp.int32, (8, 128), 0)
    along = jnp.zeros((8, 128), F32)
    for k in range(8):
        along = jnp.where(sub == k, float(WEIGHTS[k]), along)
    for i in range(8):
        for j in range(8):
            r = rows(i, j)
            mass_ref[r] = weight_ref[r] * (along * float(WEIGHTS[i] * WEIGHTS[j]))


def set_slopes(source, table_ref, slope):
    slope[0], slope[1] = slopes_jk(table_ref, source[...])


def forward_i(source, carry_ref, weigh, target):
    for j in range(8):
        slopes = line(DM, [source[rows(i, j)] for i in range(8)])
        back = line(DM.T, [weigh[rows(i, j)] * slopes[i] for i in range(8)])
        for i in range(8):
            r = rows(i, j)
            target[r] = carry_ref[0, r] * slopes[i] + back[i]


def forward_jk(carry_ref, weigh, turned_ref, slope, target):
    fluxes = weigh[...] * slope[0], weigh[...] * slope[1]
    carried = carry_ref[2] * slope[0] + carry_ref[1] * slope[1]
    target[...] = target[...] + (carried + back_jk(turned_ref, *fluxes))


def adjoint_i(source, base, carry_ref, weigh, target):
    for j in range(8):
        these = [rows(i, j) for i in range(8)]
        values = [source[r] for r in these]
        slopes = line(DM, values)
        fluxes = [carry_ref[0, r] * v + weigh[r] * g for r, v, g in zip(these, values, slopes)]
        for r, back in zip(these, line(DM.T, fluxes)):
            target[r] = base[r] - back


def adjoint_jk(source, carry_ref, weigh, turned_ref, slope, target):
    flux_k = carry_ref[2] * source[...] + weigh[...] * slope[0]
    flux_j = carry_ref[1] * source[...] + weigh[...] * slope[1]
    target[...] = target[...] - back_jk(turned_ref, flux_k, flux_j)


def forward(sources, carry_ref, weigh_ref, table_ref, turned_ref, slope_ref, target, finish):
    set_slopes(sources.at[0], table_ref, slope_ref.at[0])
    for f in range(3):
        at = (carry_ref, weigh_ref.at[f])
        forward_i(sources.at[f], *at, target.at[f])
        if f < 2:
            set_slopes(sources.at[f + 1], table_ref, slope_ref.at[f + 1])
        forward_jk(*at, turned_ref, slope_ref.at[f], target.at[f])
        finish(f)


def adjoint(sources, base, carry_ref, weigh_ref, table_ref, turned_ref, slope_ref, target, finish):
    set_slopes(sources.at[0], table_ref, slope_ref.at[0])
    for f in range(3):
        at = (carry_ref, weigh_ref.at[f])
        adjoint_i(sources.at[f], base.at[f], *at, target.at[f])
        if f < 2:
            set_slopes(sources.at[f + 1], table_ref, slope_ref.at[f + 1])
        adjoint_jk(sources.at[f], *at, turned_ref, slope_ref.at[f], target.at[f])
        finish(f)


def join_heights(ref, index):
    height, _, below, above = index
    lower = ref[pl.ds(0, 64, stride=8)]
    upper = ref[pl.ds(7, 64, stride=8)]
    tall = jnp.broadcast_to(height[None], (8, 8, 128)).reshape(64, 128)
    ref[pl.ds(0, 64, stride=8)] = lower + jnp.where(tall > 0, lanes(upper, below), 0.0)
    ref[pl.ds(7, 64, stride=8)] = upper + jnp.where(tall < 127, lanes(lower, above), 0.0)


def face_rows(ends, axis, way, k):
    end = ends[axis][way]
    return pl.ds(end * 8 + k, 8, stride=64) if axis else pl.ds(end * 64 + k, 8, stride=8)


def tile(c, k):
    return pl.ds((7 * c + k) * 8, 8)


def top_tile(ref):
    return pl.ds(ref.shape[0] - 8, 8)


def send_faces(c, ref, index, ends, out, fresh):
    inverse = index[1]
    top = jnp.broadcast_to(inverse[:, 127:], (8, 128))
    lane = lax.broadcasted_iota(jnp.int32, (8, 128), 1)
    for axis in range(2):
        for way in range(2):
            face = out[2 * axis + way]
            for k in range(7):
                face[tile(c, k)] = lanes(ref[face_rows(ends, axis, way, k)], inverse)
            last = lanes(ref[face_rows(ends, axis, way, 7)], top)
            others = jnp.zeros((8, 128), F32) if fresh else face[top_tile(face)]
            face[top_tile(face)] = jnp.where(lane == c, last, others)


def take_faces(c, index, ends, got, spread_ref, axes=(0, 1)):
    height = index[0]
    above = (height + 1) & 127
    own = jnp.full((8, 128), c, jnp.int32)
    for axis in axes:
        for way in range(2):
            face = got[3 - way if axis else way]
            last = jnp.where(
                height < 127, lanes(face[tile(c, 0)], above), lanes(face[top_tile(face)], own)
            )
            parts = [lanes(face[tile(c, k)], height) for k in range(7)] + [last]
            slot = 2 * axis + jnp.minimum(ends[axis][way], 1)
            for k, part in enumerate(parts):
                spread_ref[c, slot, pl.ds(8 * k, 8)] = part * ends[2][axis] if way else part


def assembled(c, i, j, joined, spread_ref, axes=(0, 1)):
    total = joined[rows(i, j)]
    for axis, (end, place) in enumerate(((i, j), (j, i))):
        if end in (0, 7) and axis in axes:
            total = total + spread_ref[c, 2 * axis + end // 7, pl.ds(place, 8, stride=8)]
    return total


def ends_of(columns):
    column = lax.rem(lax.axis_index("elem") + columns // 2, columns * DA)
    row, place = lax.div(column, columns), lax.rem(column, columns)
    row_odd, place_odd = lax.rem(row, 2), lax.rem(place, 2)
    row_inside = jnp.where((row > 0) & (row < DA - 1), 1.0, 0.0)
    place_inside = jnp.where((place > 0) & (place < columns - 1), 1.0, 0.0)
    return (
        (7 - 7 * row_odd, 7 * row_odd),
        (7 - 7 * place_odd, 7 * place_odd),
        (row_inside, place_inside),
    )


def index_of(index_ref):
    return tuple(index_ref[n] for n in range(4))


def index_kernel(
    columns,
    moment_far,
    state_far,
    weight_far,
    diff_far,
    numbers_far,
    moment_ref,
    state_ref,
    mass_ref,
    weigh_ref,
    table_ref,
    turned_ref,
    index_ref,
    joined_ref,
    ie_ref,
    io_ref,
    je_ref,
    jo_ref,
    weight_ref,
    numbers_ref,
    diff_ref,
    arrived,
):
    joined_state = joined_ref.at[pl.ds(0, 3)]
    far = (numbers_far, weight_far, diff_far, state_far, moment_far, state_far)
    near = (numbers_ref, weight_ref, diff_ref, joined_state, moment_ref, state_ref)
    copies = [pltpu.make_async_copy(a, b, arrived.at[n]) for n, (a, b) in enumerate(zip(far, near))]
    for copy in copies:
        copy.start()
    for axis in range(2):
        write_table(DM, axis, table_ref, 128 * axis, 0)
        write_table(DM.T, axis, turned_ref, 0, 384 * axis)
    ends = ends_of(columns)
    copies[0].wait()
    height = jnp.broadcast_to(numbers_ref[...] & 127, (8, 128))
    square = jnp.broadcast_to(height[:1].astype(F32), (128, 128)).T
    lane = lax.broadcasted_iota(jnp.int32, (128, 128), 1).astype(F32)
    row = lax.broadcasted_iota(jnp.int32, (128, 128), 0).astype(F32)
    inverse = jnp.sum(jnp.where(square == lane, row, 0.0), axis=0, keepdims=True)
    inverse = jnp.broadcast_to(inverse, (8, 128)).astype(jnp.int32)
    index = (
        height,
        inverse,
        lanes(inverse, (height - 1) & 127),
        lanes(inverse, (height + 1) & 127),
    )
    for n in range(4):
        index_ref[n] = index[n]
    copies[1].wait()
    set_mass(weight_ref, mass_ref)
    joined_ref[3] = mass_ref[...]
    out = (ie_ref, io_ref, je_ref, jo_ref)
    join_heights(joined_ref.at[3], index)
    send_faces(3, joined_ref.at[3], index, ends, out, True)
    copies[2].wait()
    for f in range(3):
        weigh_ref[f] = mass_ref[...] * (DT * diff_ref[f])
    copies[3].wait()
    for c in range(3):
        join_heights(joined_ref.at[c], index)
        send_faces(c, joined_ref.at[c], index, ends, out, False)
    copies[4].wait()
    copies[5].wait()


def moment_kernel(
    columns,
    moment_ref,
    flow_ref,
    mass_ref,
    weigh_ref,
    table_ref,
    turned_ref,
    index_ref,
    carry_ref,
    joined_ref,
    ie_ref,
    io_ref,
    je_ref,
    jo_ref,
    slope_ref,
):
    ends = ends_of(columns)
    index = index_of(index_ref)
    out = (ie_ref, io_ref, je_ref, jo_ref)
    for d in range(3):
        carry_ref[d] = mass_ref[...] * (DT * flow_ref[d])

    def finish(f):
        join_heights(joined_ref.at[f], index)
        send_faces(f, joined_ref.at[f], index, ends, out, f == 0)

    at = (carry_ref, weigh_ref, table_ref, turned_ref, slope_ref)
    forward(moment_ref, *at, joined_ref, finish)


def edge_kernel(columns, way, ie_ref, io_ref, face, *refs):
    ends, out = ends_of(columns), refs[-1]
    out[...] = face[...]
    tiles = face.shape[0] // 8
    r = pl.ds(ends[1][way], tiles, stride=8)
    for other, got in enumerate((ie_ref, io_ref)):
        w = pl.ds(ends[0][other], tiles, stride=8)
        part = got[r]
        out[w] = out[w] + (part * ends[2][0] if other else part)


def state_kernel(
    columns,
    first,
    state_ref,
    carry_ref,
    weigh_ref,
    table_ref,
    turned_ref,
    index_ref,
    joined_ref,
    *refs,
):
    ends = ends_of(columns)
    index = index_of(index_ref)
    if first:
        got, (inverse_ref, state_out, joined_out), refs = refs[:4], refs[4:7], refs[7:]
        out, (slope_ref, hold_ref, spread_ref) = refs[:4], refs[4:]
        take_faces(3, index, ends, got, spread_ref)
        for i in range(8):
            for j in range(8):
                inverse_ref[rows(i, j)] = 1.0 / assembled(3, i, j, joined_ref.at[3], spread_ref)
    else:
        inverse_ref, *got = refs[:5]
        state_far, token_ref, slope_ref, hold_ref, spread_ref, state_out, sent = refs[5:]
        token_ref[...] = jnp.zeros_like(token_ref)
    for f in range(3):
        take_faces(f, index, ends, got, spread_ref)
        for i in range(8):
            for j in range(8):
                total = assembled(f, i, j, joined_ref.at[f], spread_ref)
                hold_ref[f, rows(i, j)] = total * inverse_ref[rows(i, j)]

    def finish(f):
        if first:
            joined_out[f] = state_out[f]
            join_heights(joined_out.at[f], index)
            send_faces(f, joined_out.at[f], index, ends, out, f == 0)
        else:
            send_out(f, state_out, state_far, sent).start()

    at = (carry_ref, weigh_ref, table_ref, turned_ref, slope_ref)
    adjoint(hold_ref, state_ref, *at, state_out, finish)
    if not first:
        for f in range(3):
            send_out(f, state_out, state_far, sent).wait()


def send_out(f, near, far, sent):
    return pltpu.make_async_copy(near.at[f], far.at[f], sent.at[f])


def moment_step(f, ends, index, moment_ref, joined_ref, inverse_ref, got, spread_ref, moment_out):
    take_faces(f, index, ends, got, spread_ref)
    for i in range(8):
        for j in range(8):
            r = rows(i, j)
            total = assembled(f, i, j, joined_ref.at[f], spread_ref)
            moment_out[f, r] = moment_ref[f, r] - total * inverse_ref[r]


def middle_kernel(
    columns,
    moment_ref,
    carry_ref,
    weigh_ref,
    table_ref,
    turned_ref,
    index_ref,
    inverse_ref,
    joined_ref,
    gie_ref,
    gio_ref,
    gjo_ref,
    gje_ref,
    moment_out,
    joined_out,
    ie_ref,
    io_ref,
    je_ref,
    jo_ref,
    slope_ref,
    spread_ref,
):
    ends = ends_of(columns)
    index = index_of(index_ref)
    out = (ie_ref, io_ref, je_ref, jo_ref)
    got = (gie_ref, gio_ref, gjo_ref, gje_ref)
    for f in range(3):
        moment_step(f, ends, index, moment_ref, joined_ref, inverse_ref, got, spread_ref, moment_out)

    def finish(f):
        join_heights(joined_out.at[f], index)
        send_faces(f, joined_out.at[f], index, ends, out, f == 0)

    at = (carry_ref, weigh_ref, table_ref, turned_ref, slope_ref)
    forward(moment_out, *at, joined_out, finish)


def inner_kernel(
    columns,
    moment_ref,
    index_ref,
    inverse_ref,
    joined_ref,
    gie_ref,
    gio_ref,
    token_ref,
    moment_far,
    moment_out,
    spread_ref,
    sent,
):
    ends = ends_of(columns)
    index = index_of(index_ref)
    for f in range(3):
        take_faces(f, index, ends, (gie_ref, gio_ref), spread_ref, (0,))
        for i in range(8):
            for j in range(8):
                r = rows(i, j)
                total = assembled(f, i, j, joined_ref.at[f], spread_ref, (0,))
                moment_out[f, i, j] = moment_ref[f, r] - total * inverse_ref[r]
        send_out(f, moment_out, moment_far, sent).start()
    for f in range(3):
        send_out(f, moment_out, moment_far, sent).wait()


def outer_kernel(
    columns,
    inner_far,
    moment_ref,
    index_ref,
    inverse_ref,
    gjo_ref,
    gje_ref,
    moment_far,
    spread_ref,
    rows_ref,
    sent,
):
    ends = ends_of(columns)
    index = index_of(index_ref)
    got = (None, None, gjo_ref, gje_ref)
    copies = []
    for f in range(3):
        take_faces(f, index, ends, got, spread_ref, (1,))
        for end in range(2):
            for i in range(8):
                part = spread_ref[f, 2 + end, pl.ds(i, 8, stride=8)]
                kept = moment_ref[f, i, 7 * end]
                rows_ref[f, end, i] = kept - part * inverse_ref[rows(i, 7 * end)]
            copy = pltpu.make_async_copy(
                rows_ref.at[f, end], moment_far.at[f, :, 7 * end], sent.at[2 * f + end]
            )
            copy.start()
            copies.append(copy)
    for copy in copies:
        copy.wait()


VMEM = pl.BlockSpec(memory_space=pltpu.VMEM)
FAR = pl.BlockSpec(memory_space=pltpu.HBM)


def call(kernel, specs, shapes, scratch, flops, *operands, first_out=VMEM, aliases={}):
    moved = sum(o.size * 4 for o in operands) + sum(int(np.prod(s)) * 4 for s, _ in shapes)
    return pl.pallas_call(
        kernel,
        out_shape=[jax.ShapeDtypeStruct(s, t) for s, t in shapes],
        in_specs=specs,
        out_specs=[first_out] + [VMEM] * (len(shapes) - 1),
        scratch_shapes=scratch,
        input_output_aliases=aliases,
        compiler_params=pltpu.CompilerParams(vmem_limit_bytes=32 * 1024 * 1024),
        cost_estimate=pl.CostEstimate(flops=flops, bytes_accessed=moved, transcendentals=0),
    )(*operands)


def pairings(devices):
    columns = devices // DA
    device = lambda row, place: (row % DA * columns + place - columns // 2) % devices

    def both(pairs):
        return pairs + [(b, a) for a, b in pairs]

    places, halves = range(columns), range(0, columns, 2)
    along_i = [
        [(device(r, s), device(r + 1, s)) for r in range(0, DA, 2) for s in places],
        [(device(r, s), device(r + 1, s)) for r in range(1, DA - 1, 2) for s in places]
        + [(device(r, s), device(r, s + 1)) for r in (0, DA - 1) for s in halves],
    ]
    along_j = [
        [(device(r, s), device(r, s + 1)) for r in range(DA) for s in halves],
        [(device(r, s - 1), device(r, s)) for r in range(DA) for s in halves if s]
        + [(device(r, columns - 1), device(r + 1, 0)) for r in range(DA)],
    ]
    return [both(p) for p in along_i], [both(p) for p in along_j]


def shards(moment_fields, adjoint_fields, velocity, mass_weights, diffusivity, numbering):
    devices = lax.axis_size("elem")
    columns = devices // DA
    along_i, along_j = pairings(devices)
    whole, block = ((3, 512, 128), F32), ((512, 128), F32)
    work = pltpu.VMEM((3, 512, 128), F32)
    slopes = pltpu.VMEM((3, 2, 512, 128), F32)

    def spread(count):
        return pltpu.VMEM((count, 4, 64, 128), F32)

    def exchange(block, pairs):
        return lax.ppermute(block, "elem", pairs)

    def settle(block, *after):
        anywhere = pl.BlockSpec(memory_space=pl.ANY)
        return pl.pallas_call(
            lambda *refs: None,
            out_shape=jax.ShapeDtypeStruct(block.shape, block.dtype),
            in_specs=[anywhere] * (1 + len(after)),
            out_specs=anywhere,
            input_output_aliases={0: 0},
            compiler_params=pltpu.CompilerParams(vmem_limit_bytes=1024 * 1024),
        )(block, *after)

    def edge(count, way, *operands):
        return call(
            functools.partial(edge_kernel, columns, way),
            [VMEM] * len(operands),
            [(face_shape(count), F32)],
            [],
            count * 64 * 128,
            *operands,
        )[0]

    def meet(count, faces):
        got_i = [exchange(faces[way], along_i[way]) for way in range(2)]
        far_face = edge(count, 1, *got_i, faces[3])
        near_face = edge(count, 0, *got_i, faces[2], far_face)
        return got_i + [exchange(far_face, along_j[1]), exchange(near_face, along_j[0])]

    def settled(got, *after):
        return got[:2] + [settle(got[2], *after), got[3]]

    def far(array):
        return pltpu.with_memory_space_constraint(array, pltpu.HBM)

    def face_shape(count):
        return ((7 * count + 1) * 8, 128)

    def faces_shape(count):
        return [(face_shape(count), F32)] * 4

    moment, state, mass, weigh, table, turned, index, joined_state, *faces_state = call(
        functools.partial(index_kernel, columns),
        [FAR] * 5,
        [whole, whole, block, whole]
        + [((256, 384), BF16), ((128, 768), BF16)]
        + [((4, 8, 128), jnp.int32), ((4, 512, 128), F32)]
        + faces_shape(4),
        [
            pltpu.VMEM((512, 128), F32),
            pltpu.VMEM((1, 128), jnp.int32),
            pltpu.SMEM((3,), F32),
            pltpu.SemaphoreType.DMA((6,)),
        ],
        1_000_000,
        *map(far, (moment_fields, adjoint_fields, mass_weights, diffusivity)),
        far(numbering.reshape(1, 128)),
    )
    got_state = meet(4, faces_state)
    carry, joined_moment, *faces_moment = call(
        functools.partial(moment_kernel, columns),
        [VMEM] * 7,
        [whole, whole] + faces_shape(3),
        [slopes],
        20_000_000,
        moment,
        velocity,
        mass,
        weigh,
        table,
        turned,
        index,
    )
    tables = (carry, weigh, table, turned, index)
    got_moment = meet(3, faces_moment)
    inverse, state, joined_state, *faces_state = call(
        functools.partial(state_kernel, columns, True),
        [VMEM] * 11,
        [block, whole, whole] + faces_shape(3),
        [slopes, work, spread(4)],
        20_000_000,
        state,
        *tables,
        joined_state,
        *settled(got_state),
    )
    got_state = meet(3, faces_state)
    moment, joined_moment, *faces_moment = call(
        functools.partial(middle_kernel, columns),
        [VMEM] * 12,
        [whole, whole] + faces_shape(3),
        [slopes, spread(3)],
        20_000_000,
        moment,
        *tables,
        inverse,
        joined_moment,
        *settled(got_moment, inverse),
    )
    got_moment = meet(3, faces_moment)
    state, token = call(
        functools.partial(state_kernel, columns, False),
        [VMEM] * 12,
        [whole, ((8, 128), F32)],
        [slopes, work, spread(3), work] + [pltpu.SemaphoreType.DMA((3,))],
        20_000_000,
        state,
        *tables,
        joined_state,
        inverse,
        *settled(got_state),
        first_out=FAR,
    )
    cube = ((3, 8, 8, 8, 128), F32)
    inner, kept = call(
        functools.partial(inner_kernel, columns),
        [VMEM] * 7,
        [cube, cube],
        [spread(3), pltpu.SemaphoreType.DMA((3,))],
        1_000_000,
        moment,
        index,
        inverse,
        joined_moment,
        *got_moment[:2],
        token,
        first_out=FAR,
    )
    far_face, near_face = got_moment[2:]
    (moment,) = call(
        functools.partial(outer_kernel, columns),
        [FAR] + [VMEM] * 5,
        [cube],
        [
            spread(3),
            pltpu.VMEM((3, 2, 8, 8, 128), F32),
            pltpu.SemaphoreType.DMA((6,)),
        ],
        1_000_000,
        far(inner),
        kept,
        index,
        inverse,
        settle(far_face, kept),
        near_face,
        first_out=FAR,
        aliases={0: 0},
    )
    moment = moment.reshape(whole[0])
    return moment, state


def solution(mesh):
    in_specs = (
        P(None, None, "elem"),
        P(None, None, "elem"),
        P(None, None, "elem"),
        P(None, "elem"),
        P(),
        P("elem"),
    )
    out_specs = (P(None, None, "elem"), P(None, None, "elem"))
    return jax.shard_map(shards, mesh=mesh, in_specs=in_specs, out_specs=out_specs, check_vma=False)
```

```python
import functools

import jax
import jax.numpy as jnp
import numpy as np
from jax import lax
from jax.experimental import pallas as pl
from jax.experimental.pallas import tpu as pltpu
from jax.sharding import PartitionSpec as P

DA = 4
DT = 0.001
F32 = jnp.float32
BF16 = jnp.bfloat16


def gll_tables():
    points = [
        -1.0,
        -0.8717401485096066,
        -0.5917001814331423,
        -0.2092992179024789,
        0.2092992179024789,
        0.5917001814331423,
        0.8717401485096066,
        1.0,
    ]
    weights = [
        0.03571428571428571,
        0.21070422714350603,
        0.3411226924835044,
        0.4124587946587038,
        0.4124587946587038,
        0.3411226924835044,
        0.21070422714350603,
        0.03571428571428571,
    ]
    barycentric = []
    for left_index in range(8):
        product = 1.0
        for right_index in range(8):
            if right_index != left_index:
                product = product * (points[left_index] - points[right_index])
        barycentric.append(1.0 / product)
    derivative = np.zeros((8, 8))
    for left_index in range(8):
        row_total = 0.0
        for right_index in range(8):
            if left_index != right_index:
                entry = (
                    barycentric[right_index]
                    / barycentric[left_index]
                    / (points[left_index] - points[right_index])
                )
                derivative[left_index, right_index] = entry
                row_total = row_total + entry
        derivative[left_index, left_index] = -row_total
    return derivative, np.asarray(weights)


DM, WEIGHTS = gll_tables()


def line(table, values):
    sums = [values[q] + values[7 - q] for q in range(4)]
    differences = [values[q] - values[7 - q] for q in range(4)]
    out = [None] * 8
    for i in range(4):
        even = odd = None
        for q in range(4):
            on_sum = float(table[i, q] + table[i, 7 - q]) / 2
            on_difference = float(table[i, q] - table[i, 7 - q]) / 2
            even = sums[q] * on_sum if even is None else even + sums[q] * on_sum
            odd = (
                differences[q] * on_difference
                if odd is None
                else odd + differences[q] * on_difference
            )
        out[i] = odd + even
        out[7 - i] = odd - even
    return out


def rows(i, j):
    return pl.ds((8 * i + j) * 8, 8)


def split(block):
    wide = jnp.concatenate([block[128 * n : 128 * (n + 1)] for n in range(4)], axis=1)
    high = wide.astype(BF16)
    low = (wide - high.astype(F32)).astype(BF16)
    return [high, high, low]


def tall(wide):
    return jnp.concatenate([wide[:, 128 * n : 128 * (n + 1)] for n in range(4)], axis=0)


def slopes_jk(table_ref, block):
    parts = jnp.concatenate(split(block), axis=0)
    out = jnp.dot(table_ref[...], parts, preferred_element_type=F32)
    return tall(out[:128]), tall(out[128:])


def back_jk(turned_ref, flux_k, flux_j):
    parts = jnp.concatenate(split(flux_k) + split(flux_j), axis=0)
    return tall(jnp.dot(turned_ref[...], parts, preferred_element_type=F32))


def write_table(table, axis, table_ref, start, column):
    sub = lax.broadcasted_iota(jnp.int32, (8, 128), 0)
    lane = lax.broadcasted_iota(jnp.int32, (8, 128), 1)
    zero = jnp.zeros((8, 128), F32)
    place = lax.shift_right_logical(lane, 3)
    entry = place & 7 if axis else lane & 7
    bases = []
    for n in range(8):
        one_row = zero
        for q in range(8):
            one_row = jnp.where(entry == q, float(table[n, q]), one_row)
        bases.append(one_row)
    if axis:
        bases = [jnp.where((lane & 7) == sub, one_row, zero) for one_row in bases]
        place = lax.shift_right_logical(lane, 6)
    else:
        base = zero
        for n in range(8):
            base = jnp.where(sub == n, bases[n], base)
        bases = [base]
    highs = [base.astype(BF16).astype(F32) for base in bases]
    lows = [base - high for base, high in zip(bases, highs)]
    for a in range(0, 16, 2):
        parts = []
        for values in (highs, lows):
            pair = []
            for block in (a, a + 1):
                own = place == (block // 8 if axis else block)
                pair.append(jnp.where(own, values[block % 8 if axis else 0], zero))
            parts.append(jnp.concatenate(pair, axis=0))
        wide = jnp.concatenate([parts[0], parts[1], parts[0]], axis=1)
        table_ref[pl.ds(start + 8 * a, 16), column : column + 384] = wide.astype(BF16)


def lanes(block, index):
    wide = jnp.broadcast_to(index[None], (block.shape[0] // 8, 8, 128)).reshape(block.shape)
    return jnp.take_along_axis(block, wide, axis=1, mode="promise_in_bounds")


def set_mass(weight_ref, mass_ref):
    sub = lax.broadcasted_iota(jnp.int32, (8, 128), 0)
    along = jnp.zeros((8, 128), F32)
    for k in range(8):
        along = jnp.where(sub == k, float(WEIGHTS[k]), along)
    for i in range(8):
        for j in range(8):
            r = rows(i, j)
            mass_ref[r] = weight_ref[r] * (along * float(WEIGHTS[i] * WEIGHTS[j]))


def set_slopes(source, table_ref, slope):
    slope[0], slope[1] = slopes_jk(table_ref, source[...])


def forward_i(source, carry_ref, weigh, target):
    for j in range(8):
        slopes = line(DM, [source[rows(i, j)] for i in range(8)])
        back = line(DM.T, [weigh[rows(i, j)] * slopes[i] for i in range(8)])
        for i in range(8):
            r = rows(i, j)
            target[r] = carry_ref[0, r] * slopes[i] + back[i]


def forward_jk(carry_ref, weigh, turned_ref, slope, target):
    fluxes = weigh[...] * slope[0], weigh[...] * slope[1]
    carried = carry_ref[2] * slope[0] + carry_ref[1] * slope[1]
    target[...] = target[...] + (carried + back_jk(turned_ref, *fluxes))


def adjoint_i(source, base, carry_ref, weigh, target):
    for j in range(8):
        these = [rows(i, j) for i in range(8)]
        values = [source[r] for r in these]
        slopes = line(DM, values)
        fluxes = [carry_ref[0, r] * v + weigh[r] * g for r, v, g in zip(these, values, slopes)]
        for r, back in zip(these, line(DM.T, fluxes)):
            target[r] = base[r] - back


def adjoint_jk(source, carry_ref, weigh, turned_ref, slope, target):
    flux_k = carry_ref[2] * source[...] + weigh[...] * slope[0]
    flux_j = carry_ref[1] * source[...] + weigh[...] * slope[1]
    target[...] = target[...] - back_jk(turned_ref, flux_k, flux_j)


def forward(sources, carry_ref, weigh_ref, table_ref, turned_ref, slope_ref, target, finish):
    set_slopes(sources.at[0], table_ref, slope_ref.at[0])
    for f in range(3):
        at = (carry_ref, weigh_ref.at[f])
        forward_i(sources.at[f], *at, target.at[f])
        if f < 2:
            set_slopes(sources.at[f + 1], table_ref, slope_ref.at[f + 1])
        forward_jk(*at, turned_ref, slope_ref.at[f], target.at[f])
        finish(f)


def adjoint(sources, base, carry_ref, weigh_ref, table_ref, turned_ref, slope_ref, target, finish):
    set_slopes(sources.at[0], table_ref, slope_ref.at[0])
    for f in range(3):
        at = (carry_ref, weigh_ref.at[f])
        adjoint_i(sources.at[f], base.at[f], *at, target.at[f])
        if f < 2:
            set_slopes(sources.at[f + 1], table_ref, slope_ref.at[f + 1])
        adjoint_jk(sources.at[f], *at, turned_ref, slope_ref.at[f], target.at[f])
        finish(f)


def join_heights(ref, index):
    height, _, below, above = index
    lower = ref[pl.ds(0, 64, stride=8)]
    upper = ref[pl.ds(7, 64, stride=8)]
    tall = jnp.broadcast_to(height[None], (8, 8, 128)).reshape(64, 128)
    ref[pl.ds(0, 64, stride=8)] = lower + jnp.where(tall > 0, lanes(upper, below), 0.0)
    ref[pl.ds(7, 64, stride=8)] = upper + jnp.where(tall < 127, lanes(lower, above), 0.0)


def face_rows(ends, axis, way, k):
    end = ends[axis][way]
    return pl.ds(end * 8 + k, 8, stride=64) if axis else pl.ds(end * 64 + k, 8, stride=8)


def tile(c, k):
    return pl.ds((7 * c + k) * 8, 8)


def top_tile(ref):
    return pl.ds(ref.shape[0] - 8, 8)


def send_faces(c, ref, index, ends, out, fresh):
    inverse = index[1]
    top = jnp.broadcast_to(inverse[:, 127:], (8, 128))
    lane = lax.broadcasted_iota(jnp.int32, (8, 128), 1)
    for axis in range(2):
        for way in range(2):
            face = out[2 * axis + way]
            for k in range(7):
                face[tile(c, k)] = lanes(ref[face_rows(ends, axis, way, k)], inverse)
            last = lanes(ref[face_rows(ends, axis, way, 7)], top)
            others = jnp.zeros((8, 128), F32) if fresh else face[top_tile(face)]
            face[top_tile(face)] = jnp.where(lane == c, last, others)


def take_faces(c, index, ends, got, spread_ref, axes=(0, 1)):
    height = index[0]
    above = (height + 1) & 127
    own = jnp.full((8, 128), c, jnp.int32)
    for axis in axes:
        for way in range(2):
            face = got[3 - way if axis else way]
            last = jnp.where(
                height < 127, lanes(face[tile(c, 0)], above), lanes(face[top_tile(face)], own)
            )
            parts = [lanes(face[tile(c, k)], height) for k in range(7)] + [last]
            slot = 2 * axis + jnp.minimum(ends[axis][way], 1)
            for k, part in enumerate(parts):
                spread_ref[c, slot, pl.ds(8 * k, 8)] = part * ends[2][axis] if way else part


def assembled(c, i, j, joined, spread_ref, axes=(0, 1)):
    total = joined[rows(i, j)]
    for axis, (end, place) in enumerate(((i, j), (j, i))):
        if end in (0, 7) and axis in axes:
            total = total + spread_ref[c, 2 * axis + end // 7, pl.ds(place, 8, stride=8)]
    return total


def ends_of(columns):
    column = lax.rem(lax.axis_index("elem") + columns // 2, columns * DA)
    row, place = lax.div(column, columns), lax.rem(column, columns)
    row_odd, place_odd = lax.rem(row, 2), lax.rem(place, 2)
    row_inside = jnp.where((row > 0) & (row < DA - 1), 1.0, 0.0)
    place_inside = jnp.where((place > 0) & (place < columns - 1), 1.0, 0.0)
    return (
        (7 - 7 * row_odd, 7 * row_odd),
        (7 - 7 * place_odd, 7 * place_odd),
        (row_inside, place_inside),
    )


def index_of(index_ref):
    return tuple(index_ref[n] for n in range(4))


def index_kernel(
    columns,
    moment_far,
    state_far,
    weight_far,
    diff_far,
    numbers_far,
    moment_ref,
    state_ref,
    mass_ref,
    weigh_ref,
    table_ref,
    turned_ref,
    index_ref,
    joined_ref,
    ie_ref,
    io_ref,
    je_ref,
    jo_ref,
    weight_ref,
    numbers_ref,
    diff_ref,
    arrived,
):
    joined_state = joined_ref.at[pl.ds(0, 3)]
    far = (numbers_far, weight_far, diff_far, state_far, moment_far, state_far)
    near = (numbers_ref, weight_ref, diff_ref, joined_state, moment_ref, state_ref)
    copies = [pltpu.make_async_copy(a, b, arrived.at[n]) for n, (a, b) in enumerate(zip(far, near))]
    for copy in copies[:4]:
        copy.start()
    for axis in range(2):
        write_table(DM, axis, table_ref, 128 * axis, 0)
        write_table(DM.T, axis, turned_ref, 0, 384 * axis)
    ends = ends_of(columns)
    copies[0].wait()
    for copy in copies[4:]:
        copy.start()
    height = jnp.broadcast_to(numbers_ref[...] & 127, (8, 128))
    square = jnp.broadcast_to(height[:1].astype(F32), (128, 128)).T
    lane = lax.broadcasted_iota(jnp.int32, (128, 128), 1).astype(F32)
    row = lax.broadcasted_iota(jnp.int32, (128, 128), 0).astype(F32)
    inverse = jnp.sum(jnp.where(square == lane, row, 0.0), axis=0, keepdims=True)
    inverse = jnp.broadcast_to(inverse, (8, 128)).astype(jnp.int32)
    index = (
        height,
        inverse,
        lanes(inverse, (height - 1) & 127),
        lanes(inverse, (height + 1) & 127),
    )
    for n in range(4):
        index_ref[n] = index[n]
    copies[1].wait()
    set_mass(weight_ref, mass_ref)
    joined_ref[3] = mass_ref[...]
    out = (ie_ref, io_ref, je_ref, jo_ref)
    join_heights(joined_ref.at[3], index)
    send_faces(3, joined_ref.at[3], index, ends, out, True)
    copies[2].wait()
    for f in range(3):
        weigh_ref[f] = mass_ref[...] * (DT * diff_ref[f])
    copies[3].wait()
    for c in range(3):
        join_heights(joined_ref.at[c], index)
        send_faces(c, joined_ref.at[c], index, ends, out, False)
    copies[4].wait()
    copies[5].wait()


def moment_kernel(
    columns,
    moment_ref,
    flow_ref,
    mass_ref,
    weigh_ref,
    table_ref,
    turned_ref,
    index_ref,
    carry_ref,
    joined_ref,
    ie_ref,
    io_ref,
    je_ref,
    jo_ref,
    slope_ref,
):
    ends = ends_of(columns)
    index = index_of(index_ref)
    out = (ie_ref, io_ref, je_ref, jo_ref)
    for d in range(3):
        carry_ref[d] = mass_ref[...] * (DT * flow_ref[d])

    def finish(f):
        join_heights(joined_ref.at[f], index)
        send_faces(f, joined_ref.at[f], index, ends, out, f == 0)

    at = (carry_ref, weigh_ref, table_ref, turned_ref, slope_ref)
    forward(moment_ref, *at, joined_ref, finish)


def edge_kernel(columns, way, ie_ref, io_ref, face, *refs):
    ends, out = ends_of(columns), refs[-1]
    out[...] = face[...]
    tiles = face.shape[0] // 8
    r = pl.ds(ends[1][way], tiles, stride=8)
    for other, got in enumerate((ie_ref, io_ref)):
        w = pl.ds(ends[0][other], tiles, stride=8)
        part = got[r]
        out[w] = out[w] + (part * ends[2][0] if other else part)


def state_kernel(
    columns,
    first,
    state_ref,
    carry_ref,
    weigh_ref,
    table_ref,
    turned_ref,
    index_ref,
    joined_ref,
    *refs,
):
    ends = ends_of(columns)
    index = index_of(index_ref)
    if first:
        got, (inverse_ref, state_out, joined_out), refs = refs[:4], refs[4:7], refs[7:]
        out, (slope_ref, hold_ref, spread_ref) = refs[:4], refs[4:]
        take_faces(3, index, ends, got, spread_ref)
        for i in range(8):
            for j in range(8):
                inverse_ref[rows(i, j)] = 1.0 / assembled(3, i, j, joined_ref.at[3], spread_ref)
    else:
        inverse_ref, *got = refs[:5]
        state_far, token_ref, slope_ref, hold_ref, spread_ref, state_out, sent = refs[5:]
        token_ref[...] = jnp.zeros_like(token_ref)
    for f in range(3):
        take_faces(f, index, ends, got, spread_ref)
        for i in range(8):
            for j in range(8):
                total = assembled(f, i, j, joined_ref.at[f], spread_ref)
                hold_ref[f, rows(i, j)] = total * inverse_ref[rows(i, j)]

    def finish(f):
        if first:
            joined_out[f] = state_out[f]
            join_heights(joined_out.at[f], index)
            send_faces(f, joined_out.at[f], index, ends, out, f == 0)
        else:
            send_out(f, state_out, state_far, sent).start()

    at = (carry_ref, weigh_ref, table_ref, turned_ref, slope_ref)
    adjoint(hold_ref, state_ref, *at, state_out, finish)
    if not first:
        for f in range(3):
            send_out(f, state_out, state_far, sent).wait()


def send_out(f, near, far, sent):
    return pltpu.make_async_copy(near.at[f], far.at[f], sent.at[f])


def moment_step(f, ends, index, moment_ref, joined_ref, inverse_ref, got, spread_ref, moment_out):
    take_faces(f, index, ends, got, spread_ref)
    for i in range(8):
        for j in range(8):
            r = rows(i, j)
            total = assembled(f, i, j, joined_ref.at[f], spread_ref)
            moment_out[f, r] = moment_ref[f, r] - total * inverse_ref[r]


def middle_kernel(
    columns,
    moment_ref,
    carry_ref,
    weigh_ref,
    table_ref,
    turned_ref,
    index_ref,
    inverse_ref,
    joined_ref,
    gie_ref,
    gio_ref,
    gjo_ref,
    gje_ref,
    moment_out,
    joined_out,
    ie_ref,
    io_ref,
    je_ref,
    jo_ref,
    slope_ref,
    spread_ref,
):
    ends = ends_of(columns)
    index = index_of(index_ref)
    out = (ie_ref, io_ref, je_ref, jo_ref)
    got = (gie_ref, gio_ref, gjo_ref, gje_ref)
    for f in range(3):
        moment_step(f, ends, index, moment_ref, joined_ref, inverse_ref, got, spread_ref, moment_out)

    def finish(f):
        join_heights(joined_out.at[f], index)
        send_faces(f, joined_out.at[f], index, ends, out, f == 0)

    at = (carry_ref, weigh_ref, table_ref, turned_ref, slope_ref)
    forward(moment_out, *at, joined_out, finish)


def inner_kernel(
    columns,
    moment_ref,
    index_ref,
    inverse_ref,
    joined_ref,
    gie_ref,
    gio_ref,
    token_ref,
    moment_far,
    moment_out,
    spread_ref,
    sent,
):
    ends = ends_of(columns)
    index = index_of(index_ref)
    for f in range(3):
        take_faces(f, index, ends, (gie_ref, gio_ref), spread_ref, (0,))
        for i in range(8):
            for j in range(8):
                r = rows(i, j)
                total = assembled(f, i, j, joined_ref.at[f], spread_ref, (0,))
                moment_out[f, i, j] = moment_ref[f, r] - total * inverse_ref[r]
        send_out(f, moment_out, moment_far, sent).start()
    for f in range(3):
        send_out(f, moment_out, moment_far, sent).wait()


def outer_kernel(
    columns,
    inner_far,
    moment_ref,
    index_ref,
    inverse_ref,
    gjo_ref,
    gje_ref,
    moment_far,
    spread_ref,
    rows_ref,
    sent,
):
    ends = ends_of(columns)
    index = index_of(index_ref)
    got = (None, None, gjo_ref, gje_ref)
    copies = []
    for f in range(3):
        take_faces(f, index, ends, got, spread_ref, (1,))
        for end in range(2):
            for i in range(8):
                part = spread_ref[f, 2 + end, pl.ds(i, 8, stride=8)]
                kept = moment_ref[f, i, 7 * end]
                rows_ref[f, end, i] = kept - part * inverse_ref[rows(i, 7 * end)]
            copy = pltpu.make_async_copy(
                rows_ref.at[f, end], moment_far.at[f, :, 7 * end], sent.at[2 * f + end]
            )
            copy.start()
            copies.append(copy)
    for copy in copies:
        copy.wait()


VMEM = pl.BlockSpec(memory_space=pltpu.VMEM)
FAR = pl.BlockSpec(memory_space=pltpu.HBM)


def call(kernel, specs, shapes, scratch, flops, *operands, first_out=VMEM, aliases={}):
    moved = sum(o.size * 4 for o in operands) + sum(int(np.prod(s)) * 4 for s, _ in shapes)
    return pl.pallas_call(
        kernel,
        out_shape=[jax.ShapeDtypeStruct(s, t) for s, t in shapes],
        in_specs=specs,
        out_specs=[first_out] + [VMEM] * (len(shapes) - 1),
        scratch_shapes=scratch,
        input_output_aliases=aliases,
        compiler_params=pltpu.CompilerParams(vmem_limit_bytes=32 * 1024 * 1024),
        cost_estimate=pl.CostEstimate(flops=flops, bytes_accessed=moved, transcendentals=0),
    )(*operands)


def pairings(devices):
    columns = devices // DA
    device = lambda row, place: (row % DA * columns + place - columns // 2) % devices

    def both(pairs):
        return pairs + [(b, a) for a, b in pairs]

    places, halves = range(columns), range(0, columns, 2)
    along_i = [
        [(device(r, s), device(r + 1, s)) for r in range(0, DA, 2) for s in places],
        [(device(r, s), device(r + 1, s)) for r in range(1, DA - 1, 2) for s in places]
        + [(device(r, s), device(r, s + 1)) for r in (0, DA - 1) for s in halves],
    ]
    along_j = [
        [(device(r, s), device(r, s + 1)) for r in range(DA) for s in halves],
        [(device(r, s - 1), device(r, s)) for r in range(DA) for s in halves if s]
        + [(device(r, columns - 1), device(r + 1, 0)) for r in range(DA)],
    ]
    return [both(p) for p in along_i], [both(p) for p in along_j]


def shards(moment_fields, adjoint_fields, velocity, mass_weights, diffusivity, numbering):
    devices = lax.axis_size("elem")
    columns = devices // DA
    along_i, along_j = pairings(devices)
    whole, block = ((3, 512, 128), F32), ((512, 128), F32)
    work = pltpu.VMEM((3, 512, 128), F32)
    slopes = pltpu.VMEM((3, 2, 512, 128), F32)

    def spread(count):
        return pltpu.VMEM((count, 4, 64, 128), F32)

    def exchange(block, pairs):
        return lax.ppermute(block, "elem", pairs)

    def settle(block, *after):
        anywhere = pl.BlockSpec(memory_space=pl.ANY)
        return pl.pallas_call(
            lambda *refs: None,
            out_shape=jax.ShapeDtypeStruct(block.shape, block.dtype),
            in_specs=[anywhere] * (1 + len(after)),
            out_specs=anywhere,
            input_output_aliases={0: 0},
            compiler_params=pltpu.CompilerParams(vmem_limit_bytes=1024 * 1024),
        )(block, *after)

    def edge(count, way, *operands):
        return call(
            functools.partial(edge_kernel, columns, way),
            [VMEM] * len(operands),
            [(face_shape(count), F32)],
            [],
            count * 64 * 128,
            *operands,
        )[0]

    def meet(count, faces):
        got_i = [exchange(faces[way], along_i[way]) for way in range(2)]
        far_face = edge(count, 1, *got_i, faces[3])
        near_face = edge(count, 0, *got_i, faces[2], far_face)
        return got_i + [exchange(far_face, along_j[1]), exchange(near_face, along_j[0])]

    def settled(got, *after):
        return got[:2] + [settle(got[2], *after), got[3]]

    def far(array):
        return pltpu.with_memory_space_constraint(array, pltpu.HBM)

    def face_shape(count):
        return ((7 * count + 1) * 8, 128)

    def faces_shape(count):
        return [(face_shape(count), F32)] * 4

    moment, state, mass, weigh, table, turned, index, joined_state, *faces_state = call(
        functools.partial(index_kernel, columns),
        [FAR] * 5,
        [whole, whole, block, whole]
        + [((256, 384), BF16), ((128, 768), BF16)]
        + [((4, 8, 128), jnp.int32), ((4, 512, 128), F32)]
        + faces_shape(4),
        [
            pltpu.VMEM((512, 128), F32),
            pltpu.VMEM((1, 128), jnp.int32),
            pltpu.SMEM((3,), F32),
            pltpu.SemaphoreType.DMA((6,)),
        ],
        1_000_000,
        *map(far, (moment_fields, adjoint_fields, mass_weights, diffusivity)),
        far(numbering.reshape(1, 128)),
    )
    got_state = meet(4, faces_state)
    carry, joined_moment, *faces_moment = call(
        functools.partial(moment_kernel, columns),
        [VMEM] * 7,
        [whole, whole] + faces_shape(3),
        [slopes],
        20_000_000,
        moment,
        velocity,
        mass,
        weigh,
        table,
        turned,
        index,
    )
    tables = (carry, weigh, table, turned, index)
    got_moment = meet(3, faces_moment)
    inverse, state, joined_state, *faces_state = call(
        functools.partial(state_kernel, columns, True),
        [VMEM] * 11,
        [block, whole, whole] + faces_shape(3),
        [slopes, work, spread(4)],
        20_000_000,
        state,
        *tables,
        joined_state,
        *settled(got_state),
    )
    got_state = meet(3, faces_state)
    moment, joined_moment, *faces_moment = call(
        functools.partial(middle_kernel, columns),
        [VMEM] * 12,
        [whole, whole] + faces_shape(3),
        [slopes, spread(3)],
        20_000_000,
        moment,
        *tables,
        inverse,
        joined_moment,
        *settled(got_moment, inverse),
    )
    got_moment = meet(3, faces_moment)
    state, token = call(
        functools.partial(state_kernel, columns, False),
        [VMEM] * 12,
        [whole, ((8, 128), F32)],
        [slopes, work, spread(3), work] + [pltpu.SemaphoreType.DMA((3,))],
        20_000_000,
        state,
        *tables,
        joined_state,
        inverse,
        *settled(got_state),
        first_out=FAR,
    )
    cube = ((3, 8, 8, 8, 128), F32)
    inner, kept = call(
        functools.partial(inner_kernel, columns),
        [VMEM] * 7,
        [cube, cube],
        [spread(3), pltpu.SemaphoreType.DMA((3,))],
        1_000_000,
        moment,
        index,
        inverse,
        joined_moment,
        *got_moment[:2],
        token,
        first_out=FAR,
    )
    far_face, near_face = got_moment[2:]
    (moment,) = call(
        functools.partial(outer_kernel, columns),
        [FAR] + [VMEM] * 5,
        [cube],
        [
            spread(3),
            pltpu.VMEM((3, 2, 8, 8, 128), F32),
            pltpu.SemaphoreType.DMA((6,)),
        ],
        1_000_000,
        far(inner),
        kept,
        index,
        inverse,
        settle(far_face, kept),
        near_face,
        first_out=FAR,
        aliases={0: 0},
    )
    moment = moment.reshape(whole[0])
    return moment, state


def solution(mesh):
    in_specs = (
        P(None, None, "elem"),
        P(None, None, "elem"),
        P(None, None, "elem"),
        P(None, "elem"),
        P(),
        P("elem"),
    )
    out_specs = (P(None, None, "elem"), P(None, None, "elem"))
    return jax.shard_map(shards, mesh=mesh, in_specs=in_specs, out_specs=out_specs, check_vma=False)
```
